256 devices in a mesh: gx: 4 (over x), gy: 8 (over y, core), gz: 8 (over z).
Axes of the slice: x: 4, y: 4, z: 8, core: 2. Of those that a mesh axis runs over, the one named last changes fastest.
Arguments:
- volume: bfloat16 [32, 64, 32, 1024], P(None, 'gz', 'gx', 'gy'), may hold values from -6 to 6
- cotangent: bfloat16 [32, 64, 32, 1024], P(None, 'gz', 'gx', 'gy'), may hold values from -6 to 6
- weight_one: bfloat16 [27, 32, 32], replicated, may hold values from -0.21875 to 0.21875
- weight_two: bfloat16 [27, 64, 32], replicated, may hold values from -0.21875 to 0.21875
- weight_three: bfloat16 [27, 256, 64], replicated, may hold values from -0.15625 to 0.15625
- weight_four: bfloat16 [32, 256], replicated, may hold values from -0.375 to 0.375
Outputs:
- output: bfloat16 [32, 64, 32, 1024], P(None, 'gz', 'gx', 'gy')
- grad_volume: bfloat16 [32, 64, 32, 1024], P(None, 'gz', 'gx', 'gy')
- grad_one: float32 [27, 32, 32], replicated
- grad_two: float32 [27, 64, 32], replicated
- grad_three: float32 [27, 256, 64], replicated
- grad_four: float32 [32, 256], replicated
The draws below stay inside these ranges and needn't reach their ends.
All inputs are finite; a program needn't handle non-finite values.
Results may differ from the reference program's by a relative error of at most 0.027.
Values may be sent and summed in bfloat16 or wider, within the bound.
A program may use at most 128 MiB of HBM per device.

```python
import math
import jax
import jax.numpy as jnp
from jax import lax

C1 = 32
C2 = 64
C3 = 256
NZ = 64
NX = 32
NY = 1024


def levels(stream_key, extent, pieces, least, largest):
    factor_of = 1.0
    for position, shards_of in pieces:
        heights = jax.random.uniform(jax.random.fold_in(jax.random.fold_in(stream_key, 6), position), (shards_of,), jnp.float32, least / len(pieces), largest / len(pieces))
        factor_of = factor_of * jnp.repeat(jnp.exp(heights), extent[position] // shards_of).reshape((-1,) + (1,) * (len(extent) - 1 - position))
    return factor_of


def noise(own_key, extent, width, bound, pieces=(), kind=jnp.bfloat16):
    values = jax.random.normal(own_key, extent, jnp.float32) * width
    if len(pieces) > 0:
        values = levels(own_key, extent, pieces, -0.22, 0.18) * values
    return jnp.clip(values, min=-bound, max=bound).astype(kind)


def setup_inputs(seed: int = 0) -> dict:
    splits = jax.random.split(jax.random.key(seed), 7)
    volume = noise(splits[0], (C1, NZ, NX, NY), 1.0, 6.0, ((1, 8), (2, 4), (3, 8)))
    cotangent = noise(splits[1], (C1, NZ, NX, NY), 1.0, 6.0, ((1, 8), (2, 4), (3, 8)))
    weight_one = noise(splits[2], (27, C1, C1), (27 * C1) ** -0.5, 0.21875)
    weight_two = noise(splits[3], (27, C2, C1), (27 * C1) ** -0.5, 0.21875)
    weight_three = noise(splits[4], (27, C3, C2), (27 * C2) ** -0.5, 0.15625)
    weight_four = noise(splits[5], (C1, C3), C3 ** -0.5, 0.375)
    return dict(volume=volume, cotangent=cotangent, weight_one=weight_one, weight_two=weight_two, weight_three=weight_three, weight_four=weight_four)


inv_root_eight = 1.0 / math.sqrt(8.0)
layout_names = ('NCDHW', 'OIDHW', 'NCDHW')

def slope(pre):
    sig = jax.nn.sigmoid(pre)
    return sig * (1.0 + pre * (1.0 - sig))

def pad_one(field):
    return jnp.pad(field, ((0, 0), (1, 1), (1, 1), (1, 1)))

def conv_padded(padded, weight):
    kernel = weight.astype(jnp.float32).reshape(3, 3, 3, weight.shape[1], weight.shape[2])
    kernel = jnp.transpose(kernel, (3, 4, 0, 1, 2))
    result = lax.conv_general_dilated(padded.astype(jnp.float32)[None], kernel, (1, 1, 1), 'VALID', dimension_numbers=layout_names, precision=lax.Precision.HIGHEST)
    return result[0]

def conv_transpose(padded_grad, weight):
    kernel = weight.astype(jnp.float32).reshape(3, 3, 3, weight.shape[1], weight.shape[2])[::-1, ::-1, ::-1]
    kernel = jnp.transpose(kernel, (4, 3, 0, 1, 2))
    result = lax.conv_general_dilated(padded_grad.astype(jnp.float32)[None], kernel, (1, 1, 1), 'VALID', dimension_numbers=layout_names, precision=lax.Precision.HIGHEST)
    return result[0]

def weight_grad(grad, padded_in):
    result = lax.conv_general_dilated(padded_in.astype(jnp.float32)[:, None], grad.astype(jnp.float32)[:, None], (1, 1, 1), 'VALID', dimension_numbers=layout_names, precision=lax.Precision.HIGHEST)
    result = jnp.transpose(result, (2, 3, 4, 1, 0))
    return result.reshape(27, grad.shape[0], padded_in.shape[0])

def project(matrix, field):
    return jnp.einsum('oc,czxy->ozxy', matrix.astype(jnp.float32), field.astype(jnp.float32), precision=lax.Precision.HIGHEST)

def project_back(matrix, field):
    return jnp.einsum('oc,ozxy->czxy', matrix.astype(jnp.float32), field.astype(jnp.float32), precision=lax.Precision.HIGHEST)

def outer_sum(left, right):
    return jnp.einsum('ozxy,czxy->oc', left.astype(jnp.float32), right.astype(jnp.float32), precision=lax.Precision.HIGHEST)

def pool_sum(field, factor):
    channels, size_z, size_x, size_y = field.shape
    blocks = field.reshape(channels, size_z // factor, factor, size_x // factor, factor, size_y // factor, factor)
    return lax.optimization_barrier(jnp.sum(blocks.astype(jnp.float32), axis=(2, 4, 6)))

def upsample(field, factor):
    channels, size_z, size_x, size_y = field.shape
    wide = jnp.broadcast_to(field[:, :, None, :, None, :, None], (channels, size_z, factor, size_x, factor, size_y, factor))
    return wide.reshape(channels, size_z * factor, size_x * factor, size_y * factor)

def reference(volume, cotangent, weight_one, weight_two, weight_three, weight_four):
    cells = NZ * NX * NY
    padded_in = pad_one(volume)
    pre_one = conv_padded(padded_in, weight_one)
    act_one = jax.nn.silu(pre_one).astype(jnp.bfloat16)
    pool_one = (pool_sum(act_one, 2) * inv_root_eight).astype(jnp.bfloat16)
    padded_pool = pad_one(pool_one)
    pre_two = conv_padded(padded_pool, weight_two)
    act_two = jax.nn.silu(pre_two).astype(jnp.bfloat16)
    coarse_in = (pool_sum(act_two, 4) * 0.125).astype(jnp.bfloat16)
    padded_coarse = pad_one(coarse_in)
    pre_three = conv_padded(padded_coarse, weight_three)
    act_three = jax.nn.silu(pre_three).astype(jnp.bfloat16)
    coarse_out = project(weight_four, act_three).astype(jnp.bfloat16)
    output = (act_one.astype(jnp.float32) + upsample(coarse_out, 8).astype(jnp.float32)).astype(jnp.bfloat16)
    coarse_grad = pool_sum(cotangent, 8).astype(jnp.bfloat16)
    coarse_scale = 1.0 / math.sqrt(cells / 512.0)
    grad_four = outer_sum(coarse_grad, act_three) * coarse_scale
    grad_act3 = project_back(weight_four, coarse_grad)
    grad_pre3 = (grad_act3 * slope(pre_three)).astype(jnp.bfloat16)
    grad_three = weight_grad(grad_pre3, padded_coarse) * coarse_scale
    grad_coarse = conv_transpose(pad_one(grad_pre3), weight_three)
    grad_pre2 = (upsample(grad_coarse, 4) * 0.125 * slope(pre_two)).astype(jnp.bfloat16)
    grad_two = weight_grad(grad_pre2, padded_pool) * (1.0 / math.sqrt(cells / 8.0))
    grad_pool = conv_transpose(pad_one(grad_pre2), weight_two)
    grad_act1 = cotangent.astype(jnp.float32) + upsample(grad_pool, 2) * inv_root_eight
    grad_pre1 = (grad_act1 * slope(pre_one)).astype(jnp.bfloat16)
    grad_one = weight_grad(grad_pre1, padded_in) * (1.0 / math.sqrt(cells * 1.0))
    grad_volume = conv_transpose(pad_one(grad_pre1), weight_one).astype(jnp.bfloat16)
    return (output, grad_volume, grad_one, grad_two, grad_three, grad_four)
```

```python
import functools
import itertools
import math

import jax
import jax.numpy as jnp
from jax import lax
from jax.experimental import pallas as pl
from jax.experimental.pallas import tpu as pltpu
from jax.sharding import PartitionSpec as P

MESH = pl.DeviceIdType.MESH
BF = jnp.bfloat16
F32 = jnp.float32
INV8 = 1.0 / math.sqrt(8.0)
STEPS = [d for d in itertools.product((-1, 0, 1), repeat=3) if d != (0, 0, 0)]

NN = ((1,), (0,))
NT = ((1,), (1,))
TN = ((0,), (0,))


def dot(a, b, dims=NN):
    return lax.dot_general(a, b, (dims, ((), ())), preferred_element_type=F32)


def rows_cols(shape):
    return (
        lax.broadcasted_iota(jnp.int32, shape, 0),
        lax.broadcasted_iota(jnp.int32, shape, 1),
    )


def hot(cond):
    return jnp.where(cond, 1.0, 0.0).astype(BF)


def roll(a, shift):
    return pltpu.roll(a, shift % a.shape[1], 1)


def silu_slope(pre):
    sig = 0.5 * (1.0 + jnp.tanh(0.5 * pre))
    act = pre * sig
    return act, sig + act * (1.0 - sig)


def split(a):
    high = a.astype(BF)
    return high, (a - high.astype(F32)).astype(BF)


class Place:
    def __init__(self, sizes):
        self.size = dict(zip(("x", "y", "z"), sizes))
        self.at = {
            "x": lax.axis_index("gx"),
            "y": lax.axis_index("gy"),
            "z": lax.axis_index("gz"),
        }

    def near(self, axis, step):
        size = self.size[axis]
        return lax.rem(self.at[axis] + (step + size), size)

    def device(self, dz, dx, dy):
        return (self.near("x", dx), self.near("y", dy), self.near("z", dz))

    def inside(self, axis, step):
        if step == 0:
            return None
        if step < 0:
            return self.at[axis] > 0
        return self.at[axis] < self.size[axis] - 1


class Halo:
    def __init__(self, place, pad, face, got, send, recv, nz, nx, ch, ylen):
        self.place, self.pad, self.face, self.got = place, pad, face, got
        self.send, self.recv = send, recv
        self.nz, self.nx, self.ch, self.ylen = nz, nx, ch, ylen

    def put(self, z, value):
        self.pad[z + 1, self.ch : self.ch * (self.nx + 1), :] = value

    def start(self):
        nz, nx, ch = self.nz, self.nx, self.ch
        r, c = rows_cols((32, nz * 128))
        edge = jnp.where(r >= 16, self.ylen - 1, 0)
        pick = hot(((r & 15) == (c >> 7)) & ((c & 127) == edge))
        own = jnp.concatenate(
            [self.pad[z + 1, ch : ch * (nx + 1), :] for z in range(nz)], axis=1
        )
        both = dot(pick, own, NT).astype(BF)
        self.face[0] = both[:16]
        self.face[1] = both[16:]
        self.copies = []
        for i, (dz, dx, dy) in enumerate(STEPS):
            if dy == 0:
                zs = {-1: (1, 1), 0: (1, nz), 1: (nz, 1)}[dz]
                xs = {-1: (ch, ch), 0: (ch, nx * ch), 1: (nx * ch, ch)}[dx]
                zd = {-1: nz + 1, 0: 1, 1: 0}[dz]
                xd = {-1: (nx + 1) * ch, 0: ch, 1: 0}[dx]
                src = self.pad.at[pl.ds(zs[0], zs[1]), pl.ds(xs[0], xs[1])]
                dst = self.pad.at[pl.ds(zd, zs[1]), pl.ds(xd, xs[1])]
            else:
                side = 0 if dy == 1 else 1
                src = self.face.at[1 - side]
                dst = self.got.at[1 - dx, side, 1 - dz]
            copy = pltpu.make_async_remote_copy(
                src_ref=src,
                dst_ref=dst,
                send_sem=self.send.at[i],
                recv_sem=self.recv.at[i],
                device_id=self.place.device(dz, dx, dy),
                device_id_type=MESH,
            )
            copy.start()
            self.copies.append(copy)

    def arrive(self):
        for copy in self.copies:
            copy.wait_recv()
        nz, nx, ch = self.nz, self.nx, self.ch
        at, size = self.place.at, self.place.size
        plane = jnp.zeros(self.pad.shape[1:], BF)
        column = jnp.zeros((nz + 2, ch, 128), BF)

        @pl.when(at["z"] == 0)
        def _():
            self.pad[0] = plane

        @pl.when(at["z"] == size["z"] - 1)
        def _():
            self.pad[nz + 1] = plane

        @pl.when(at["x"] == 0)
        def _():
            self.pad[:, 0:ch, :] = column

        @pl.when(at["x"] == size["x"] - 1)
        def _():
            self.pad[:, (nx + 1) * ch :, :] = column

    def columns(self):
        nz, nx, ch = self.nz, self.nx, self.ch
        at, size = self.place.at, self.place.size
        r, c = rows_cols((96, 128))
        group, z = r >> 4, r & 15
        side = jnp.where(group >= 3, 1, 0)
        dz = group - 3 * side
        zp = c & 15
        first, last = (
            jnp.where(at["z"] > 0, 0, -1),
            jnp.where(at["z"] < size["z"] - 1, nz + 1, -1),
        )
        low, high = (
            jnp.where(at["y"] > 0, 0, -1),
            jnp.where(at["y"] < size["y"] - 1, 1, -1),
        )
        mid = (dz == 1) & (z < nz) & (zp == z + 1)
        below = (dz == 0) & (z == nz - 1) & (zp == first)
        above = (dz == 2) & (z == 0) & (zp == last)
        lane = (side == (c >> 4)) & ((side == low) | (side == high))
        pick = hot((mid | below | above) & lane)
        parts = []
        for dx in range(3):
            wide = slice(0, nx * ch)
            if dx == 0:
                wide = slice((nx - 1) * ch, nx * ch)
            if dx == 2:
                wide = slice(0, ch)
            src = self.got[dx].reshape(96, nx * ch)[:, wide]
            part = dot(src, pick, TN)
            if dx != 1:
                part = jnp.where(self.place.inside("x", dx - 1), part, 0.0)
            parts.append(part.astype(BF))
        return jnp.concatenate(parts, axis=0)

    def shifted(self):
        cols = self.columns()
        lane = rows_cols(cols.shape)[1]
        for zp in range(self.nz + 2):
            base = self.pad[zp]
            low = jnp.where(lane == 0, roll(cols, -zp), roll(base, 1))
            end = self.ylen - 1
            high = jnp.where(lane == end, roll(cols, end - 16 - zp), roll(base, -1))
            yield zp, (low, base, high)

    def finish(self):
        for copy in self.copies:
            copy.wait_send()


def fill_fine(halo, u):
    rows = (halo.nx + 2) * halo.ch
    for zp, parts in halo.shifted():
        for ky, part in enumerate(parts):
            if zp <= 5:
                u[zp, ky * rows : (ky + 1) * rows, 0:128] = part
            if zp >= 4:
                u[zp - 4, ky * rows : (ky + 1) * rows, 128:256] = part


def fill_half(halo, u):
    before = None
    for zp, parts in halo.shifted():
        if before is not None:
            j = zp - 1
            for ky in range(3):
                lane = rows_cols(parts[ky].shape)[1]
                both = jnp.where(lane < 64, before[ky], roll(parts[ky], 64))
                if j <= 2:
                    u[j * 3 + ky, :, 0:128] = both
                if j >= 2:
                    u[(j - 2) * 3 + ky, :, 128:256] = both
        before = parts


def put_half(halo, value):
    lane = rows_cols((value.shape[0], 128))[1]
    for z in range(4):
        half = value[:, 128 * (z // 2) : 128 * (z // 2) + 128]
        if z % 2:
            half = roll(half, 64)
        halo.put(z, jnp.where(lane < 64, half, jnp.zeros_like(half)))


def toeplitz(dst, blocks, nx, rows, width):
    dst[...] = jnp.zeros(dst.shape, BF)
    for kz, ky in itertools.product(range(3), range(3)):
        band = jnp.concatenate([blocks(kz, kx, ky) for kx in range(3)], axis=1)
        base = (kz * 3 + ky) * (nx + 2) * width
        for x in range(nx):
            dst[rows * x : rows * (x + 1), base + width * x : base + width * (x + 3)] = band


def coarse_start(place, box, send, recv):
    copies = []
    for i, (dz, dx, dy) in enumerate(STEPS):
        copy = pltpu.make_async_remote_copy(
            src_ref=box.at[1, 1, 1],
            dst_ref=box.at[1 - dz, 1 - dx, 1 - dy],
            send_sem=send.at[i],
            recv_sem=recv.at[i],
            device_id=place.device(dz, dx, dy),
            device_id_type=MESH,
        )
        copy.start()
        copies.append(copy)
    return copies


def coarse_shifts(place, box):
    wide = []
    for dz, dx in itertools.product((-1, 0, 1), (-1, 0, 1)):
        rows = []
        for dy in (-1, 0, 1):
            block = box[dz + 1, dx + 1, dy + 1]
            for axis, step in (("z", dz), ("x", dx), ("y", dy)):
                if step:
                    block = jnp.where(place.inside(axis, step), block, jnp.zeros_like(block))
            rows.append(block)
        wide.append(jnp.concatenate(rows, axis=0))
    wide = jnp.concatenate(wide, axis=1)
    r, c = rows_cols((48, 48))
    pick = hot(c == (r & 15) + (r >> 4) + 15)
    return dot(pick, wide).astype(BF)


def kernel(
    sizes, vol, cot, w1, w2, w3, w4,
    out, gvol, p1, p2, p3, p4,
    v_pad, v_face, v_got, q_pad, q_face, q_got,
    h_pad, h_face, h_got, g_pad, g_face, g_got,
    u1, ug, u2, uh, t1, tt1, t2, tt2, w3c,
    sl1, act1, cot1, g1, box_in, box_gp, send, recv,
):
    place = Place(sizes)
    barrier = pltpu.get_barrier_semaphore()
    for step in STEPS:
        pl.semaphore_signal(
            barrier, inc=1, device_id=place.device(*step), device_id_type=MESH
        )
    r, c = rows_cols((256, 256))
    perm = hot(((r & 31) == (c >> 3)) & ((r >> 5) == (c & 7)))
    back = hot(((c & 31) == (r >> 3)) & ((c >> 5) == (r & 7)))

    def two(ref, zz):
        return jnp.concatenate(
            [ref[:, zz].reshape(256, 128), ref[:, zz + 4].reshape(256, 128)], axis=1
        )

    hv = Halo(place, v_pad, v_face, v_got, send.at[0], recv.at[0], 8, 8, 32, 128)
    hq = Halo(place, q_pad, q_face, q_got, send.at[1], recv.at[1], 4, 4, 32, 64)
    hh = Halo(place, h_pad, h_face, h_got, send.at[2], recv.at[2], 4, 4, 64, 64)
    hg = Halo(place, g_pad, g_face, g_got, send.at[3], recv.at[3], 8, 8, 32, 128)
    for zz in range(4):
        rows = dot(perm, two(vol, zz)).astype(BF)
        hv.put(zz, rows[:, :128])
        hv.put(zz + 4, rows[:, 128:])
    pl.semaphore_wait(barrier, len(STEPS))
    hv.start()

    for zz in range(4):
        cot1[zz] = dot(perm, two(cot, zz)).astype(BF)
    r, c = rows_cols((32, 32))
    eye = hot(r == c)
    toeplitz(t1, lambda kz, kx, ky: w1[kz * 9 + kx * 3 + ky], 8, 32, 32)
    toeplitz(t2, lambda kz, kx, ky: w2[kz * 9 + kx * 3 + ky], 4, 64, 32)
    flat1 = dot(eye, w1[...].reshape(864, 32), NT).astype(BF)
    flat2 = dot(eye, w2[...].reshape(1728, 32), NT).astype(BF)

    def turned(flat, width):
        def block(kz, kx, ky):
            k = (2 - kz) * 9 + (2 - kx) * 3 + (2 - ky)
            return flat[:, k * width : (k + 1) * width]

        return block

    toeplitz(tt1, turned(flat1, 32), 8, 32, 32)
    toeplitz(tt2, turned(flat2, 64), 4, 32, 64)
    for k in range(27):
        w3c[:, 64 * k : 64 * (k + 1)] = w3[k]
    cg = jnp.sum(cot[...].astype(F32), axis=(1, 2))
    cg = cg + roll(cg, -1)
    cg = cg + roll(cg, -2)
    cg = (cg + roll(cg, -4)).astype(BF)

    hv.arrive()
    fill_fine(hv, u1)
    for zz in range(4):
        pre = dot(t1[...], u1[zz : zz + 3].reshape(2880, 256))
        act, slope = silu_slope(pre)
        act1[zz] = act.astype(BF)
        sl1[zz] = slope
    r, c = rows_cols((512, 256))
    z2 = 2 * ((r >> 7) & 1) + (r >> 8)
    pick = hot(((c >> 6) == z2) & ((r & 127) == 2 * (c & 63)))
    pooled = []
    for a, b in ((0, 1), (2, 3)):
        s = act1[a].astype(F32) + act1[b].astype(F32)
        s = jnp.sum(s.reshape(4, 2, 32, 256), axis=1).reshape(128, 256)
        s = s + roll(s, -1)
        pooled.append((s * INV8).astype(BF))
    q1 = dot(jnp.concatenate(pooled, axis=1), pick).astype(BF)
    put_half(hq, q1)
    hq.start()

    hq.arrive()
    fill_half(hq, u2)
    pre2 = dot(t2[...], u2[...].reshape(1728, 256))
    act2, slope2 = silu_slope(pre2)
    s = jnp.sum(act2.astype(BF).astype(F32).reshape(4, 64, 256), axis=0)
    s = s[:, :128] + s[:, 128:]
    s = s + roll(s, 64)
    s = s + roll(s, -1)
    s = s + roll(s, -2)
    cin = (s * 0.125).astype(BF)
    zero = jnp.zeros((64, 128), BF)
    r, c = rows_cols((16, 128))
    own = dot(hot(c == 4 * r), jnp.concatenate([cin, zero], axis=0), NT)
    own += dot(hot(c == 8 * r), jnp.concatenate([zero, cg, zero[:32]], axis=0), NT)
    own = own.astype(BF)
    box_in[1, 1, 1] = own
    first = coarse_start(place, box_in, send.at[4], recv.at[4])
    for copy in first:
        copy.wait_recv()
    near = coarse_shifts(place, box_in)

    def tap(kz, kx, ky, width, valid):
        base = (kz * 3 + kx) * width
        return near[16 * ky : 16 * (ky + 1), base : base + valid]

    taps = list(itertools.product(range(3), range(3), range(3)))
    x3 = jnp.concatenate([tap(*k, 128, 64) for k in taps], axis=1)
    pre3 = dot(x3, w3c[...], NT)
    act3, slope3 = silu_slope(pre3)
    act3 = act3.astype(BF)
    cgt = own[:, 64:96]
    gp3 = (dot(cgt, w4[...]) * slope3).astype(BF)
    box_gp[1, 1, 1] = gp3
    second = coarse_start(place, box_gp, send.at[5], recv.at[5])
    co = dot(w4[...], act3, NT).astype(BF)
    p4[...] = dot(cgt, act3, TN)
    p3[...] = dot(gp3, x3, TN)
    r, c = rows_cols((16, 128))
    co = dot(co, hot(r == (c >> 3)))
    co = jnp.concatenate([jnp.concatenate([co] * 8, axis=0)] * 2, axis=1)
    for zz in range(4):
        rows = dot(back, (act1[zz].astype(F32) + co).astype(BF)).astype(BF)
        out[:, zz] = rows[:, :128].reshape(32, 8, 128)
        out[:, zz + 4] = rows[:, 128:].reshape(32, 8, 128)
    for copy in second:
        copy.wait_recv()
    near = coarse_shifts(place, box_gp)
    x3t = jnp.concatenate(
        [tap(2 - kz, 2 - kx, 2 - ky, 256, 256) for kz, kx, ky in taps], axis=1
    )
    gc = dot(x3t, w3[...].reshape(6912, 64))
    r, c = rows_cols((16, 256))
    pick = hot(r == ((c & 63) >> 2))
    up = sum(dot(part, pick, TN) for part in split(gc)) * 0.125
    gp2 = (jnp.concatenate([up] * 4, axis=0) * slope2).astype(BF)
    put_half(hh, gp2)
    hh.start()
    for kz in range(3):
        g = dot(gp2, u2[3 * kz : 3 * kz + 3].reshape(576, 256), NT)
        for ky in range(3):
            p2[kz * 3 + ky] = sum(
                g[64 * x : 64 * x + 64, ky * 192 + 32 * x : ky * 192 + 32 * x + 96]
                for x in range(4)
            )
    hh.arrive()
    fill_half(hh, uh)
    gpool = dot(tt2[...], uh[...].reshape(3456, 256))
    r, c = rows_cols((256, 256))
    parts = split(gpool)
    for h in range(2):
        pick = hot(((r >> 6) == 2 * (c >> 7) + h) & ((r & 63) == ((c & 127) >> 1)))
        up = sum(dot(part, pick) for part in parts) * INV8
        up = jnp.concatenate(
            [up[32 * (x // 2) : 32 * (x // 2) + 32] for x in range(8)], axis=0
        )
        for zz in (2 * h, 2 * h + 1):
            gp1 = ((cot1[zz].astype(F32) + up) * sl1[zz]).astype(BF)
            hg.put(zz, gp1[:, :128])
            hg.put(zz + 4, gp1[:, 128:])
            g1[:, 256 * zz : 256 * zz + 256] = gp1
    hg.start()
    for kz in range(3):
        uc = jnp.concatenate([u1[kz + zz] for zz in range(4)], axis=1)
        g = dot(g1[...], uc, NT)
        for ky in range(3):
            p1[kz * 3 + ky] = sum(
                g[32 * x : 32 * x + 32, ky * 320 + 32 * x : ky * 320 + 32 * x + 96]
                for x in range(8)
            )
    hg.arrive()
    fill_fine(hg, ug)
    for zz in range(4):
        rows = dot(tt1[...], ug[zz : zz + 3].reshape(2880, 256)).astype(BF)
        rows = dot(back, rows).astype(BF)
        gvol[:, zz] = rows[:, :128].reshape(32, 8, 128)
        gvol[:, zz + 4] = rows[:, 128:].reshape(32, 8, 128)
    for halo in (hv, hq, hh, hg):
        halo.finish()
    for copy in first + second:
        copy.wait_send()


def halo_scratch(nz, nx, ch):
    return [
        pltpu.VMEM((nz + 2, (nx + 2) * ch, 128), BF),
        pltpu.VMEM((2, 16, nx * ch), BF),
        pltpu.VMEM((3, 2, 3, 16, nx * ch), BF),
    ]


def body(sizes, cells, vol, cot, w1, w2, w3, w4):
    shape = jax.ShapeDtypeStruct
    field = shape((32, 8, 8, 128), BF)
    vmem = pl.BlockSpec(memory_space=pltpu.VMEM)
    out, gvol, p1, p2, p3, p4 = pl.pallas_call(
        functools.partial(kernel, sizes),
        out_shape=[
            field,
            field,
            shape((9, 32, 96), F32),
            shape((9, 64, 96), F32),
            shape((256, 1728), F32),
            shape((32, 256), F32),
        ],
        in_specs=[vmem] * 6,
        out_specs=[vmem] * 6,
        scratch_shapes=[
            *halo_scratch(8, 8, 32),
            *halo_scratch(4, 4, 32),
            *halo_scratch(4, 4, 64),
            *halo_scratch(8, 8, 32),
            pltpu.VMEM((6, 960, 256), BF),
            pltpu.VMEM((6, 960, 256), BF),
            pltpu.VMEM((9, 192, 256), BF),
            pltpu.VMEM((9, 384, 256), BF),
            pltpu.VMEM((256, 2880), BF),
            pltpu.VMEM((256, 2880), BF),
            pltpu.VMEM((256, 1728), BF),
            pltpu.VMEM((128, 3456), BF),
            pltpu.VMEM((256, 1728), BF),
            pltpu.VMEM((4, 256, 256), F32),
            pltpu.VMEM((4, 256, 256), BF),
            pltpu.VMEM((4, 256, 256), BF),
            pltpu.VMEM((256, 1024), BF),
            pltpu.VMEM((3, 3, 3, 16, 128), BF),
            pltpu.VMEM((3, 3, 3, 16, 256), BF),
            pltpu.SemaphoreType.DMA((6, 26)),
            pltpu.SemaphoreType.DMA((6, 26)),
        ],
        compiler_params=pltpu.CompilerParams(
            collective_id=0, has_side_effects=True, vmem_limit_bytes=56 * 1024 * 1024
        ),
        name="unet",
    )(vol, cot, w1, w2, w3, w4)
    sum_three = lax.psum(p3.astype(BF), ("gx", "gy", "gz")).astype(F32)
    sum_one, sum_two, sum_four = lax.psum((p1, p2, p4), ("gx", "gy", "gz"))

    def ordered(part):
        part = part.reshape(3, 3, part.shape[1], 3, 32)
        return jnp.transpose(part, (0, 3, 1, 2, 4)).reshape(27, part.shape[2], 32)

    coarse = 1.0 / math.sqrt(cells / 512.0)
    three = jnp.transpose(sum_three.reshape(256, 27, 64), (1, 0, 2))
    return (
        out,
        gvol,
        ordered(sum_one) * (1.0 / math.sqrt(cells * 1.0)),
        ordered(sum_two) * (1.0 / math.sqrt(cells / 8.0)),
        three * coarse,
        sum_four * coarse,
    )


def solution(mesh):
    sizes = (mesh.shape["gx"], mesh.shape["gy"], mesh.shape["gz"])
    cells = 32 * 8 * 8 * 128 // 32 * sizes[0] * sizes[1] * sizes[2]
    field = P(None, "gz", "gx", "gy")
    return jax.shard_map(
        functools.partial(body, sizes, cells),
        mesh=mesh,
        in_specs=(field, field, P(), P(), P(), P()),
        out_specs=(field, field, P(), P(), P(), P()),
        check_vma=False,
    )
```

```python
import functools
import itertools
import math

import jax
import jax.numpy as jnp
from jax import lax
from jax.experimental import pallas as pl
from jax.experimental.pallas import tpu as pltpu
from jax.sharding import PartitionSpec as P

MESH = pl.DeviceIdType.MESH
BF = jnp.bfloat16
F32 = jnp.float32
INV8 = 1.0 / math.sqrt(8.0)
STEPS = [d for d in itertools.product((-1, 0, 1), repeat=3) if d != (0, 0, 0)]

NN = ((1,), (0,))
NT = ((1,), (1,))
TN = ((0,), (0,))


def dot(a, b, dims=NN):
    return lax.dot_general(a, b, (dims, ((), ())), preferred_element_type=F32)


def rows_cols(shape):
    return (
        lax.broadcasted_iota(jnp.int32, shape, 0),
        lax.broadcasted_iota(jnp.int32, shape, 1),
    )


def hot(cond):
    return jnp.where(cond, 1.0, 0.0).astype(BF)


def roll(a, shift):
    return pltpu.roll(a, shift % a.shape[1], 1)


def silu_slope(pre):
    sig = 0.5 * (1.0 + jnp.tanh(0.5 * pre))
    act = pre * sig
    return act, sig + act * (1.0 - sig)


def split(a):
    high = a.astype(BF)
    return high, (a - high.astype(F32)).astype(BF)


class Place:
    def __init__(self, sizes):
        self.size = dict(zip(("x", "y", "z"), sizes))
        self.at = {
            "x": lax.axis_index("gx"),
            "y": lax.axis_index("gy"),
            "z": lax.axis_index("gz"),
        }

    def near(self, axis, step):
        size = self.size[axis]
        return lax.rem(self.at[axis] + (step + size), size)

    def device(self, dz, dx, dy):
        return (self.near("x", dx), self.near("y", dy), self.near("z", dz))

    def inside(self, axis, step):
        if step == 0:
            return None
        if step < 0:
            return self.at[axis] > 0
        return self.at[axis] < self.size[axis] - 1


class Halo:
    def __init__(self, place, pad, face, got, send, recv, nz, nx, ch, ylen):
        self.place, self.pad, self.face, self.got = place, pad, face, got
        self.send, self.recv = send, recv
        self.nz, self.nx, self.ch, self.ylen = nz, nx, ch, ylen

    def put(self, z, value):
        self.pad[z + 1, self.ch : self.ch * (self.nx + 1), :] = value

    def start(self):
        nz, nx, ch = self.nz, self.nx, self.ch
        r, c = rows_cols((32, nz * 128))
        edge = jnp.where(r >= 16, self.ylen - 1, 0)
        pick = hot(((r & 15) == (c >> 7)) & ((c & 127) == edge))
        own = jnp.concatenate(
            [self.pad[z + 1, ch : ch * (nx + 1), :] for z in range(nz)], axis=1
        )
        both = dot(pick, own, NT).astype(BF)
        self.face[0] = both[:16]
        self.face[1] = both[16:]
        self.copies = []
        for i, (dz, dx, dy) in enumerate(STEPS):
            if dy == 0:
                zs = {-1: (1, 1), 0: (1, nz), 1: (nz, 1)}[dz]
                xs = {-1: (ch, ch), 0: (ch, nx * ch), 1: (nx * ch, ch)}[dx]
                zd = {-1: nz + 1, 0: 1, 1: 0}[dz]
                xd = {-1: (nx + 1) * ch, 0: ch, 1: 0}[dx]
                src = self.pad.at[pl.ds(zs[0], zs[1]), pl.ds(xs[0], xs[1])]
                dst = self.pad.at[pl.ds(zd, zs[1]), pl.ds(xd, xs[1])]
            else:
                side = 0 if dy == 1 else 1
                src = self.face.at[1 - side]
                dst = self.got.at[1 - dx, side, 1 - dz]
            copy = pltpu.make_async_remote_copy(
                src_ref=src,
                dst_ref=dst,
                send_sem=self.send.at[i],
                recv_sem=self.recv.at[i],
                device_id=self.place.device(dz, dx, dy),
                device_id_type=MESH,
            )
            copy.start()
            self.copies.append(copy)

    def arrive(self):
        for copy in self.copies:
            copy.wait_recv()
        nz, nx, ch = self.nz, self.nx, self.ch
        at, size = self.place.at, self.place.size
        plane = jnp.zeros(self.pad.shape[1:], BF)
        column = jnp.zeros((nz + 2, ch, 128), BF)

        @pl.when(at["z"] == 0)
        def _():
            self.pad[0] = plane

        @pl.when(at["z"] == size["z"] - 1)
        def _():
            self.pad[nz + 1] = plane

        @pl.when(at["x"] == 0)
        def _():
            self.pad[:, 0:ch, :] = column

        @pl.when(at["x"] == size["x"] - 1)
        def _():
            self.pad[:, (nx + 1) * ch :, :] = column

    def columns(self):
        nz, nx, ch = self.nz, self.nx, self.ch
        at, size = self.place.at, self.place.size
        r, c = rows_cols((96, 128))
        group, z = r >> 4, r & 15
        side = jnp.where(group >= 3, 1, 0)
        dz = group - 3 * side
        zp = c & 15
        first, last = (
            jnp.where(at["z"] > 0, 0, -1),
            jnp.where(at["z"] < size["z"] - 1, nz + 1, -1),
        )
        low, high = (
            jnp.where(at["y"] > 0, 0, -1),
            jnp.where(at["y"] < size["y"] - 1, 1, -1),
        )
        mid = (dz == 1) & (z < nz) & (zp == z + 1)
        below = (dz == 0) & (z == nz - 1) & (zp == first)
        above = (dz == 2) & (z == 0) & (zp == last)
        lane = (side == (c >> 4)) & ((side == low) | (side == high))
        pick = hot((mid | below | above) & lane)
        parts = []
        for dx in range(3):
            wide = slice(0, nx * ch)
            if dx == 0:
                wide = slice((nx - 1) * ch, nx * ch)
            if dx == 2:
                wide = slice(0, ch)
            src = self.got[dx].reshape(96, nx * ch)[:, wide]
            part = dot(src, pick, TN)
            if dx != 1:
                part = jnp.where(self.place.inside("x", dx - 1), part, 0.0)
            parts.append(part.astype(BF))
        return jnp.concatenate(parts, axis=0)

    def shifted(self):
        cols = self.columns()
        lane = rows_cols(cols.shape)[1]
        for zp in range(self.nz + 2):
            base = self.pad[zp]
            low = jnp.where(lane == 0, roll(cols, -zp), roll(base, 1))
            end = self.ylen - 1
            high = jnp.where(lane == end, roll(cols, end - 16 - zp), roll(base, -1))
            yield zp, (low, base, high)

    def finish(self):
        for copy in self.copies:
            copy.wait_send()


def fill_fine(halo, u):
    rows = (halo.nx + 2) * halo.ch
    for zp, parts in halo.shifted():
        for ky, part in enumerate(parts):
            if zp <= 5:
                u[zp, ky * rows : (ky + 1) * rows, 0:128] = part
            if zp >= 4:
                u[zp - 4, ky * rows : (ky + 1) * rows, 128:256] = part


def fill_half(halo, u):
    before = None
    for zp, parts in halo.shifted():
        if before is not None:
            j = zp - 1
            for ky in range(3):
                lane = rows_cols(parts[ky].shape)[1]
                both = jnp.where(lane < 64, before[ky], roll(parts[ky], 64))
                if j <= 2:
                    u[j * 3 + ky, :, 0:128] = both
                if j >= 2:
                    u[(j - 2) * 3 + ky, :, 128:256] = both
        before = parts


def put_half(halo, value):
    lane = rows_cols((value.shape[0], 128))[1]
    for z in range(4):
        half = value[:, 128 * (z // 2) : 128 * (z // 2) + 128]
        if z % 2:
            half = roll(half, 64)
        halo.put(z, jnp.where(lane < 64, half, jnp.zeros_like(half)))


def toeplitz(dst, blocks, nx, rows, width):
    dst[...] = jnp.zeros(dst.shape, BF)
    for kz, ky in itertools.product(range(3), range(3)):
        band = jnp.concatenate([blocks(kz, kx, ky) for kx in range(3)], axis=1)
        base = (kz * 3 + ky) * (nx + 2) * width
        for x in range(nx):
            dst[rows * x : rows * (x + 1), base + width * x : base + width * (x + 3)] = band


def coarse_start(place, box, send, recv):
    copies = []
    for i, (dz, dx, dy) in enumerate(STEPS):
        copy = pltpu.make_async_remote_copy(
            src_ref=box.at[1, 1, 1],
            dst_ref=box.at[1 - dz, 1 - dx, 1 - dy],
            send_sem=send.at[i],
            recv_sem=recv.at[i],
            device_id=place.device(dz, dx, dy),
            device_id_type=MESH,
        )
        copy.start()
        copies.append(copy)
    return copies


def coarse_shifts(place, box):
    wide = []
    for dz, dx in itertools.product((-1, 0, 1), (-1, 0, 1)):
        rows = []
        for dy in (-1, 0, 1):
            block = box[dz + 1, dx + 1, dy + 1]
            for axis, step in (("z", dz), ("x", dx), ("y", dy)):
                if step:
                    block = jnp.where(place.inside(axis, step), block, jnp.zeros_like(block))
            rows.append(block)
        wide.append(jnp.concatenate(rows, axis=0))
    wide = jnp.concatenate(wide, axis=1)
    r, c = rows_cols((48, 48))
    pick = hot(c == (r & 15) + (r >> 4) + 15)
    width = box.shape[-1]
    return dot(pick, wide).astype(BF), wide[8:40, 4 * width : 5 * width]


class Group:
    def __init__(self, place, kind, send, recv):
        self.place, self.kind, self.send, self.recv = place, kind, send, recv
        size = place.size
        self.count = {
            "plane": size["x"] * size["z"],
            "line": size["y"],
            "chips": size["y"] // 2,
            "cores": 2,
        }[kind]

    def member(self, q):
        at, size = self.place.at, self.place.size
        if self.kind == "plane":
            x = lax.rem(at["x"] + q // size["z"], size["x"])
            z = lax.rem(at["z"] + lax.rem(q, size["z"]), size["z"])
            return (x, at["y"], z), x * size["z"] + z
        if self.kind == "line":
            y = lax.rem(at["y"] + q, size["y"])
            return (at["x"], y, at["z"]), y
        if self.kind == "chips":
            y = lax.rem(at["y"] + 2 * q, size["y"])
            return (at["x"], y, at["z"]), y // 2
        y = at["y"] + 1 - 2 * lax.rem(at["y"], 2)
        return (at["x"], y, at["z"]), lax.rem(y, 2)

    def start(self, src, dst):
        def one(q, carry):
            device, index = self.member(q)
            pltpu.make_async_remote_copy(
                src_ref=src(index),
                dst_ref=dst,
                send_sem=self.send,
                recv_sem=self.recv,
                device_id=device,
                device_id_type=MESH,
            ).start()
            return carry

        lax.fori_loop(1, self.count, one, 0)

    def _all(self, slots):
        ref = slots.at[pl.ds(0, self.count - 1)]
        return pltpu.make_async_remote_copy(
            src_ref=ref,
            dst_ref=ref,
            send_sem=self.send,
            recv_sem=self.recv,
            device_id=self.member(1)[0],
            device_id_type=MESH,
        )

    def arrive(self, slots):
        if self.count > 1:
            self._all(slots).wait_recv()

    def finish(self, slots):
        if self.count > 1:
            self._all(slots).wait_send()


class Total:
    def __init__(self, place, mine, landed, line, done, send, recv):
        self.mine, self.landed, self.line, self.done = mine, landed, line, done
        self.at = place.at
        self.me = place.at["x"] * place.size["z"] + place.at["z"]
        self.one = Group(place, "plane", send.at[0], recv.at[0])
        self.two = Group(place, "line", send.at[1], recv.at[1])
        self.three = Group(place, "plane", send.at[2], recv.at[2])

    def scatter(self):
        self.one.start(lambda index: self.mine.at[index], self.landed.at[self.me])
        self.landed[self.me] = self.mine[self.me]

    def cross(self):
        self.one.arrive(self.landed)
        self.line[self.at["y"]] = jnp.sum(self.landed[...], axis=0)
        own = self.line.at[self.at["y"]]
        self.two.start(lambda index: own, own)

    def gather(self):
        self.two.arrive(self.line)
        self.done[self.me] = jnp.sum(self.line[...], axis=0)
        own = self.done.at[self.me]
        self.three.start(lambda index: own, own)

    def arrive(self):
        self.three.arrive(self.done)

    def finish(self):
        self.one.finish(self.landed)
        self.two.finish(self.line)
        self.three.finish(self.done)


def kernel(
    sizes, scales, vol, cot, w1, w2, w3, w4,
    out, gvol, d1, d2, d3, d4,
    v_pad, v_face, v_got, q_pad, q_face, q_got,
    h_pad, h_face, h_got, g_pad, g_face, g_got,
    u1, ug, u2, uh, t1, tt1, t2, tt2,
    sl1, act1, cot1, g1, box_in, box_gp, send, recv,
    note, seen, near_y, tap_sum, tap_line, tap_all,
    m1, l1, y1, f1, m2, l2, y2, f2, gsend, grecv,
):
    place = Place(sizes)
    seen[...] = jnp.zeros(seen.shape, BF)
    barrier = pltpu.get_barrier_semaphore()
    partners = [place.device(*s) for s in STEPS if s[2] != 0 and s[:2] != (0, 0)]
    for device in partners:
        pl.semaphore_signal(barrier, inc=1, device_id=device, device_id_type=MESH)
    groups = [
        Group(place, kind, gsend.at[i], grecv.at[i])
        for i, kind in enumerate(("plane", "line", "plane", "chips", "cores"))
    ]
    gather, across, plane, chips, cores = groups
    total = len(partners)
    for group in (gather, across):

        def greet(q, carry, group=group):
            device = group.member(q)[0]
            pl.semaphore_signal(barrier, inc=1, device_id=device, device_id_type=MESH)
            return carry

        lax.fori_loop(1, group.count, greet, 0)
        total += group.count - 1
    ix, iy, iz = place.at["x"], place.at["y"], place.at["z"]
    nx, nz = place.size["x"], place.size["z"]
    me = ix * nz + iz
    m1[27:32] = jnp.zeros((5, 8, 128), F32)
    m2[27:32] = jnp.zeros((5, 16, 128), F32)
    r, c = rows_cols((256, 256))
    perm = hot(((r & 31) == (c >> 3)) & ((r >> 5) == (c & 7)))
    back = hot(((c & 31) == (r >> 3)) & ((c >> 5) == (r & 7)))

    def two(ref, zz):
        return jnp.concatenate(
            [ref[:, zz].reshape(256, 128), ref[:, zz + 4].reshape(256, 128)], axis=1
        )

    hv = Halo(place, v_pad, v_face, v_got, send.at[0], recv.at[0], 8, 8, 32, 128)
    hq = Halo(place, q_pad, q_face, q_got, send.at[1], recv.at[1], 4, 4, 32, 64)
    hh = Halo(place, h_pad, h_face, h_got, send.at[2], recv.at[2], 4, 4, 64, 64)
    hg = Halo(place, g_pad, g_face, g_got, send.at[3], recv.at[3], 8, 8, 32, 128)
    sum1 = Total(place, m1, l1, y1, f1, gsend.at[pl.ds(5, 3)], grecv.at[pl.ds(5, 3)])
    sum2 = Total(place, m2, l2, y2, f2, gsend.at[pl.ds(8, 3)], grecv.at[pl.ds(8, 3)])
    for zz in range(4):
        rows = dot(perm, two(vol, zz)).astype(BF)
        hv.put(zz, rows[:, :128])
        hv.put(zz + 4, rows[:, 128:])
    pl.semaphore_wait(barrier, total)
    hv.start()

    for zz in range(4):
        cot1[zz] = dot(perm, two(cot, zz)).astype(BF)
    r, c = rows_cols((32, 32))
    eye = hot(r == c)
    toeplitz(t1, lambda kz, kx, ky: w1[kz * 9 + kx * 3 + ky], 8, 32, 32)
    flat1 = dot(eye, w1[...].reshape(864, 32), NT).astype(BF)
    r, c = rows_cols((64, 64))
    flat2 = dot(hot(r == c), w2[...].reshape(864, 64), NT).astype(BF)

    def back_tap(kz, kx, ky):
        return (2 - kz) * 9 + (2 - kx) * 3 + (2 - ky)

    def turned(kz, kx, ky):
        k = back_tap(kz, kx, ky)
        return flat1[:, k * 32 : (k + 1) * 32]

    def straight(kz, kx, ky):
        k = kz * 9 + kx * 3 + ky
        return flat2[:, k * 32 : (k + 1) * 32]

    toeplitz(t2, straight, 4, 64, 32)
    toeplitz(tt1, turned, 8, 32, 32)
    toeplitz(tt2, lambda *k: w2[back_tap(*k)], 4, 32, 64)
    cg = jnp.sum(cot[...].astype(F32), axis=(1, 2))
    cg = cg + roll(cg, -1)
    cg = cg + roll(cg, -2)
    cg = (cg + roll(cg, -4)).astype(BF)

    hv.arrive()
    fill_fine(hv, u1)
    for zz in range(4):
        pre = dot(t1[...], u1[zz : zz + 3].reshape(2880, 256))
        act, slope = silu_slope(pre)
        act1[zz] = act.astype(BF)
        sl1[zz] = slope
    r, c = rows_cols((512, 256))
    z2 = 2 * ((r >> 7) & 1) + (r >> 8)
    pick = hot(((c >> 6) == z2) & ((r & 127) == 2 * (c & 63)))
    pooled = []
    for a, b in ((0, 1), (2, 3)):
        s = act1[a].astype(F32) + act1[b].astype(F32)
        s = jnp.sum(s.reshape(4, 2, 32, 256), axis=1).reshape(128, 256)
        s = s + roll(s, -1)
        pooled.append((s * INV8).astype(BF))
    q1 = dot(jnp.concatenate(pooled, axis=1), pick).astype(BF)
    put_half(hq, q1)
    hq.start()

    hq.arrive()
    fill_half(hq, u2)
    pre2 = dot(t2[...], u2[...].reshape(1728, 256))
    act2, slope2 = silu_slope(pre2)
    s = jnp.sum(act2.astype(BF).astype(F32).reshape(4, 64, 256), axis=0)
    s = s[:, :128] + s[:, 128:]
    s = s + roll(s, 64)
    s = s + roll(s, -1)
    s = s + roll(s, -2)
    cin = (s * 0.125).astype(BF)
    zero = jnp.zeros((64, 128), BF)
    r, c = rows_cols((16, 128))
    own = dot(hot(c == 4 * r), jnp.concatenate([cin, zero], axis=0), NT)
    own += dot(hot(c == 8 * r), jnp.concatenate([zero, cg, zero[:32]], axis=0), NT)
    own = own.astype(BF)
    box_in[1, 1, 1] = own
    first = coarse_start(place, box_in, send.at[4], recv.at[4])
    for copy in first:
        copy.wait_recv()
    near, own = coarse_shifts(place, box_in)
    note[...] = own
    gather.start(lambda index: note, seen.at[(iz + 1) * (nx + 2) + ix + 1])
    seen[(iz + 1) * (nx + 2) + ix + 1] = own

    def tap(kz, kx, ky, width, valid):
        base = (kz * 3 + kx) * width
        return near[16 * ky : 16 * (ky + 1), base : base + valid]

    taps = list(itertools.product(range(3), range(3), range(3)))
    x3 = jnp.concatenate([tap(*k, 128, 64) for k in taps], axis=1)
    pre3 = dot(x3, w3[...].reshape(1728, 256))
    act3, slope3 = silu_slope(pre3)
    act3 = act3.astype(BF)
    cgt = own[8:24, 64:96]
    gp3 = (dot(cgt, w4[...]) * slope3).astype(BF)
    box_gp[1, 1, 1] = gp3
    second = coarse_start(place, box_gp, send.at[5], recv.at[5])
    co = dot(w4[...], act3, NT).astype(BF)
    part4 = dot(cgt, act3, TN)
    for i in range(4):
        half, col = i % 2, 128 * (i // 2)
        m2[27 + i] = part4[16 * half : 16 * half + 16, col : col + 128]
    r, c = rows_cols((16, 128))
    co = dot(co, hot(r == (c >> 3)))
    co = jnp.concatenate([jnp.concatenate([co] * 8, axis=0)] * 2, axis=1)
    for zz in range(4):
        rows = dot(back, (act1[zz].astype(F32) + co).astype(BF)).astype(BF)
        out[:, zz] = rows[:, :128].reshape(32, 8, 128)
        out[:, zz + 4] = rows[:, 128:].reshape(32, 8, 128)
    for copy in second:
        copy.wait_recv()
    near = coarse_shifts(place, box_gp)[0]
    gc = sum(
        dot(w3[kz * 9 + kx * 3 + ky], tap(2 - kz, 2 - kx, 2 - ky, 256, 256), NT)
        for kz, kx, ky in taps
    )
    r, c = rows_cols((16, 256))
    pick = hot(r == ((c & 63) >> 2))
    up = sum(dot(part, pick) for part in split(gc)) * 0.125
    gp2 = (jnp.concatenate([up] * 4, axis=0) * slope2).astype(BF)
    put_half(hh, gp2)
    hh.start()
    lane = rows_cols((16, 128))[1]
    for kz in range(3):
        g = dot(u2[3 * kz : 3 * kz + 3].reshape(576, 256), gp2, NT)
        for ky, kx in itertools.product(range(3), range(3)):
            cut = [
                g[ky * 192 + 32 * (x + kx) :][:32, 128 * (x // 2) : 128 * (x // 2) + 128]
                for x in range(4)
            ]
            even, odd = cut[0] + cut[2], cut[1] + cut[3]
            low = (even + roll(odd, 64))[:16]
            high = (roll(even, 64) + odd)[16:]
            m2[kz * 9 + kx * 3 + ky] = jnp.where(lane < 64, low, high)
    sum2.scatter()
    gather.arrive(seen)
    for ky in range(3):
        near_y[ky] = seen[:, 7 + ky : 23 + ky, :]
    lane = rows_cols((16, 128))[1]
    pair = jnp.where(lane < 64, near_y[0], pltpu.roll(near_y[1], 64, 2))
    both = jnp.concatenate([pair, near_y[2]], axis=2)
    both = both.reshape(nz + 2, nx + 2, 16, 256)
    pre = sum(
        dot(
            both[kz : kz + nz, kx : kx + nx].reshape(nz * nx * 16, 256)[:, :192],
            w3[kz * 9 + kx * 3 : kz * 9 + kx * 3 + 3].reshape(192, 256),
        )
        for kz, kx in itertools.product(range(3), range(3))
    )
    slope = silu_slope(pre)[1]
    mid = near_y[1].reshape(nz + 2, nx + 2, 16, 128)[1 : nz + 1, 1 : nx + 1]
    mid = mid.reshape(nz * nx * 16, 128)[:, 64:96]
    gp = (dot(mid, w4[...]) * slope).astype(BF)
    k = lax.rem(me, 27)
    kz, kx, ky = k // 9, lax.rem(k // 3, 3), lax.rem(k, 3)
    rows = jnp.concatenate(
        [
            near_y[ky, pl.ds((z + kz) * (nx + 2) + kx, nx)].reshape(nx * 16, 128)
            for z in range(nz)
        ],
        axis=0,
    )
    tap_sum[...] = dot(rows, gp, TN)[:64].reshape(8, 8, 256)
    across.start(lambda index: tap_sum.at[index], tap_line.at[iy])
    tap_line[iy] = tap_sum[iy]
    hh.arrive()
    fill_half(hh, uh)
    across.arrive(tap_line)
    s = jnp.sum(tap_line[...], axis=0) * scales[2]
    tap_all[iy, me] = jnp.concatenate([s[:, :128], s[:, 128:]], axis=0).astype(BF)
    own = tap_all.at[iy, me]
    plane.start(lambda index: own, own)
    sum2.cross()
    gpool = dot(tt2[...], uh[...].reshape(3456, 256))
    r, c = rows_cols((256, 256))
    parts = split(gpool)
    for h in range(2):
        pick = hot(((r >> 6) == 2 * (c >> 7) + h) & ((r & 63) == ((c & 127) >> 1)))
        up = sum(dot(part, pick) for part in parts) * INV8
        up = jnp.concatenate(
            [up[32 * (x // 2) : 32 * (x // 2) + 32] for x in range(8)], axis=0
        )
        for zz in (2 * h, 2 * h + 1):
            gp1 = ((cot1[zz].astype(F32) + up) * sl1[zz]).astype(BF)
            hg.put(zz, gp1[:, :128])
            hg.put(zz + 4, gp1[:, 128:])
            g1[:, 256 * zz : 256 * zz + 256] = gp1
    hg.start()
    for kz in range(3):
        uc = jnp.concatenate([u1[kz + zz] for zz in range(4)], axis=1)
        g = dot(g1[...], uc, NT)
        for ky in range(3):
            band = sum(
                g[32 * x : 32 * x + 32, ky * 320 + 32 * x : ky * 320 + 32 * x + 96]
                for x in range(8)
            )
            for kx in range(3):
                m1[kz * 9 + kx * 3 + ky] = jnp.concatenate(
                    [band[8 * i : 8 * i + 8, 32 * kx : 32 * kx + 32] for i in range(4)],
                    axis=1,
                )
    sum1.scatter()
    sum2.gather()
    plane.arrive(tap_all.at[iy])
    own = tap_all.at[iy]
    chips.start(lambda index: own, own)
    hg.arrive()
    fill_fine(hg, ug)
    sum1.cross()

    def fine_back(zz):
        rows = dot(tt1[...], ug[zz : zz + 3].reshape(2880, 256)).astype(BF)
        rows = dot(back, rows).astype(BF)
        gvol[:, zz] = rows[:, :128].reshape(32, 8, 128)
        gvol[:, zz + 4] = rows[:, 128:].reshape(32, 8, 128)

    fine_back(0)
    fine_back(1)
    chips.arrive(tap_all)
    core = lax.rem(iy, 2)

    def to_core(c, carry):
        device, index = cores.member(1)
        own = tap_all.at[2 * c + core]
        pltpu.make_async_remote_copy(
            src_ref=own,
            dst_ref=own,
            send_sem=cores.send,
            recv_sem=cores.recv,
            device_id=device,
            device_id_type=MESH,
        ).start()
        return carry

    lax.fori_loop(0, chips.count, to_core, 0)
    sum1.gather()
    fine_back(2)
    fine_back(3)
    sum2.arrive()
    for k in range(27):
        wide = f2[k] * scales[1]
        d2[k] = jnp.concatenate([wide[:, :64], wide[:, 64:]], axis=0)
    for i in range(4):
        half, col = i % 2, 128 * (i // 2)
        d4[16 * half : 16 * half + 16, col : col + 128] = f2[27 + i] * scales[2]
    sum1.arrive()
    for k in range(27):
        wide = f1[k] * scales[0]
        d1[k] = jnp.concatenate([wide[:, 32 * i : 32 * i + 32] for i in range(4)], axis=0)
    rest = tap_all.at[pl.ds(0, chips.count)]
    rest = pltpu.make_async_remote_copy(
        src_ref=rest,
        dst_ref=rest,
        send_sem=cores.send,
        recv_sem=cores.recv,
        device_id=cores.member(1)[0],
        device_id_type=MESH,
    )
    rest.wait_recv()
    for j in range(place.size["y"]):
        for k in range(27):
            block = tap_all[j, k].astype(F32)
            d3[k, 8 * j : 8 * j + 8, :] = jnp.concatenate([block[:8], block[8:]], axis=1)
    rest.wait_send()
    for halo in (hv, hq, hh, hg):
        halo.finish()
    for copy in first + second:
        copy.wait_send()
    gather.finish(seen)
    across.finish(tap_line)
    plane.finish(tap_all.at[iy])
    chips.finish(tap_all)
    sum1.finish()
    sum2.finish()


def halo_scratch(nz, nx, ch):
    return [
        pltpu.VMEM((nz + 2, (nx + 2) * ch, 128), BF),
        pltpu.VMEM((2, 16, nx * ch), BF),
        pltpu.VMEM((3, 2, 3, 16, nx * ch), BF),
    ]


def body(sizes, cells, vol, cot, w1, w2, w3, w4):
    shape = jax.ShapeDtypeStruct
    field = shape((32, 8, 8, 128), BF)
    vmem = pl.BlockSpec(memory_space=pltpu.VMEM)
    nx, ny, nz = sizes
    coarse = 1.0 / math.sqrt(cells / 512.0)
    scales = (1.0 / math.sqrt(cells * 1.0), 1.0 / math.sqrt(cells / 8.0), coarse)
    total = lambda r: [
        pltpu.VMEM((32, r, 128), F32),
        pltpu.VMEM((32, r, 128), F32),
        pltpu.VMEM((ny, r, 128), F32),
        pltpu.VMEM((32, r, 128), F32),
    ]
    out, gvol, d1, d2, d3, d4 = pl.pallas_call(
        functools.partial(kernel, sizes, scales),
        out_shape=[
            field,
            field,
            shape((27, 32, 32), F32),
            shape((27, 32, 64), F32),
            shape((27, 64, 256), F32),
            shape((32, 256), F32),
        ],
        in_specs=[vmem] * 6,
        out_specs=[vmem] * 6,
        scratch_shapes=[
            *halo_scratch(8, 8, 32),
            *halo_scratch(4, 4, 32),
            *halo_scratch(4, 4, 64),
            *halo_scratch(8, 8, 32),
            pltpu.VMEM((6, 960, 256), BF),
            pltpu.VMEM((6, 960, 256), BF),
            pltpu.VMEM((9, 192, 256), BF),
            pltpu.VMEM((9, 384, 256), BF),
            pltpu.VMEM((256, 2880), BF),
            pltpu.VMEM((256, 2880), BF),
            pltpu.VMEM((256, 1728), BF),
            pltpu.VMEM((128, 3456), BF),
            pltpu.VMEM((4, 256, 256), F32),
            pltpu.VMEM((4, 256, 256), BF),
            pltpu.VMEM((4, 256, 256), BF),
            pltpu.VMEM((256, 1024), BF),
            pltpu.VMEM((3, 3, 3, 16, 128), BF),
            pltpu.VMEM((3, 3, 3, 16, 256), BF),
            pltpu.SemaphoreType.DMA((6, 26)),
            pltpu.SemaphoreType.DMA((6, 26)),
            pltpu.VMEM((32, 128), BF),
            pltpu.VMEM(((nz + 2) * (nx + 2), 32, 128), BF),
            pltpu.VMEM((3, (nz + 2) * (nx + 2), 16, 128), BF),
            pltpu.VMEM((8, 8, 256), F32),
            pltpu.VMEM((ny, 8, 256), F32),
            pltpu.VMEM((ny, 32, 16, 128), BF),
            *total(8),
            *total(16),
            pltpu.SemaphoreType.DMA((11,)),
            pltpu.SemaphoreType.DMA((11,)),
        ],
        compiler_params=pltpu.CompilerParams(
            collective_id=0, has_side_effects=True, vmem_limit_bytes=60 * 1024 * 1024
        ),
        name="unet",
    )(vol, cot, w1, jnp.swapaxes(w2, 1, 2), jnp.swapaxes(w3, 1, 2), w4)
    return out, gvol, d1, jnp.swapaxes(d2, 1, 2), jnp.swapaxes(d3, 1, 2), d4


def solution(mesh):
    sizes = (mesh.shape["gx"], mesh.shape["gy"], mesh.shape["gz"])
    cells = 8 * 8 * 128 * sizes[0] * sizes[1] * sizes[2]
    field = P(None, "gz", "gx", "gy")
    return jax.shard_map(
        functools.partial(body, sizes, cells),
        mesh=mesh,
        in_specs=(field, field, P(), P(), P(), P()),
        out_specs=(field, field, P(), P(), P(), P()),
        check_vma=False,
    )
```

```python
import functools
import itertools
import math

import jax
import jax.numpy as jnp
from jax import lax
from jax.experimental import pallas as pl
from jax.experimental.pallas import tpu as pltpu
from jax.sharding import PartitionSpec as P

MESH = pl.DeviceIdType.MESH
BF = jnp.bfloat16
F32 = jnp.float32
INV8 = 1.0 / math.sqrt(8.0)
STEPS = sorted(
    (d for d in itertools.product((-1, 0, 1), repeat=3) if d != (0, 0, 0)),
    key=lambda d: -sum(map(abs, d)),
)

NN = ((1,), (0,))
NT = ((1,), (1,))
TN = ((0,), (0,))


def dot(a, b, dims=NN):
    return lax.dot_general(a, b, (dims, ((), ())), preferred_element_type=F32)


def rows_cols(shape):
    return (
        lax.broadcasted_iota(jnp.int32, shape, 0),
        lax.broadcasted_iota(jnp.int32, shape, 1),
    )


def hot(cond):
    return jnp.where(cond, 1.0, 0.0).astype(BF)


def roll(a, shift):
    return pltpu.roll(a, shift % a.shape[1], 1)


def silu_slope(pre):
    sig = 0.5 * (1.0 + jnp.tanh(0.5 * pre))
    act = pre * sig
    return act, sig + act * (1.0 - sig)


def split(a):
    high = a.astype(BF)
    return high, (a - high.astype(F32)).astype(BF)


class Place:
    def __init__(self, sizes):
        self.size = dict(zip(("x", "y", "z"), sizes))
        self.at = {
            "x": lax.axis_index("gx"),
            "y": lax.axis_index("gy"),
            "z": lax.axis_index("gz"),
        }

    def near(self, axis, step):
        size = self.size[axis]
        return lax.rem(self.at[axis] + (step + size), size)

    def device(self, dz, dx, dy):
        return (self.near("x", dx), self.near("y", dy), self.near("z", dz))

    def inside(self, axis, step):
        if step == 0:
            return None
        if step < 0:
            return self.at[axis] > 0
        return self.at[axis] < self.size[axis] - 1


class Halo:
    def __init__(self, place, pad, face, got, send, recv, nz, nx, ch, ylen):
        self.place, self.pad, self.face, self.got = place, pad, face, got
        self.send, self.recv = send, recv
        self.nz, self.nx, self.ch, self.ylen = nz, nx, ch, ylen

    def put(self, z, value):
        self.pad[z + 1, self.ch : self.ch * (self.nx + 1), :] = value

    def start(self):
        nz, nx, ch = self.nz, self.nx, self.ch
        r, c = rows_cols((32, nz * 128))
        edge = jnp.where(r >= 16, self.ylen - 1, 0)
        pick = hot(((r & 15) == (c >> 7)) & ((c & 127) == edge))
        own = jnp.concatenate(
            [self.pad[z + 1, ch : ch * (nx + 1), :] for z in range(nz)], axis=1
        )
        both = dot(pick, own, NT).astype(BF)
        self.face[0] = both[:16]
        self.face[1] = both[16:]
        self.copies = []
        for i, (dz, dx, dy) in enumerate(STEPS):
            if dy == 0:
                zs = {-1: (1, 1), 0: (1, nz), 1: (nz, 1)}[dz]
                xs = {-1: (ch, ch), 0: (ch, nx * ch), 1: (nx * ch, ch)}[dx]
                zd = {-1: nz + 1, 0: 1, 1: 0}[dz]
                xd = {-1: (nx + 1) * ch, 0: ch, 1: 0}[dx]
                src = self.pad.at[pl.ds(zs[0], zs[1]), pl.ds(xs[0], xs[1])]
                dst = self.pad.at[pl.ds(zd, zs[1]), pl.ds(xd, xs[1])]
            else:
                side = 0 if dy == 1 else 1
                src = self.face.at[1 - side]
                dst = self.got.at[1 - dx, side, 1 - dz]
            copy = pltpu.make_async_remote_copy(
                src_ref=src,
                dst_ref=dst,
                send_sem=self.send.at[i],
                recv_sem=self.recv.at[i],
                device_id=self.place.device(dz, dx, dy),
                device_id_type=MESH,
            )
            copy.start()
            self.copies.append(copy)

    def arrive(self):
        for copy in self.copies:
            copy.wait_recv()
        nz, nx, ch = self.nz, self.nx, self.ch
        at, size = self.place.at, self.place.size
        plane = jnp.zeros(self.pad.shape[1:], BF)
        column = jnp.zeros((nz + 2, ch, 128), BF)

        @pl.when(at["z"] == 0)
        def _():
            self.pad[0] = plane

        @pl.when(at["z"] == size["z"] - 1)
        def _():
            self.pad[nz + 1] = plane

        @pl.when(at["x"] == 0)
        def _():
            self.pad[:, 0:ch, :] = column

        @pl.when(at["x"] == size["x"] - 1)
        def _():
            self.pad[:, (nx + 1) * ch :, :] = column

    def columns(self):
        nz, nx, ch = self.nz, self.nx, self.ch
        at, size = self.place.at, self.place.size
        r, c = rows_cols((96, 128))
        group, z = r >> 4, r & 15
        side = jnp.where(group >= 3, 1, 0)
        dz = group - 3 * side
        zp = c & 15
        first, last = (
            jnp.where(at["z"] > 0, 0, -1),
            jnp.where(at["z"] < size["z"] - 1, nz + 1, -1),
        )
        low, high = (
            jnp.where(at["y"] > 0, 0, -1),
            jnp.where(at["y"] < size["y"] - 1, 1, -1),
        )
        mid = (dz == 1) & (z < nz) & (zp == z + 1)
        below = (dz == 0) & (z == nz - 1) & (zp == first)
        above = (dz == 2) & (z == 0) & (zp == last)
        lane = (side == (c >> 4)) & ((side == low) | (side == high))
        pick = hot((mid | below | above) & lane)
        parts = []
        for dx in range(3):
            wide = slice(0, nx * ch)
            if dx == 0:
                wide = slice((nx - 1) * ch, nx * ch)
            if dx == 2:
                wide = slice(0, ch)
            src = self.got[dx].reshape(96, nx * ch)[:, wide]
            part = dot(src, pick, TN)
            if dx != 1:
                part = jnp.where(self.place.inside("x", dx - 1), part, 0.0)
            parts.append(part.astype(BF))
        return jnp.concatenate(parts, axis=0)

    def shifted(self):
        cols = self.columns()
        lane = rows_cols(cols.shape)[1]
        for zp in range(self.nz + 2):
            base = self.pad[zp]
            low = jnp.where(lane == 0, roll(cols, -zp), roll(base, 1))
            end = self.ylen - 1
            high = jnp.where(lane == end, roll(cols, end - 16 - zp), roll(base, -1))
            yield zp, (low, base, high)

    def finish(self):
        for copy in self.copies:
            copy.wait_send()


def fill_fine(halo, u):
    rows = (halo.nx + 2) * halo.ch
    for zp, parts in halo.shifted():
        for ky, part in enumerate(parts):
            if zp <= 5:
                u[zp, ky * rows : (ky + 1) * rows, 0:128] = part
            if zp >= 4:
                u[zp - 4, ky * rows : (ky + 1) * rows, 128:256] = part


def fill_half(halo, u):
    before = None
    for zp, parts in halo.shifted():
        if before is not None:
            j = zp - 1
            for ky in range(3):
                lane = rows_cols(parts[ky].shape)[1]
                both = jnp.where(lane < 64, before[ky], roll(parts[ky], 64))
                if j <= 2:
                    u[j * 3 + ky, :, 0:128] = both
                if j >= 2:
                    u[(j - 2) * 3 + ky, :, 128:256] = both
        before = parts


def put_half(halo, value):
    lane = rows_cols((value.shape[0], 128))[1]
    for z in range(4):
        half = value[:, 128 * (z // 2) : 128 * (z // 2) + 128]
        if z % 2:
            half = roll(half, 64)
        halo.put(z, jnp.where(lane < 64, half, jnp.zeros_like(half)))


def toeplitz(dst, blocks, nx, rows, width):
    dst[...] = jnp.zeros(dst.shape, BF)
    for kz, ky in itertools.product(range(3), range(3)):
        band = jnp.concatenate([blocks(kz, kx, ky) for kx in range(3)], axis=1)
        base = (kz * 3 + ky) * (nx + 2) * width
        for x in range(nx):
            dst[rows * x : rows * (x + 1), base + width * x : base + width * (x + 3)] = band


def coarse_start(place, box, send, recv):
    copies = []
    for i, (dz, dx, dy) in enumerate(STEPS):
        copy = pltpu.make_async_remote_copy(
            src_ref=box.at[1, 1, 1],
            dst_ref=box.at[1 - dz, 1 - dx, 1 - dy],
            send_sem=send.at[i],
            recv_sem=recv.at[i],
            device_id=place.device(dz, dx, dy),
            device_id_type=MESH,
        )
        copy.start()
        copies.append(copy)
    return copies


def coarse_shifts(place, box):
    wide = []
    for dz, dx in itertools.product((-1, 0, 1), (-1, 0, 1)):
        rows = []
        for dy in (-1, 0, 1):
            block = box[dz + 1, dx + 1, dy + 1]
            for axis, step in (("z", dz), ("x", dx), ("y", dy)):
                if step:
                    block = jnp.where(place.inside(axis, step), block, jnp.zeros_like(block))
            rows.append(block)
        wide.append(jnp.concatenate(rows, axis=0))
    wide = jnp.concatenate(wide, axis=1)
    r, c = rows_cols((48, 48))
    pick = hot(c == (r & 15) + (r >> 4) + 15)
    width = box.shape[-1]
    return dot(pick, wide).astype(BF), wide[8:40, 4 * width : 5 * width]


class Group:
    def __init__(self, place, kind, send, recv):
        self.place, self.kind, self.send, self.recv = place, kind, send, recv
        size = place.size
        self.count = {
            "plane": size["x"] * size["z"],
            "sheet": size["x"] * size["y"],
            "line": size["y"],
            "depth": size["z"],
            "chips": size["y"] // 2,
            "cores": 2,
        }[kind]

    def member(self, q):
        at, size = self.place.at, self.place.size
        if self.kind == "plane":
            x = lax.rem(at["x"] + q // size["z"], size["x"])
            z = lax.rem(at["z"] + lax.rem(q, size["z"]), size["z"])
            return (x, at["y"], z), x * size["z"] + z
        if self.kind == "sheet":
            x = lax.rem(at["x"] + q // size["y"], size["x"])
            y = lax.rem(at["y"] + lax.rem(q, size["y"]), size["y"])
            return (x, y, at["z"]), x * size["y"] + y
        if self.kind == "depth":
            z = lax.rem(at["z"] + q, size["z"])
            return (at["x"], at["y"], z), z
        if self.kind == "line":
            y = lax.rem(at["y"] + q, size["y"])
            return (at["x"], y, at["z"]), y
        if self.kind == "chips":
            y = lax.rem(at["y"] + 2 * q, size["y"])
            return (at["x"], y, at["z"]), y // 2
        y = at["y"] + 1 - 2 * lax.rem(at["y"], 2)
        return (at["x"], y, at["z"]), lax.rem(y, 2)

    def start(self, src, dst):
        def one(q, carry):
            device, index = self.member(q)
            pltpu.make_async_remote_copy(
                src_ref=src(index),
                dst_ref=dst,
                send_sem=self.send,
                recv_sem=self.recv,
                device_id=device,
                device_id_type=MESH,
            ).start()
            return carry

        lax.fori_loop(1, self.count, one, 0)

    def _all(self, slots):
        ref = slots.at[pl.ds(0, self.count - 1)]
        return pltpu.make_async_remote_copy(
            src_ref=ref,
            dst_ref=ref,
            send_sem=self.send,
            recv_sem=self.recv,
            device_id=self.member(1)[0],
            device_id_type=MESH,
        )

    def arrive(self, slots):
        if self.count > 1:
            self._all(slots).wait_recv()

    def finish(self, slots):
        if self.count > 1:
            self._all(slots).wait_send()


class Total:
    def __init__(self, place, mine, landed, line, done, send, recv):
        self.mine, self.landed, self.line, self.done = mine, landed, line, done
        self.at = place.at
        self.me = place.at["x"] * place.size["y"] + place.at["y"]
        self.one = Group(place, "sheet", send.at[0], recv.at[0])
        self.two = Group(place, "depth", send.at[1], recv.at[1])
        self.three = Group(place, "sheet", send.at[2], recv.at[2])

    def scatter(self):
        self.one.start(lambda index: self.mine.at[index], self.landed.at[self.me])
        self.landed[self.me] = self.mine[self.me]

    def cross(self):
        self.one.arrive(self.landed)
        self.line[self.at["z"]] = jnp.sum(self.landed[...], axis=0)
        own = self.line.at[self.at["z"]]
        self.two.start(lambda index: own, own)

    def gather(self, scale):
        self.two.arrive(self.line)
        total = jnp.sum(self.line[...], axis=0) * scale
        self.done[self.me] = total.astype(self.done.dtype)
        own = self.done.at[self.me]
        self.three.start(lambda index: own, own)

    def arrive(self):
        self.three.arrive(self.done)

    def finish(self):
        self.one.finish(self.landed)
        self.two.finish(self.line)
        self.three.finish(self.done)


def kernel(
    sizes, scales, vol_in, cot_in, w1_in, w2_in, w3_in, w4_in,
    out, gvol, d1, d2, d3,
    v_pad, v_face, v_got, q_pad, q_face, q_got,
    h_pad, h_face, h_got, g_pad, g_face, g_got,
    u1, ug, u2, uh, t1, tt1, t2, tt2,
    sl1, act1, cot1, g1, box_in, box_gp, send, recv,
    note, seen, near_y, tap_sum, tap_line, tap_all,
    m1, l1, y1, f1, m2, l2, y2, f2, gsend, grecv,
    vol, cot, w1, w2, w3, w4, out_rows, gvol_rows, local,
):
    place = Place(sizes)
    seen[...] = jnp.zeros(seen.shape, BF)
    barrier = pltpu.get_barrier_semaphore()
    partners = [place.device(*s) for s in STEPS if s[0] != 0 and s[2] != 0]
    for device in partners:
        pl.semaphore_signal(barrier, inc=1, device_id=device, device_id_type=MESH)
    sums = [
        Group(place, kind, gsend.at[i], grecv.at[i])
        for i, kind in enumerate(("plane", "line", "plane", "chips", "cores"))
    ]
    gather, across, plane, chips, cores = sums
    total = len(partners)
    for kind in ("plane", "sheet"):
        group = Group(place, kind, None, None)

        def greet(q, carry, group=group):
            device = group.member(q)[0]
            pl.semaphore_signal(barrier, inc=1, device_id=device, device_id_type=MESH)
            return carry

        lax.fori_loop(1, group.count, greet, 0)
        total += group.count - 1
    loads = [
        pltpu.make_async_copy(src, dst, local.at[i])
        for i, (src, dst) in enumerate(
            (
                (vol_in, vol), (cot_in, cot), (w1_in, w1),
                (w2_in, w2), (w3_in, w3), (w4_in, w4),
            )
        )
    ]
    for load in loads:
        load.start()
    stores = []

    def store(src, dst):
        copy = pltpu.make_async_copy(src, dst, local.at[len(loads) + len(stores)])
        copy.start()
        stores.append(copy)

    ix, iy, iz = place.at["x"], place.at["y"], place.at["z"]
    nx, nz = place.size["x"], place.size["z"]
    me = ix * nz + iz
    m1[27:32] = jnp.zeros((5, 8, 128), F32)
    m2[27:32] = jnp.zeros((5, 16, 128), F32)
    r, c = rows_cols((256, 256))
    perm = hot(((r & 31) == (c >> 3)) & ((r >> 5) == (c & 7)))

    def two(ref, zz):
        return jnp.concatenate(
            [ref[:, zz].reshape(256, 128), ref[:, zz + 4].reshape(256, 128)], axis=1
        )

    hv = Halo(place, v_pad, v_face, v_got, send.at[0], recv.at[0], 8, 8, 32, 128)
    hq = Halo(place, q_pad, q_face, q_got, send.at[1], recv.at[1], 4, 4, 32, 64)
    hh = Halo(place, h_pad, h_face, h_got, send.at[2], recv.at[2], 4, 4, 64, 64)
    hg = Halo(place, g_pad, g_face, g_got, send.at[3], recv.at[3], 8, 8, 32, 128)
    sum1 = Total(place, m1, l1, y1, f1, gsend.at[pl.ds(5, 3)], grecv.at[pl.ds(5, 3)])
    sum2 = Total(place, m2, l2, y2, f2, gsend.at[pl.ds(8, 3)], grecv.at[pl.ds(8, 3)])
    loads[0].wait()
    for zz in range(4):
        rows = dot(perm, two(vol, zz)).astype(BF)
        hv.put(zz, rows[:, :128])
        hv.put(zz + 4, rows[:, 128:])
    pl.semaphore_wait(barrier, total)
    hv.start()
    for load in loads[1:]:
        load.wait()

    for zz in range(4):
        cot1[zz] = dot(perm, two(cot, zz)).astype(BF)
    r, c = rows_cols((32, 32))
    eye = hot(r == c)
    toeplitz(t1, lambda kz, kx, ky: w1[kz * 9 + kx * 3 + ky], 8, 32, 32)
    flat1 = dot(eye, w1[...].reshape(864, 32), NT).astype(BF)
    r, c = rows_cols((64, 64))
    flat2 = dot(hot(r == c), w2[...].reshape(864, 64), NT).astype(BF)

    def back_tap(kz, kx, ky):
        return (2 - kz) * 9 + (2 - kx) * 3 + (2 - ky)

    def turned(kz, kx, ky):
        k = back_tap(kz, kx, ky)
        return flat1[:, k * 32 : (k + 1) * 32]

    def straight(kz, kx, ky):
        k = kz * 9 + kx * 3 + ky
        return flat2[:, k * 32 : (k + 1) * 32]

    toeplitz(t2, straight, 4, 64, 32)
    toeplitz(tt1, turned, 8, 32, 32)
    toeplitz(tt2, lambda *k: w2[back_tap(*k)], 4, 32, 64)
    cg = jnp.sum(cot[...].astype(F32), axis=(1, 2))
    cg = cg + roll(cg, -1)
    cg = cg + roll(cg, -2)
    cg = (cg + roll(cg, -4)).astype(BF)

    hv.arrive()
    fill_fine(hv, u1)
    for zz in range(4):
        pre = dot(t1[...], u1[zz : zz + 3].reshape(2880, 256))
        act, slope = silu_slope(pre)
        act1[zz] = act.astype(BF)
        sl1[zz] = slope
    r, c = rows_cols((512, 256))
    z2 = 2 * ((r >> 7) & 1) + (r >> 8)
    pick = hot(((c >> 6) == z2) & ((r & 127) == 2 * (c & 63)))
    pooled = []
    for a, b in ((0, 1), (2, 3)):
        s = act1[a].astype(F32) + act1[b].astype(F32)
        s = jnp.sum(s.reshape(4, 2, 32, 256), axis=1).reshape(128, 256)
        s = s + roll(s, -1)
        pooled.append((s * INV8).astype(BF))
    q1 = dot(jnp.concatenate(pooled, axis=1), pick).astype(BF)
    put_half(hq, q1)
    hq.start()

    hq.arrive()
    fill_half(hq, u2)
    pre2 = dot(t2[...], u2[...].reshape(1728, 256))
    act2, slope2 = silu_slope(pre2)
    s = jnp.sum(act2.astype(BF).astype(F32).reshape(4, 64, 256), axis=0)
    s = s[:, :128] + s[:, 128:]
    s = s + roll(s, 64)
    s = s + roll(s, -1)
    s = s + roll(s, -2)
    cin = (s * 0.125).astype(BF)
    zero = jnp.zeros((64, 128), BF)
    r, c = rows_cols((16, 128))
    own = dot(hot(c == 4 * r), jnp.concatenate([cin, zero], axis=0), NT)
    own += dot(hot(c == 8 * r), jnp.concatenate([zero, cg, zero[:32]], axis=0), NT)
    own = own.astype(BF)
    box_in[1, 1, 1] = own
    first = coarse_start(place, box_in, send.at[4], recv.at[4])
    for copy in first:
        copy.wait_recv()
    near, own = coarse_shifts(place, box_in)
    note[...] = own

    def tap(kz, kx, ky, width, valid):
        base = (kz * 3 + kx) * width
        return near[16 * ky : 16 * (ky + 1), base : base + valid]

    taps = list(itertools.product(range(3), range(3), range(3)))
    x3 = jnp.concatenate([tap(*k, 128, 64) for k in taps], axis=1)
    pre3 = dot(x3, w3[...].reshape(1728, 256))
    act3, slope3 = silu_slope(pre3)
    act3 = act3.astype(BF)
    cgt = own[8:24, 64:96]
    gp3 = (dot(cgt, w4[...]) * slope3).astype(BF)
    box_gp[1, 1, 1] = gp3
    second = coarse_start(place, box_gp, send.at[5], recv.at[5])
    gather.start(lambda index: note, seen.at[(iz + 1) * (nx + 2) + ix + 1])
    seen[(iz + 1) * (nx + 2) + ix + 1] = own
    co = dot(w4[...], act3, NT).astype(BF)
    part4 = dot(cgt, act3, TN)
    for i in range(4):
        half, col = i % 2, 128 * (i // 2)
        m2[27 + i] = part4[16 * half : 16 * half + 16, col : col + 128]
    r, c = rows_cols((16, 128))
    co = dot(co, hot(r == (c >> 3)))
    co = jnp.concatenate([jnp.concatenate([co] * 8, axis=0)] * 2, axis=1)
    for zz in range(4):
        out_rows[zz] = (act1[zz].astype(F32) + co).astype(BF)
    store(out_rows, out)
    for copy in second:
        copy.wait_recv()
    near = coarse_shifts(place, box_gp)[0]
    gc = sum(
        dot(w3[kz * 9 + kx * 3 + ky], tap(2 - kz, 2 - kx, 2 - ky, 256, 256), NT)
        for kz, kx, ky in taps
    )
    r, c = rows_cols((16, 256))
    pick = hot(r == ((c & 63) >> 2))
    up = sum(dot(part, pick) for part in split(gc)) * 0.125
    gp2 = (jnp.concatenate([up] * 4, axis=0) * slope2).astype(BF)
    put_half(hh, gp2)
    hh.start()
    lane = rows_cols((16, 128))[1]
    for kz in range(3):
        g = dot(u2[3 * kz : 3 * kz + 3].reshape(576, 256), gp2, NT)
        for ky, kx in itertools.product(range(3), range(3)):
            cut = [
                g[ky * 192 + 32 * (x + kx) :][:32, 128 * (x // 2) : 128 * (x // 2) + 128]
                for x in range(4)
            ]
            even, odd = cut[0] + cut[2], cut[1] + cut[3]
            low = (even + roll(odd, 64))[:16]
            high = (roll(even, 64) + odd)[16:]
            m2[kz * 9 + kx * 3 + ky] = jnp.where(lane < 64, low, high)
    sum2.scatter()
    gather.arrive(seen)
    for ky in range(3):
        near_y[ky] = seen[:, 7 + ky : 23 + ky, :]
    lane = rows_cols((16, 128))[1]
    pair = jnp.where(lane < 64, near_y[0], pltpu.roll(near_y[1], 64, 2))
    both = jnp.concatenate([pair, near_y[2]], axis=2)
    both = both.reshape(nz + 2, nx + 2, 16, 256)
    pre = sum(
        dot(
            both[kz : kz + nz, kx : kx + nx].reshape(nz * nx * 16, 256)[:, :192],
            w3[kz * 9 + kx * 3 : kz * 9 + kx * 3 + 3].reshape(192, 256),
        )
        for kz, kx in itertools.product(range(3), range(3))
    )
    slope = silu_slope(pre)[1]
    mid = near_y[1].reshape(nz + 2, nx + 2, 16, 128)[1 : nz + 1, 1 : nx + 1]
    mid = mid.reshape(nz * nx * 16, 128)[:, 64:96]
    gp = (dot(mid, w4[...]) * slope).astype(BF)
    k = lax.rem(me, 27)
    kz, kx, ky = k // 9, lax.rem(k // 3, 3), lax.rem(k, 3)
    rows = jnp.concatenate(
        [
            near_y[ky, pl.ds((z + kz) * (nx + 2) + kx, nx)].reshape(nx * 16, 128)
            for z in range(nz)
        ],
        axis=0,
    )
    tap_sum[...] = dot(rows, gp, TN)[:64].reshape(8, 8, 256)
    across.start(lambda index: tap_sum.at[index], tap_line.at[iy])
    tap_line[iy] = tap_sum[iy]
    hh.arrive()
    across.arrive(tap_line)
    s = jnp.sum(tap_line[...], axis=0) * scales[2]
    tap_all[iy, me] = jnp.concatenate([s[:, :128], s[:, 128:]], axis=0).astype(BF)
    own_tap = tap_all.at[iy, me]
    plane.start(lambda index: own_tap, own_tap)
    sum2.cross()
    fill_half(hh, uh)
    gpool = dot(tt2[...], uh[...].reshape(3456, 256))
    r, c = rows_cols((256, 256))
    parts = split(gpool)
    for h in range(2):
        pick = hot(((r >> 6) == 2 * (c >> 7) + h) & ((r & 63) == ((c & 127) >> 1)))
        up = sum(dot(part, pick) for part in parts) * INV8
        up = jnp.concatenate(
            [up[32 * (x // 2) : 32 * (x // 2) + 32] for x in range(8)], axis=0
        )
        for zz in (2 * h, 2 * h + 1):
            gp1 = ((cot1[zz].astype(F32) + up) * sl1[zz]).astype(BF)
            hg.put(zz, gp1[:, :128])
            hg.put(zz + 4, gp1[:, 128:])
            g1[:, 256 * zz : 256 * zz + 256] = gp1
    for kz in range(3):
        uc = jnp.concatenate([u1[kz + zz] for zz in range(4)], axis=1)
        g = dot(g1[...], uc, NT)
        for ky in range(3):
            band = sum(
                g[32 * x : 32 * x + 32, ky * 320 + 32 * x : ky * 320 + 32 * x + 96]
                for x in range(8)
            )
            for kx in range(3):
                m1[kz * 9 + kx * 3 + ky] = jnp.concatenate(
                    [band[8 * i : 8 * i + 8, 32 * kx : 32 * kx + 32] for i in range(4)],
                    axis=1,
                )
    sum1.scatter()
    hg.start()
    plane.arrive(tap_all.at[iy])
    own_range = tap_all.at[iy]
    chips.start(lambda index: own_range, own_range)
    sum1.cross()
    sum2.gather(scales[1])
    hg.arrive()
    fill_fine(hg, ug)
    sum1.gather(scales[0])
    for zz in range(4):
        rows = dot(tt1[...], ug[zz : zz + 3].reshape(2880, 256))
        gvol_rows[zz] = rows.astype(BF)
    store(gvol_rows, gvol)
    chips.arrive(tap_all)
    core = lax.rem(iy, 2)

    def to_core(c, carry):
        own = tap_all.at[2 * c + core]
        pltpu.make_async_remote_copy(
            src_ref=own,
            dst_ref=own,
            send_sem=cores.send,
            recv_sem=cores.recv,
            device_id=cores.member(1)[0],
            device_id_type=MESH,
        ).start()
        return carry

    lax.fori_loop(0, chips.count, to_core, 0)
    sum2.arrive()
    store(f2, d2)
    sum1.arrive()
    store(f1, d1)
    rest = tap_all.at[pl.ds(0, chips.count)]
    rest = pltpu.make_async_remote_copy(
        src_ref=rest,
        dst_ref=rest,
        send_sem=cores.send,
        recv_sem=cores.recv,
        device_id=cores.member(1)[0],
        device_id_type=MESH,
    )
    rest.wait_recv()
    store(tap_all, d3)
    rest.wait_send()
    for halo in (hv, hq, hh, hg):
        halo.finish()
    for copy in first + second:
        copy.wait_send()
    gather.finish(seen)
    across.finish(tap_line)
    plane.finish(tap_all.at[iy])
    chips.finish(tap_all)
    sum1.finish()
    sum2.finish()
    for copy in stores:
        copy.wait()


def last_kernel(
    scale, out_rows, gvol_rows, f1, f2, tap_all,
    out, gvol, d1, d2, d3, d4,
    out_v, gvol_v, v1, v2, v3, sems,
):
    r, c = rows_cols((256, 256))
    back = hot(((c & 31) == (r >> 3)) & ((c >> 5) == (r & 7)))
    copies = []

    def store(src, dst):
        copy = pltpu.make_async_copy(src, dst, sems.at[len(copies)])
        copy.start()
        copies.append(copy)

    for j in range(tap_all.shape[0]):
        for k in range(27):
            block = tap_all[j, k].astype(F32)
            v3[k, 8 * j : 8 * j + 8, :] = jnp.concatenate([block[:8], block[8:]], axis=1)
    store(v3, d3)
    for src, mid, dst in ((out_rows, out_v, out), (gvol_rows, gvol_v, gvol)):
        for zz in range(4):
            rows = dot(back, src[zz]).astype(BF)
            mid[:, zz] = rows[:, :128].reshape(32, 8, 128)
            mid[:, zz + 4] = rows[:, 128:].reshape(32, 8, 128)
        store(mid, dst)
    for k in range(27):
        wide = f2[k].astype(F32)
        v2[k] = jnp.concatenate([wide[:, :64], wide[:, 64:]], axis=0)
    store(v2, d2)
    for k in range(27):
        wide = f1[k]
        v1[k] = jnp.concatenate([wide[:, 32 * i : 32 * i + 32] for i in range(4)], axis=0)
    store(v1, d1)
    for i in range(4):
        half, col = i % 2, 128 * (i // 2)
        d4[16 * half : 16 * half + 16, col : col + 128] = f2[27 + i].astype(F32) * scale
    for copy in copies:
        copy.wait()


def halo_scratch(nz, nx, ch):
    return [
        pltpu.VMEM((nz + 2, (nx + 2) * ch, 128), BF),
        pltpu.VMEM((2, 16, nx * ch), BF),
        pltpu.VMEM((3, 2, 3, 16, nx * ch), BF),
    ]


def body(sizes, cells, vol, cot, w1, w2, w3, w4):
    shape = jax.ShapeDtypeStruct
    field = shape((32, 8, 8, 128), BF)
    vmem = pl.BlockSpec(memory_space=pltpu.VMEM)
    nx, ny, nz = sizes
    coarse = 1.0 / math.sqrt(cells / 512.0)
    scales = (1.0 / math.sqrt(cells * 1.0), 1.0 / math.sqrt(cells / 8.0), coarse)
    total = lambda r: [
        pltpu.VMEM((32, r, 128), F32),
        pltpu.VMEM((32, r, 128), F32),
        pltpu.VMEM((nz, r, 128), F32),
        pltpu.VMEM((32, r, 128), F32 if r == 8 else BF),
    ]
    rows = shape((4, 256, 256), BF)
    anywhere = pl.BlockSpec(memory_space=pl.ANY)
    mid = pl.pallas_call(
        functools.partial(kernel, sizes, scales),
        out_shape=[
            rows,
            rows,
            shape((32, 8, 128), F32),
            shape((32, 16, 128), BF),
            shape((ny, 32, 16, 128), BF),
        ],
        in_specs=[pl.BlockSpec(memory_space=pltpu.HBM)] * 6,
        out_specs=[anywhere] * 5,
        scratch_shapes=[
            *halo_scratch(8, 8, 32),
            *halo_scratch(4, 4, 32),
            *halo_scratch(4, 4, 64),
            *halo_scratch(8, 8, 32),
            pltpu.VMEM((6, 960, 256), BF),
            pltpu.VMEM((6, 960, 256), BF),
            pltpu.VMEM((9, 192, 256), BF),
            pltpu.VMEM((9, 384, 256), BF),
            pltpu.VMEM((256, 2880), BF),
            pltpu.VMEM((256, 2880), BF),
            pltpu.VMEM((256, 1728), BF),
            pltpu.VMEM((128, 3456), BF),
            pltpu.VMEM((4, 256, 256), F32),
            pltpu.VMEM((4, 256, 256), BF),
            pltpu.VMEM((4, 256, 256), BF),
            pltpu.VMEM((256, 1024), BF),
            pltpu.VMEM((3, 3, 3, 16, 128), BF),
            pltpu.VMEM((3, 3, 3, 16, 256), BF),
            pltpu.SemaphoreType.DMA((6, 26)),
            pltpu.SemaphoreType.DMA((6, 26)),
            pltpu.VMEM((32, 128), BF),
            pltpu.VMEM(((nz + 2) * (nx + 2), 32, 128), BF),
            pltpu.VMEM((3, (nz + 2) * (nx + 2), 16, 128), BF),
            pltpu.VMEM((8, 8, 256), F32),
            pltpu.VMEM((ny, 8, 256), F32),
            pltpu.VMEM((ny, 32, 16, 128), BF),
            *total(8),
            *total(16),
            pltpu.SemaphoreType.DMA((11,)),
            pltpu.SemaphoreType.DMA((11,)),
            pltpu.VMEM((32, 8, 8, 128), BF),
            pltpu.VMEM((32, 8, 8, 128), BF),
            pltpu.VMEM((27, 32, 32), BF),
            pltpu.VMEM((27, 32, 64), BF),
            pltpu.VMEM((27, 64, 256), BF),
            pltpu.VMEM((32, 256), BF),
            pltpu.VMEM((4, 256, 256), BF),
            pltpu.VMEM((4, 256, 256), BF),
            pltpu.SemaphoreType.DMA((11,)),
        ],
        compiler_params=pltpu.CompilerParams(
            collective_id=0, has_side_effects=True, vmem_limit_bytes=48 * 1024 * 1024
        ),
        name="unet",
    )(vol, cot, w1, jnp.swapaxes(w2, 1, 2), jnp.swapaxes(w3, 1, 2), w4)
    finals = [
        field,
        field,
        shape((27, 32, 32), F32),
        shape((27, 32, 64), F32),
        shape((27, 64, 256), F32),
        shape((32, 256), F32),
    ]
    out, gvol, d1, d2, d3, d4 = pl.pallas_call(
        functools.partial(last_kernel, scales[2] / scales[1]),
        out_shape=finals,
        in_specs=[vmem] * 5,
        out_specs=[anywhere] * 5 + [vmem],
        scratch_shapes=[pltpu.VMEM(f.shape, f.dtype) for f in finals[:5]]
        + [pltpu.SemaphoreType.DMA((5,))],
        compiler_params=pltpu.CompilerParams(vmem_limit_bytes=32 * 1024 * 1024),
        name="finish",
    )(*mid)
    return out, gvol, d1, jnp.swapaxes(d2, 1, 2), jnp.swapaxes(d3, 1, 2), d4


def solution(mesh):
    sizes = (mesh.shape["gx"], mesh.shape["gy"], mesh.shape["gz"])
    cells = 8 * 8 * 128 * sizes[0] * sizes[1] * sizes[2]
    field = P(None, "gz", "gx", "gy")
    return jax.shard_map(
        functools.partial(body, sizes, cells),
        mesh=mesh,
        in_specs=(field, field, P(), P(), P(), P()),
        out_specs=(field, field, P(), P(), P(), P()),
        check_vma=False,
    )
```

```python
import functools
import itertools
import math

import jax
import jax.numpy as jnp
from jax import lax
from jax.experimental import pallas as pl
from jax.experimental.pallas import tpu as pltpu
from jax.sharding import PartitionSpec as P

MESH = pl.DeviceIdType.MESH
BF = jnp.bfloat16
F32 = jnp.float32
INV8 = 1.0 / math.sqrt(8.0)
STEPS = sorted(
    (d for d in itertools.product((-1, 0, 1), repeat=3) if d != (0, 0, 0)),
    key=lambda d: -sum(map(abs, d)),
)

NN = ((1,), (0,))
NT = ((1,), (1,))
TN = ((0,), (0,))


def dot(a, b, dims=NN):
    return lax.dot_general(a, b, (dims, ((), ())), preferred_element_type=F32)


def rows_cols(shape):
    return (
        lax.broadcasted_iota(jnp.int32, shape, 0),
        lax.broadcasted_iota(jnp.int32, shape, 1),
    )


def hot(cond):
    return jnp.where(cond, 1.0, 0.0).astype(BF)


def roll(a, shift):
    return pltpu.roll(a, shift % a.shape[1], 1)


def silu_slope(pre):
    sig = 0.5 * (1.0 + jnp.tanh(0.5 * pre))
    act = pre * sig
    return act, sig + act * (1.0 - sig)


def split(a):
    high = a.astype(BF)
    return high, (a - high.astype(F32)).astype(BF)


class Place:
    def __init__(self, sizes):
        self.size = dict(zip(("x", "y", "z"), sizes))
        self.at = {
            "x": lax.axis_index("gx"),
            "y": lax.axis_index("gy"),
            "z": lax.axis_index("gz"),
        }

    def near(self, axis, step):
        size = self.size[axis]
        return lax.rem(self.at[axis] + (step + size), size)

    def device(self, dz, dx, dy):
        return (self.near("x", dx), self.near("y", dy), self.near("z", dz))

    def inside(self, axis, step):
        if step == 0:
            return None
        if step < 0:
            return self.at[axis] > 0
        return self.at[axis] < self.size[axis] - 1


class Halo:
    def __init__(self, place, pad, face, got, send, recv, nz, nx, ch, ylen):
        self.place, self.pad, self.face, self.got = place, pad, face, got
        self.send, self.recv = send, recv
        self.nz, self.nx, self.ch, self.ylen = nz, nx, ch, ylen

    def put(self, z, value):
        self.pad[z + 1, self.ch : self.ch * (self.nx + 1), :] = value

    def start(self):
        nz, nx, ch = self.nz, self.nx, self.ch
        r, c = rows_cols((32, nz * 128))
        edge = jnp.where(r >= 16, self.ylen - 1, 0)
        pick = hot(((r & 15) == (c >> 7)) & ((c & 127) == edge))
        own = jnp.concatenate(
            [self.pad[z + 1, ch : ch * (nx + 1), :] for z in range(nz)], axis=1
        )
        both = dot(pick, own, NT).astype(BF)
        self.face[0] = both[:16]
        self.face[1] = both[16:]
        self.copies = []
        for i, (dz, dx, dy) in enumerate(STEPS):
            if dy == 0:
                zs = {-1: (1, 1), 0: (1, nz), 1: (nz, 1)}[dz]
                xs = {-1: (ch, ch), 0: (ch, nx * ch), 1: (nx * ch, ch)}[dx]
                zd = {-1: nz + 1, 0: 1, 1: 0}[dz]
                xd = {-1: (nx + 1) * ch, 0: ch, 1: 0}[dx]
                src = self.pad.at[pl.ds(zs[0], zs[1]), pl.ds(xs[0], xs[1])]
                dst = self.pad.at[pl.ds(zd, zs[1]), pl.ds(xd, xs[1])]
            else:
                side = 0 if dy == 1 else 1
                src = self.face.at[1 - side]
                dst = self.got.at[1 - dx, side, 1 - dz]
            copy = pltpu.make_async_remote_copy(
                src_ref=src,
                dst_ref=dst,
                send_sem=self.send.at[i],
                recv_sem=self.recv.at[i],
                device_id=self.place.device(dz, dx, dy),
                device_id_type=MESH,
            )
            copy.start()
            self.copies.append(copy)

    def arrive(self):
        for copy in self.copies:
            copy.wait_recv()
        nz, nx, ch = self.nz, self.nx, self.ch
        at, size = self.place.at, self.place.size
        plane = jnp.zeros(self.pad.shape[1:], BF)
        column = jnp.zeros((nz + 2, ch, 128), BF)

        @pl.when(at["z"] == 0)
        def _():
            self.pad[0] = plane

        @pl.when(at["z"] == size["z"] - 1)
        def _():
            self.pad[nz + 1] = plane

        @pl.when(at["x"] == 0)
        def _():
            self.pad[:, 0:ch, :] = column

        @pl.when(at["x"] == size["x"] - 1)
        def _():
            self.pad[:, (nx + 1) * ch :, :] = column

    def columns(self):
        nz, nx, ch = self.nz, self.nx, self.ch
        at, size = self.place.at, self.place.size
        r, c = rows_cols((96, 128))
        group, z = r >> 4, r & 15
        side = jnp.where(group >= 3, 1, 0)
        dz = group - 3 * side
        zp = c & 15
        first, last = (
            jnp.where(at["z"] > 0, 0, -1),
            jnp.where(at["z"] < size["z"] - 1, nz + 1, -1),
        )
        low, high = (
            jnp.where(at["y"] > 0, 0, -1),
            jnp.where(at["y"] < size["y"] - 1, 1, -1),
        )
        mid = (dz == 1) & (z < nz) & (zp == z + 1)
        below = (dz == 0) & (z == nz - 1) & (zp == first)
        above = (dz == 2) & (z == 0) & (zp == last)
        lane = (side == (c >> 4)) & ((side == low) | (side == high))
        pick = hot((mid | below | above) & lane)
        parts = []
        for dx in range(3):
            wide = slice(0, nx * ch)
            if dx == 0:
                wide = slice((nx - 1) * ch, nx * ch)
            if dx == 2:
                wide = slice(0, ch)
            src = self.got[dx].reshape(96, nx * ch)[:, wide]
            part = dot(src, pick, TN)
            if dx != 1:
                part = jnp.where(self.place.inside("x", dx - 1), part, 0.0)
            parts.append(part.astype(BF))
        return jnp.concatenate(parts, axis=0)

    def shifted(self):
        cols = self.columns()
        lane = rows_cols(cols.shape)[1]
        for zp in range(self.nz + 2):
            base = self.pad[zp]
            low = jnp.where(lane == 0, roll(cols, -zp), roll(base, 1))
            end = self.ylen - 1
            high = jnp.where(lane == end, roll(cols, end - 16 - zp), roll(base, -1))
            yield zp, (low, base, high)

    def finish(self):
        for copy in self.copies:
            copy.wait_send()


def fill_fine(halo, u):
    rows = (halo.nx + 2) * halo.ch
    for zp, parts in halo.shifted():
        for ky, part in enumerate(parts):
            if zp <= 5:
                u[zp, ky * rows : (ky + 1) * rows, 0:128] = part
            if zp >= 4:
                u[zp - 4, ky * rows : (ky + 1) * rows, 128:256] = part


def fill_half(halo, u):
    before = None
    for zp, parts in halo.shifted():
        if before is not None:
            j = zp - 1
            for ky in range(3):
                lane = rows_cols(parts[ky].shape)[1]
                both = jnp.where(lane < 64, before[ky], roll(parts[ky], 64))
                if j <= 2:
                    u[j * 3 + ky, :, 0:128] = both
                if j >= 2:
                    u[(j - 2) * 3 + ky, :, 128:256] = both
        before = parts


def put_half(halo, value):
    lane = rows_cols((value.shape[0], 128))[1]
    for z in range(4):
        half = value[:, 128 * (z // 2) : 128 * (z // 2) + 128]
        if z % 2:
            half = roll(half, 64)
        halo.put(z, jnp.where(lane < 64, half, jnp.zeros_like(half)))


def toeplitz(dst, blocks, nx, rows, width):
    dst[...] = jnp.zeros(dst.shape, BF)
    for kz, ky in itertools.product(range(3), range(3)):
        band = jnp.concatenate([blocks(kz, kx, ky) for kx in range(3)], axis=1)
        base = (kz * 3 + ky) * (nx + 2) * width
        for x in range(nx):
            dst[rows * x : rows * (x + 1), base + width * x : base + width * (x + 3)] = band


class Group:
    def __init__(self, place, kind, send, recv):
        self.place, self.kind, self.send, self.recv = place, kind, send, recv
        size = place.size
        self.count = {
            "sheet": size["x"] * size["y"],
            "row": size["x"],
            "depth": size["z"],
        }[kind]

    def member(self, q):
        at, size = self.place.at, self.place.size
        if self.kind == "sheet":
            x = lax.rem(at["x"] + q // size["y"], size["x"])
            y = lax.rem(at["y"] + lax.rem(q, size["y"]), size["y"])
            return (x, y, at["z"]), x * size["y"] + y
        if self.kind == "depth":
            z = lax.rem(at["z"] + q, size["z"])
            return (at["x"], at["y"], z), z
        x = lax.rem(at["x"] + q, size["x"])
        return (x, at["y"], at["z"]), x

    def start(self, src, dst):
        def one(q, carry):
            device, index = self.member(q)
            pltpu.make_async_remote_copy(
                src_ref=src(index),
                dst_ref=dst,
                send_sem=self.send,
                recv_sem=self.recv,
                device_id=device,
                device_id_type=MESH,
            ).start()
            return carry

        lax.fori_loop(1, self.count, one, 0)

    def _all(self, ref):
        return pltpu.make_async_remote_copy(
            src_ref=ref,
            dst_ref=ref,
            send_sem=self.send,
            recv_sem=self.recv,
            device_id=self.member(1)[0],
            device_id_type=MESH,
        )

    def arrive(self, ref):
        self._all(ref).wait_recv()

    def finish(self, ref):
        self._all(ref).wait_send()


def some(ref, count):
    return ref.at[pl.ds(0, count)]


class Total:
    def __init__(self, place, mine, landed, line, done, send, recv):
        self.mine, self.landed, self.line, self.done = mine, landed, line, done
        self.at = place.at
        self.me = place.at["x"] * place.size["y"] + place.at["y"]
        self.one = Group(place, "sheet", send.at[0], recv.at[0])
        self.two = Group(place, "depth", send.at[1], recv.at[1])
        self.three = Group(place, "sheet", send.at[2], recv.at[2])

    def scatter(self):
        self.one.start(lambda index: self.mine.at[index], self.landed.at[self.me])
        self.landed[self.me] = self.mine[self.me]

    def cross(self):
        self.one.arrive(some(self.landed, self.one.count - 1))
        self.line[self.at["z"]] = jnp.sum(self.landed[...], axis=0)
        own = self.line.at[self.at["z"]]
        self.two.start(lambda index: own, own)

    def gather(self, scale):
        self.two.arrive(some(self.line, self.two.count - 1))
        total = jnp.sum(self.line[...], axis=0) * scale
        self.done[self.me] = total.astype(self.done.dtype)
        own = self.done.at[self.me]
        self.three.start(lambda index: own, own)

    def arrive(self):
        self.three.arrive(some(self.done, self.one.count - 1))

    def finish(self):
        self.one.finish(some(self.landed, self.one.count - 1))
        self.two.finish(some(self.line, self.two.count - 1))
        self.three.finish(some(self.done, self.one.count - 1))


def kernel(
    sizes, scales, vol_in, cot_in, w1_in, w2_in, w3_in, w4_in,
    out, gvol, d1, d2, d3,
    v_pad, v_face, v_got, q_pad, q_face, q_got,
    h_pad, h_face, h_got, g_pad, g_face, g_got,
    u1, ug, u2, uh, t1, tt1, t2, tt2,
    sl1, act1, cot1, g1, send, recv,
    zbox, note, wide1, wide2, near_y, tap_part, tap_sum, tap_line, tap_all,
    m1, l1, y1, f1, m2, l2, y2, f2, gsend, grecv,
    vol, cot, w1, w2, w3, w4, out_v, gvol_v, local, zsend, zrecv, csend, crecv,
):
    place = Place(sizes)
    barrier = pltpu.get_barrier_semaphore()
    partners = [place.device(*s) for s in STEPS if s[0] != 0 and s[1:] != (0, 0)]
    for device in partners:
        pl.semaphore_signal(barrier, inc=1, device_id=device, device_id_type=MESH)
    total = len(partners)
    for kind in ("sheet", "depth"):
        group = Group(place, kind, None, None)

        def greet(q, carry, group=group):
            device = group.member(q)[0]
            pl.semaphore_signal(barrier, inc=1, device_id=device, device_id_type=MESH)
            return carry

        lax.fori_loop(1, group.count, greet, 0)
        total += group.count - 1
    across, deep, row = [
        Group(place, kind, gsend.at[i], grecv.at[i])
        for i, kind in enumerate(("depth", "depth", "row"))
    ]
    loads = [
        pltpu.make_async_copy(src, dst, local.at[i])
        for i, (src, dst) in enumerate(
            (
                (vol_in, vol), (cot_in, cot), (w1_in, w1),
                (w2_in, w2), (w3_in, w3), (w4_in, w4),
            )
        )
    ]
    for load in loads:
        load.start()
    stores = []

    def store(src, dst):
        copy = pltpu.make_async_copy(src, dst, local.at[len(loads) + len(stores)])
        copy.start()
        stores.append(copy)

    ix, iy, iz = place.at["x"], place.at["y"], place.at["z"]
    nx, ny = place.size["x"], place.size["y"]
    me = ix * ny + iy
    for wide in (wide1, wide2):
        for x in range(nx + 4):
            pads = (0, ny + 1) if 2 <= x < nx + 2 else range(ny + 2)
            for y in pads:
                wide[x * (ny + 2) + y] = jnp.zeros((16, 256), BF)
    m1[27:32] = jnp.zeros((5, 8, 128), F32)
    m2[27:32] = jnp.zeros((5, 16, 128), F32)
    r, c = rows_cols((256, 256))
    perm = hot(((r & 31) == (c >> 3)) & ((r >> 5) == (c & 7)))
    back = hot(((c & 31) == (r >> 3)) & ((c >> 5) == (r & 7)))

    def fine_rows(dst, zz, rows):
        rows = dot(back, rows).astype(BF)
        dst[:, zz] = rows[:, :128].reshape(32, 8, 128)
        dst[:, zz + 4] = rows[:, 128:].reshape(32, 8, 128)


    def two(ref, zz):
        return jnp.concatenate(
            [ref[:, zz].reshape(256, 128), ref[:, zz + 4].reshape(256, 128)], axis=1
        )

    hv = Halo(place, v_pad, v_face, v_got, send.at[0], recv.at[0], 8, 8, 32, 128)
    hq = Halo(place, q_pad, q_face, q_got, send.at[1], recv.at[1], 4, 4, 32, 64)
    hh = Halo(place, h_pad, h_face, h_got, send.at[2], recv.at[2], 4, 4, 64, 64)
    hg = Halo(place, g_pad, g_face, g_got, send.at[3], recv.at[3], 8, 8, 32, 128)
    sum1 = Total(place, m1, l1, y1, f1, gsend.at[pl.ds(5, 3)], grecv.at[pl.ds(5, 3)])
    sum2 = Total(place, m2, l2, y2, f2, gsend.at[pl.ds(8, 3)], grecv.at[pl.ds(8, 3)])
    loads[0].wait()
    for zz in range(4):
        rows = dot(perm, two(vol, zz)).astype(BF)
        hv.put(zz, rows[:, :128])
        hv.put(zz + 4, rows[:, 128:])
    pl.semaphore_wait(barrier, total)
    hv.start()
    for load in loads[1:]:
        load.wait()

    for zz in range(4):
        cot1[zz] = dot(perm, two(cot, zz)).astype(BF)
    r, c = rows_cols((32, 32))
    eye = hot(r == c)
    toeplitz(t1, lambda kz, kx, ky: w1[kz * 9 + kx * 3 + ky], 8, 32, 32)
    flat1 = dot(eye, w1[...].reshape(864, 32), NT).astype(BF)
    r, c = rows_cols((64, 64))
    flat2 = dot(hot(r == c), w2[...].reshape(864, 64), NT).astype(BF)

    def back_tap(kz, kx, ky):
        return (2 - kz) * 9 + (2 - kx) * 3 + (2 - ky)

    def turned(kz, kx, ky):
        k = back_tap(kz, kx, ky)
        return flat1[:, k * 32 : (k + 1) * 32]

    def straight(kz, kx, ky):
        k = kz * 9 + kx * 3 + ky
        return flat2[:, k * 32 : (k + 1) * 32]

    toeplitz(t2, straight, 4, 64, 32)
    toeplitz(tt1, turned, 8, 32, 32)
    toeplitz(tt2, lambda *k: w2[back_tap(*k)], 4, 32, 64)
    cg = jnp.sum(cot[...].astype(F32), axis=(1, 2))
    cg = cg + roll(cg, -1)
    cg = cg + roll(cg, -2)
    cg = (cg + roll(cg, -4)).astype(BF)

    hv.arrive()
    fill_fine(hv, u1)
    for zz in range(4):
        pre = dot(t1[...], u1[zz : zz + 3].reshape(2880, 256))
        act, slope = silu_slope(pre)
        act1[zz] = act.astype(BF)
        sl1[zz] = slope
    r, c = rows_cols((512, 256))
    z2 = 2 * ((r >> 7) & 1) + (r >> 8)
    pick = hot(((c >> 6) == z2) & ((r & 127) == 2 * (c & 63)))
    pooled = []
    for a, b in ((0, 1), (2, 3)):
        s = act1[a].astype(F32) + act1[b].astype(F32)
        s = jnp.sum(s.reshape(4, 2, 32, 256), axis=1).reshape(128, 256)
        s = s + roll(s, -1)
        pooled.append((s * INV8).astype(BF))
    q1 = dot(jnp.concatenate(pooled, axis=1), pick).astype(BF)
    put_half(hq, q1)
    hq.start()

    hq.arrive()
    fill_half(hq, u2)
    pre2 = dot(t2[...], u2[...].reshape(1728, 256))
    act2, slope2 = silu_slope(pre2)
    s = jnp.sum(act2.astype(BF).astype(F32).reshape(4, 64, 256), axis=0)
    s = s[:, :128] + s[:, 128:]
    s = s + roll(s, 64)
    s = s + roll(s, -1)
    s = s + roll(s, -2)
    cin = (s * 0.125).astype(BF)
    zero = jnp.zeros((64, 128), BF)
    r, c = rows_cols((16, 128))
    own = dot(hot(c == 4 * r), jnp.concatenate([cin, zero], axis=0), NT)
    own += dot(hot(c == 8 * r), jnp.concatenate([zero, cg, zero[:32]], axis=0), NT)
    own = own.astype(BF)
    zbox[2] = own
    above = []
    for step in (-2, -1, 1, 2):
        copy = pltpu.make_async_remote_copy(
            src_ref=zbox.at[2],
            dst_ref=zbox.at[2 - step],
            send_sem=zsend.at[step + 2],
            recv_sem=zrecv.at[step + 2],
            device_id=place.device(step, 0, 0),
            device_id_type=MESH,
        )
        copy.start()
        above.append(copy)
    for copy in above:
        copy.wait_recv()
    zs = []
    for step in range(-2, 3):
        block = zbox[step + 2]
        if step:
            at = iz + step
            block = jnp.where((at >= 0) & (at < place.size["z"]), block, jnp.zeros_like(block))
        zs.append(block)
    zero = jnp.zeros((16, 64), BF)
    cin, cg = [z[:, :64] for z in zs], [z[:, 64:96] for z in zs]
    note[0] = jnp.concatenate([cin[1], cin[2], cin[3], cg[2], zero[:, :32]], axis=1)
    note[1] = jnp.concatenate([cin[0], cin[4], cg[1], cg[3], zero], axis=1)
    mine = (ix + 2) * (ny + 2) + iy + 1

    def send_wide(which, dst, kind, dx, dy):
        pltpu.make_async_remote_copy(
            src_ref=note.at[which],
            dst_ref=dst.at[mine],
            send_sem=zsend.at[kind],
            recv_sem=zrecv.at[kind],
            device_id=place.device(0, dx, dy),
            device_id_type=MESH,
        ).start()

    def all_wide(dst, kind, count):
        ref = some(dst, count)
        return pltpu.make_async_remote_copy(
            src_ref=ref,
            dst_ref=ref,
            send_sem=zsend.at[kind],
            recv_sem=zrecv.at[kind],
            device_id=place.device(0, 0, 1),
            device_id_type=MESH,
        )

    for dy, dx in itertools.product((-1, 1, 0), range(nx)):
        if (dy, dx) != (0, 0):
            send_wide(0, wide1, 5, dx, dy)
            send_wide(1, wide2, 6, dx, dy)

    far = (ny - 3) * nx
    wide1[mine] = note[0]
    wide2[mine] = note[1]
    taps = list(itertools.product(range(3), range(3), range(3)))

    def w3_rows(kx, ky):
        return jnp.concatenate([w3[kz * 9 + kx * 3 + ky] for kz in range(3)], axis=0)

    all_wide(wide1, 5, 3 * nx - 1).wait_recv()
    all_wide(wide2, 6, 3 * nx - 1).wait_recv()

    def send_far(q, carry):
        send_wide(0, wide1, 7, lax.rem(q, nx), 2 + q // nx)
        return carry

    lax.fori_loop(0, far, send_far, 0)

    near, grads = [], []
    for j in range(5):
        slots = pl.ds((ix + j) * (ny + 2) + iy, 3)
        one, two_ = wide1[slots].reshape(48, 256), wide2[slots].reshape(48, 256)
        near += [two_[:, :64], one[:, :192], two_[:, 64:128]]
        grads.append([two_[8:40, 128:160], one[8:40, 192:224], two_[8:40, 160:192]])
    r, c = rows_cols((96, 48))
    near = dot(hot(c == (r & 31) + (r >> 5) + 7), jnp.concatenate(near, axis=1)).astype(BF)
    pre3 = 0.0
    for kx, ky in itertools.product(range(3), range(3)):
        rows = [
            near[32 * ky : 32 * ky + 32, 320 * (j + kx) + 64 * z :][:, :192]
            for z, j in itertools.product(range(3), range(3))
        ]
        pre3 = pre3 + dot(jnp.concatenate(rows, axis=0), w3_rows(kx, ky))
    act3, slope3 = silu_slope(pre3)
    act3 = act3[136:152].astype(BF)
    cgs = jnp.concatenate(
        [grads[j + 1][z] for z, j in itertools.product(range(3), range(3))], axis=0
    )
    cgt = own[:, 64:96]
    gp3 = (dot(cgs, w4[...]) * slope3).astype(BF)
    r, c = rows_cols((48, 32))
    near = jnp.concatenate([gp3[32 * i : 32 * i + 32] for i in range(9)], axis=1)
    near = dot(hot(c == (r & 15) + (r >> 4) + 7), near).astype(BF)

    def tap(kz, kx, ky):
        base = (kz * 3 + kx) * 256
        return near[16 * ky : 16 * (ky + 1), base : base + 256]

    gc = sum(
        dot(w3[kz * 9 + kx * 3 + ky], tap(2 - kz, 2 - kx, 2 - ky), NT)
        for kz, kx, ky in taps
    )
    r, c = rows_cols((16, 256))
    pick = hot(r == ((c & 63) >> 2))
    up = sum(dot(part, pick) for part in split(gc)) * 0.125
    gp2 = (jnp.concatenate([up] * 4, axis=0) * slope2).astype(BF)
    put_half(hh, gp2)
    hh.start()
    co = dot(w4[...], act3, NT).astype(BF)
    part4 = dot(cgt, act3, TN)
    for i in range(4):
        half, col = i % 2, 128 * (i // 2)
        m2[27 + i] = part4[16 * half : 16 * half + 16, col : col + 128]
    lane = rows_cols((16, 128))[1]
    for kz in range(3):
        g = dot(u2[3 * kz : 3 * kz + 3].reshape(576, 256), gp2, NT)
        for ky, kx in itertools.product(range(3), range(3)):
            cut = [
                g[ky * 192 + 32 * (x + kx) :][:32, 128 * (x // 2) : 128 * (x // 2) + 128]
                for x in range(4)
            ]
            even, odd = cut[0] + cut[2], cut[1] + cut[3]
            low = (even + roll(odd, 64))[:16]
            high = (roll(even, 64) + odd)[16:]
            m2[kz * 9 + kx * 3 + ky] = jnp.where(lane < 64, low, high)
    r, c = rows_cols((16, 128))
    co = dot(co, hot(r == (c >> 3)))
    co = jnp.concatenate([jnp.concatenate([co] * 8, axis=0)] * 2, axis=1)
    for zz in range(4):
        fine_rows(out_v, zz, (act1[zz].astype(F32) + co).astype(BF))
    store(out_v, out)
    all_wide(wide1, 7, far).wait_recv()
    for x in range(nx + 2):
        start = (x + 1) * (ny + 2)
        rows = wide1[start : start + ny + 2].reshape(16 * (ny + 2), 256)
        for ky in range(3):
            near_y[ky, x] = rows[15 + ky : 15 + ky + 16 * ny]
    size = nx * 16 * ny
    pre = 0.0
    for kx, ky in itertools.product(range(3), range(3)):
        rows = near_y[ky, kx : kx + nx].reshape(size, 256)[:, :192]
        pre = pre + dot(rows, w3_rows(kx, ky))
    slope = silu_slope(pre)[1]
    cgs = near_y[1, 1 : nx + 1].reshape(size, 256)[:, 192:224]
    gp = (dot(cgs, w4[...]) * slope).astype(BF)
    k = lax.rem(me, 27)
    kz, kx, ky = k // 9, lax.rem(k // 3, 3), lax.rem(k, 3)
    rows = near_y[ky, pl.ds(kx, nx)].reshape(size, 256)
    tap_part[...] = dot(rows, gp, TN).reshape(4, 8, 8, 256)
    tap_sum[...] = tap_part[kz]
    across.start(lambda index: tap_sum.at[index], tap_line.at[iz])
    tap_line[iz] = tap_sum[iz]
    hh.arrive()
    sum2.scatter()
    across.arrive(some(tap_line, across.count - 1))
    s = jnp.sum(tap_line[...], axis=0) * scales[2]
    tap_all[ix, iy, iz] = jnp.concatenate([s[:, :128], s[:, 128:]], axis=0).astype(BF)
    own_tap = tap_all.at[ix, iy, iz]
    deep.start(lambda index: own_tap, own_tap)
    fill_half(hh, uh)
    gpool = dot(tt2[...], uh[...].reshape(3456, 256))
    r, c = rows_cols((256, 256))
    parts = split(gpool)
    for h in range(2):
        pick = hot(((r >> 6) == 2 * (c >> 7) + h) & ((r & 63) == ((c & 127) >> 1)))
        up = sum(dot(part, pick) for part in parts) * INV8
        up = jnp.concatenate(
            [up[32 * (x // 2) : 32 * (x // 2) + 32] for x in range(8)], axis=0
        )
        for zz in (2 * h, 2 * h + 1):
            gp1 = ((cot1[zz].astype(F32) + up) * sl1[zz]).astype(BF)
            hg.put(zz, gp1[:, :128])
            hg.put(zz + 4, gp1[:, 128:])
            g1[:, 256 * zz : 256 * zz + 256] = gp1
    for kz in range(3):
        uc = jnp.concatenate([u1[kz + zz] for zz in range(4)], axis=1)
        g = dot(g1[...], uc, NT)
        for ky in range(3):
            band = sum(
                g[32 * x : 32 * x + 32, ky * 320 + 32 * x : ky * 320 + 32 * x + 96]
                for x in range(8)
            )
            for kx in range(3):
                m1[kz * 9 + kx * 3 + ky] = jnp.concatenate(
                    [band[8 * i : 8 * i + 8, 32 * kx : 32 * kx + 32] for i in range(4)],
                    axis=1,
                )
    sum1.scatter()
    hg.start()
    deep_all = some(tap_all.at[ix, iy], deep.count - 1)
    deep.arrive(deep_all)
    own_depth = tap_all.at[ix, iy]
    row.start(lambda index: own_depth, own_depth)
    sum2.cross()
    sum1.cross()
    row_all = tap_all.at[pl.ds(0, nx - 1), iy]
    row.arrive(row_all)
    other = iy + 1 - 2 * lax.rem(iy, 2)

    def range_copy(y, target, lane):
        block = tap_all.at[pl.ds(0, nx), y]
        return pltpu.make_async_remote_copy(
            src_ref=block,
            dst_ref=block,
            send_sem=csend.at[lane],
            recv_sem=crecv.at[lane],
            device_id=(ix, target, iz),
            device_id_type=MESH,
        )

    hops = range(1, ny // 2)
    ranges = [range_copy(iy, lax.rem(iy + 2 * s, ny), s) for s in hops]
    for copy in ranges:
        copy.start()
    passed = [range_copy(iy, other, ny // 2)]
    passed[0].start()
    hg.arrive()
    fill_fine(hg, ug)
    sum2.gather(scales[1])
    sum1.gather(scales[0])
    for zz in range(4):
        rows = dot(tt1[...], ug[zz : zz + 3].reshape(2880, 256))
        fine_rows(gvol_v, zz, rows.astype(BF))
    store(gvol_v, gvol)
    for s, copy in zip(hops, ranges):
        copy.wait_recv()
        passed.append(range_copy(lax.rem(iy + ny - 2 * s, ny), other, ny // 2 + s))
        passed[-1].start()
    sum2.arrive()
    store(f2, d2)
    sum1.arrive()
    store(f1, d1)
    for copy in passed:
        copy.wait_recv()
    store(tap_all, d3)
    for copy in ranges + passed:
        copy.wait_send()
    for halo in (hv, hq, hh, hg):
        halo.finish()
    for copy in above:
        copy.wait_send()
    all_wide(wide1, 5, 3 * nx - 1).wait_send()
    all_wide(wide2, 6, 3 * nx - 1).wait_send()
    all_wide(wide1, 7, far).wait_send()
    across.finish(some(tap_line, across.count - 1))
    deep.finish(deep_all)
    row.finish(row_all)
    sum1.finish()
    sum2.finish()
    for copy in stores:
        copy.wait()


def last_kernel(
    scale, out_in, gvol_in, f1_in, f2_in, tap_in,
    out, gvol, d1, d2, d3, d4,
    f1, f2, tap_all, out_v, gvol_v, v1, v2, v3, sems,
):
    copies = []

    def copy(src, dst):
        one = pltpu.make_async_copy(src, dst, sems.at[len(copies)])
        one.start()
        copies.append(one)
        return one

    loads = [
        copy(tap_in, tap_all), copy(f2_in, f2), copy(f1_in, f1),
        copy(out_in, out_v), copy(gvol_in, gvol_v),
    ]
    loads[0].wait()
    for k in range(27):
        for j in range(8):
            block = tap_all[k // 8, k % 8, j].astype(F32)
            v3[k, 8 * j : 8 * j + 8, :] = jnp.concatenate([block[:8], block[8:]], axis=1)
        if k % 9 == 8:
            copy(v3.at[pl.ds(k - 8, 9)], d3.at[pl.ds(k - 8, 9)])
        if k == 8:
            for load in loads[3:]:
                load.wait()
            copy(out_v, out)
            copy(gvol_v, gvol)
    loads[1].wait()
    for k in range(27):
        wide = f2[k].astype(F32)
        v2[k] = jnp.concatenate([wide[:, :64], wide[:, 64:]], axis=0)
    copy(v2, d2)
    loads[2].wait()
    for k in range(27):
        wide = f1[k]
        v1[k] = jnp.concatenate([wide[:, 32 * i : 32 * i + 32] for i in range(4)], axis=0)
    copy(v1, d1)
    for i in range(4):
        half, col = i % 2, 128 * (i // 2)
        d4[16 * half : 16 * half + 16, col : col + 128] = f2[27 + i].astype(F32) * scale
    for one in copies[5:]:
        one.wait()


def halo_scratch(nz, nx, ch):
    return [
        pltpu.VMEM((nz + 2, (nx + 2) * ch, 128), BF),
        pltpu.VMEM((2, 16, nx * ch), BF),
        pltpu.VMEM((3, 2, 3, 16, nx * ch), BF),
    ]


def body(sizes, cells, vol, cot, w1, w2, w3, w4):
    shape = jax.ShapeDtypeStruct
    field = shape((32, 8, 8, 128), BF)
    vmem = pl.BlockSpec(memory_space=pltpu.VMEM)
    nx, ny, nz = sizes
    coarse = 1.0 / math.sqrt(cells / 512.0)
    scales = (1.0 / math.sqrt(cells * 1.0), 1.0 / math.sqrt(cells / 8.0), coarse)
    total = lambda r: [
        pltpu.VMEM((32, r, 128), F32),
        pltpu.VMEM((32, r, 128), F32),
        pltpu.VMEM((nz, r, 128), F32),
        pltpu.VMEM((32, r, 128), F32 if r == 8 else BF),
    ]
    anywhere = pl.BlockSpec(memory_space=pl.ANY)
    mid = pl.pallas_call(
        functools.partial(kernel, sizes, scales),
        out_shape=[
            field,
            field,
            shape((32, 8, 128), F32),
            shape((32, 16, 128), BF),
            shape((nx, ny, 8, 16, 128), BF),
        ],
        in_specs=[anywhere] * 6,
        out_specs=[anywhere] * 5,
        scratch_shapes=[
            *halo_scratch(8, 8, 32),
            *halo_scratch(4, 4, 32),
            *halo_scratch(4, 4, 64),
            *halo_scratch(8, 8, 32),
            pltpu.VMEM((6, 960, 256), BF),
            pltpu.VMEM((6, 960, 256), BF),
            pltpu.VMEM((9, 192, 256), BF),
            pltpu.VMEM((9, 384, 256), BF),
            pltpu.VMEM((256, 2880), BF),
            pltpu.VMEM((256, 2880), BF),
            pltpu.VMEM((256, 1728), BF),
            pltpu.VMEM((128, 3456), BF),
            pltpu.VMEM((4, 256, 256), F32),
            pltpu.VMEM((4, 256, 256), BF),
            pltpu.VMEM((4, 256, 256), BF),
            pltpu.VMEM((256, 1024), BF),
            pltpu.SemaphoreType.DMA((4, 26)),
            pltpu.SemaphoreType.DMA((4, 26)),
            pltpu.VMEM((5, 16, 128), BF),
            pltpu.VMEM((2, 16, 256), BF),
            pltpu.VMEM(((nx + 4) * (ny + 2), 16, 256), BF),
            pltpu.VMEM(((nx + 4) * (ny + 2), 16, 256), BF),
            pltpu.VMEM((3, nx + 2, 16 * ny, 256), BF),
            pltpu.VMEM((4, 8, 8, 256), F32),
            pltpu.VMEM((8, 8, 256), F32),
            pltpu.VMEM((nz, 8, 256), F32),
            pltpu.VMEM((nx, ny, 8, 16, 128), BF),
            *total(8),
            *total(16),
            pltpu.SemaphoreType.DMA((11,)),
            pltpu.SemaphoreType.DMA((11,)),
            pltpu.VMEM((32, 8, 8, 128), BF),
            pltpu.VMEM((32, 8, 8, 128), BF),
            pltpu.VMEM((27, 32, 32), BF),
            pltpu.VMEM((27, 32, 64), BF),
            pltpu.VMEM((27, 64, 256), BF),
            pltpu.VMEM((32, 256), BF),
            pltpu.VMEM((32, 8, 8, 128), BF),
            pltpu.VMEM((32, 8, 8, 128), BF),
            pltpu.SemaphoreType.DMA((11,)),
            pltpu.SemaphoreType.DMA((8,)),
            pltpu.SemaphoreType.DMA((8,)),
            pltpu.SemaphoreType.DMA((ny,)),
            pltpu.SemaphoreType.DMA((ny,)),
        ],
        compiler_params=pltpu.CompilerParams(
            collective_id=0, has_side_effects=True, vmem_limit_bytes=60 * 1024 * 1024
        ),
        name="unet",
    )(vol, cot, w1, jnp.swapaxes(w2, 1, 2), jnp.swapaxes(w3, 1, 2), w4)
    finals = [
        field,
        field,
        shape((27, 32, 32), F32),
        shape((27, 32, 64), F32),
        shape((27, 64, 256), F32),
        shape((32, 256), F32),
    ]
    out, gvol, d1, d2, d3, d4 = pl.pallas_call(
        functools.partial(last_kernel, scales[2] / scales[1]),
        out_shape=finals,
        in_specs=[anywhere] * 5,
        out_specs=[anywhere] * 5 + [vmem],
        scratch_shapes=[pltpu.VMEM(f.shape, f.dtype) for f in list(mid[2:]) + finals[:5]]
        + [pltpu.SemaphoreType.DMA((12,))],
        compiler_params=pltpu.CompilerParams(vmem_limit_bytes=60 * 1024 * 1024),
        name="finish",
    )(*mid)
    return out, gvol, d1, jnp.swapaxes(d2, 1, 2), jnp.swapaxes(d3, 1, 2), d4


def solution(mesh):
    sizes = (mesh.shape["gx"], mesh.shape["gy"], mesh.shape["gz"])
    cells = 8 * 8 * 128 * sizes[0] * sizes[1] * sizes[2]
    field = P(None, "gz", "gx", "gy")
    return jax.shard_map(
        functools.partial(body, sizes, cells),
        mesh=mesh,
        in_specs=(field, field, P(), P(), P(), P()),
        out_specs=(field, field, P(), P(), P(), P()),
        check_vma=False,
    )
```

```python
import functools
import itertools
import math

import jax
import jax.numpy as jnp
from jax import lax
from jax.experimental import pallas as pl
from jax.experimental.pallas import tpu as pltpu
from jax.sharding import PartitionSpec as P

MESH = pl.DeviceIdType.MESH
BF = jnp.bfloat16
F32 = jnp.float32
INV8 = 1.0 / math.sqrt(8.0)
STEPS = sorted(
    (d for d in itertools.product((-1, 0, 1), repeat=3) if d != (0, 0, 0)),
    key=lambda d: -sum(map(abs, d)),
)

NN = ((1,), (0,))
NT = ((1,), (1,))
TN = ((0,), (0,))


def dot(a, b, dims=NN):
    return lax.dot_general(a, b, (dims, ((), ())), preferred_element_type=F32)


def rows_cols(shape):
    return (
        lax.broadcasted_iota(jnp.int32, shape, 0),
        lax.broadcasted_iota(jnp.int32, shape, 1),
    )


def hot(cond):
    return jnp.where(cond, 1.0, 0.0).astype(BF)


def roll(a, shift):
    return pltpu.roll(a, shift % a.shape[1], 1)


def silu_slope(pre):
    sig = 0.5 * (1.0 + jnp.tanh(0.5 * pre))
    act = pre * sig
    return act, sig + act * (1.0 - sig)


def split(a):
    high = a.astype(BF)
    return high, (a - high.astype(F32)).astype(BF)


class Place:
    def __init__(self, sizes):
        self.size = dict(zip(("x", "y", "z"), sizes))
        self.at = {
            "x": lax.axis_index("gx"),
            "y": lax.axis_index("gy"),
            "z": lax.axis_index("gz"),
        }

    def near(self, axis, step):
        size = self.size[axis]
        return lax.rem(self.at[axis] + (step + size), size)

    def device(self, dz, dx, dy):
        return (self.near("x", dx), self.near("y", dy), self.near("z", dz))

    def inside(self, axis, step):
        if step == 0:
            return None
        if step < 0:
            return self.at[axis] > 0
        return self.at[axis] < self.size[axis] - 1


class Halo:
    def __init__(self, place, pad, face, got, send, recv, nz, nx, ch, ylen):
        self.place, self.pad, self.face, self.got = place, pad, face, got
        self.send, self.recv = send, recv
        self.nz, self.nx, self.ch, self.ylen = nz, nx, ch, ylen

    def put(self, z, value):
        self.pad[z + 1, self.ch : self.ch * (self.nx + 1), :] = value

    def start(self):
        nz, nx, ch = self.nz, self.nx, self.ch
        r, c = rows_cols((32, nz * 128))
        edge = jnp.where(r >= 16, self.ylen - 1, 0)
        pick = hot(((r & 15) == (c >> 7)) & ((c & 127) == edge))
        own = jnp.concatenate(
            [self.pad[z + 1, ch : ch * (nx + 1), :] for z in range(nz)], axis=1
        )
        both = dot(pick, own, NT).astype(BF)
        self.face[0] = both[:16]
        self.face[1] = both[16:]
        self.copies = []
        for i, (dz, dx, dy) in enumerate(STEPS):
            if dy == 0:
                zs = {-1: (1, 1), 0: (1, nz), 1: (nz, 1)}[dz]
                xs = {-1: (ch, ch), 0: (ch, nx * ch), 1: (nx * ch, ch)}[dx]
                zd = {-1: nz + 1, 0: 1, 1: 0}[dz]
                xd = {-1: (nx + 1) * ch, 0: ch, 1: 0}[dx]
                src = self.pad.at[pl.ds(zs[0], zs[1]), pl.ds(xs[0], xs[1])]
                dst = self.pad.at[pl.ds(zd, zs[1]), pl.ds(xd, xs[1])]
            else:
                side = 0 if dy == 1 else 1
                src = self.face.at[1 - side]
                dst = self.got.at[1 - dx, side, 1 - dz]
            copy = pltpu.make_async_remote_copy(
                src_ref=src,
                dst_ref=dst,
                send_sem=self.send.at[i],
                recv_sem=self.recv.at[i],
                device_id=self.place.device(dz, dx, dy),
                device_id_type=MESH,
            )
            copy.start()
            self.copies.append(copy)

    def arrive(self):
        for copy in self.copies:
            copy.wait_recv()
        nz, nx, ch = self.nz, self.nx, self.ch
        at, size = self.place.at, self.place.size
        plane = jnp.zeros(self.pad.shape[1:], BF)
        column = jnp.zeros((nz + 2, ch, 128), BF)

        @pl.when(at["z"] == 0)
        def _():
            self.pad[0] = plane

        @pl.when(at["z"] == size["z"] - 1)
        def _():
            self.pad[nz + 1] = plane

        @pl.when(at["x"] == 0)
        def _():
            self.pad[:, 0:ch, :] = column

        @pl.when(at["x"] == size["x"] - 1)
        def _():
            self.pad[:, (nx + 1) * ch :, :] = column

    def columns(self):
        nz, nx, ch = self.nz, self.nx, self.ch
        at, size = self.place.at, self.place.size
        r, c = rows_cols((96, 128))
        group, z = r >> 4, r & 15
        side = jnp.where(group >= 3, 1, 0)
        dz = group - 3 * side
        zp = c & 15
        first, last = (
            jnp.where(at["z"] > 0, 0, -1),
            jnp.where(at["z"] < size["z"] - 1, nz + 1, -1),
        )
        low, high = (
            jnp.where(at["y"] > 0, 0, -1),
            jnp.where(at["y"] < size["y"] - 1, 1, -1),
        )
        mid = (dz == 1) & (z < nz) & (zp == z + 1)
        below = (dz == 0) & (z == nz - 1) & (zp == first)
        above = (dz == 2) & (z == 0) & (zp == last)
        lane = (side == (c >> 4)) & ((side == low) | (side == high))
        pick = hot((mid | below | above) & lane)
        parts = []
        for dx in range(3):
            wide = slice(0, nx * ch)
            if dx == 0:
                wide = slice((nx - 1) * ch, nx * ch)
            if dx == 2:
                wide = slice(0, ch)
            src = self.got[dx].reshape(96, nx * ch)[:, wide]
            part = dot(src, pick, TN)
            if dx != 1:
                part = jnp.where(self.place.inside("x", dx - 1), part, 0.0)
            parts.append(part.astype(BF))
        return jnp.concatenate(parts, axis=0)

    def shifted(self):
        cols = self.columns()
        lane = rows_cols(cols.shape)[1]
        for zp in range(self.nz + 2):
            base = self.pad[zp]
            low = jnp.where(lane == 0, roll(cols, -zp), roll(base, 1))
            end = self.ylen - 1
            high = jnp.where(lane == end, roll(cols, end - 16 - zp), roll(base, -1))
            yield zp, (low, base, high)

    def finish(self):
        for copy in self.copies:
            copy.wait_send()


def fill_fine(halo, u):
    rows = (halo.nx + 2) * halo.ch
    for zp, parts in halo.shifted():
        for ky, part in enumerate(parts):
            if zp <= 5:
                u[zp, ky * rows : (ky + 1) * rows, 0:128] = part
            if zp >= 4:
                u[zp - 4, ky * rows : (ky + 1) * rows, 128:256] = part


def fill_half(halo, u):
    before = None
    for zp, parts in halo.shifted():
        if before is not None:
            j = zp - 1
            for ky in range(3):
                lane = rows_cols(parts[ky].shape)[1]
                both = jnp.where(lane < 64, before[ky], roll(parts[ky], 64))
                if j <= 2:
                    u[j * 3 + ky, :, 0:128] = both
                if j >= 2:
                    u[(j - 2) * 3 + ky, :, 128:256] = both
        before = parts


def put_half(halo, value):
    lane = rows_cols((value.shape[0], 128))[1]
    for z in range(4):
        half = value[:, 128 * (z // 2) : 128 * (z // 2) + 128]
        if z % 2:
            half = roll(half, 64)
        halo.put(z, jnp.where(lane < 64, half, jnp.zeros_like(half)))


def toeplitz(dst, blocks, nx, rows, width):
    dst[...] = jnp.zeros(dst.shape, BF)
    for kz, ky in itertools.product(range(3), range(3)):
        band = jnp.concatenate([blocks(kz, kx, ky) for kx in range(3)], axis=1)
        base = (kz * 3 + ky) * (nx + 2) * width
        for x in range(nx):
            dst[rows * x : rows * (x + 1), base + width * x : base + width * (x + 3)] = band


class Group:
    def __init__(self, place, kind, send, recv):
        self.place, self.kind, self.send, self.recv = place, kind, send, recv
        size = place.size
        self.count = {
            "sheet": size["x"] * size["y"],
            "row": size["x"],
            "depth": size["z"],
        }[kind]

    def member(self, q):
        at, size = self.place.at, self.place.size
        if self.kind == "sheet":
            x = lax.rem(at["x"] + q // size["y"], size["x"])
            y = lax.rem(at["y"] + lax.rem(q, size["y"]), size["y"])
            return (x, y, at["z"]), x * size["y"] + y
        if self.kind == "depth":
            z = lax.rem(at["z"] + q, size["z"])
            return (at["x"], at["y"], z), z
        x = lax.rem(at["x"] + q, size["x"])
        return (x, at["y"], at["z"]), x

    def start(self, src, dst):
        def one(q, carry):
            device, index = self.member(q)
            pltpu.make_async_remote_copy(
                src_ref=src(index),
                dst_ref=dst,
                send_sem=self.send,
                recv_sem=self.recv,
                device_id=device,
                device_id_type=MESH,
            ).start()
            return carry

        lax.fori_loop(1, self.count, one, 0)

    def _all(self, ref):
        return pltpu.make_async_remote_copy(
            src_ref=ref,
            dst_ref=ref,
            send_sem=self.send,
            recv_sem=self.recv,
            device_id=self.member(1)[0],
            device_id_type=MESH,
        )

    def arrive(self, ref):
        self._all(ref).wait_recv()

    def finish(self, ref):
        self._all(ref).wait_send()


def some(ref, count):
    return ref.at[pl.ds(0, count)]


class Total:
    def __init__(self, place, mine, landed, line, done, send, recv):
        self.mine, self.landed, self.line, self.done = mine, landed, line, done
        self.at = place.at
        self.me = place.at["x"] * place.size["y"] + place.at["y"]
        self.one = Group(place, "sheet", send.at[0], recv.at[0])
        self.two = Group(place, "depth", send.at[1], recv.at[1])
        self.three = Group(place, "sheet", send.at[2], recv.at[2])

    def scatter(self):
        self.one.start(lambda index: self.mine.at[index], self.landed.at[self.me])
        self.landed[self.me] = self.mine[self.me]

    def cross(self):
        self.one.arrive(some(self.landed, self.one.count - 1))
        self.line[self.at["z"]] = jnp.sum(self.landed[...].astype(F32), axis=0)
        own = self.line.at[self.at["z"]]
        self.two.start(lambda index: own, own)

    def gather(self, scale):
        self.two.arrive(some(self.line, self.two.count - 1))
        total = jnp.sum(self.line[...], axis=0) * scale
        self.done[self.me] = total.astype(self.done.dtype)
        own = self.done.at[self.me]
        self.three.start(lambda index: own, own)

    def arrive(self):
        self.three.arrive(some(self.done, self.one.count - 1))

    def finish(self):
        self.one.finish(some(self.landed, self.one.count - 1))
        self.two.finish(some(self.line, self.two.count - 1))
        self.three.finish(some(self.done, self.one.count - 1))


def kernel(
    sizes, scales, vol_in, cot_in, w1_in, w2_in, w3_in, w4_in,
    out, gvol, d1, d2, d3,
    v_pad, v_face, v_got, q_pad, q_face, q_got,
    h_pad, h_face, h_got, g_pad, g_face, g_got,
    u1, ug, u2, uh, t1, tt1, t2, tt2,
    sl1, act1, cot1, g1, send, recv,
    zbox, note, wide, near_y, tap_part, tap_sum, tap_line, tap_all,
    m1, l1, y1, f1, m2, l2, y2, f2, gsend, grecv,
    vol, cot, w1, w2, w3, w4, out_v, gvol_v, local, zsend, zrecv, csend, crecv,
):
    place = Place(sizes)
    barrier = pltpu.get_barrier_semaphore()
    partners = [place.device(*s) for s in STEPS if s[0] != 0 and s[1:] != (0, 0)]
    for device in partners:
        pl.semaphore_signal(barrier, inc=1, device_id=device, device_id_type=MESH)
    total = len(partners)
    for kind in ("sheet", "depth"):
        group = Group(place, kind, None, None)

        def greet(q, carry, group=group):
            device = group.member(q)[0]
            pl.semaphore_signal(barrier, inc=1, device_id=device, device_id_type=MESH)
            return carry

        lax.fori_loop(1, group.count, greet, 0)
        total += group.count - 1
    across, deep, row = [
        Group(place, kind, gsend.at[i], grecv.at[i])
        for i, kind in enumerate(("depth", "depth", "row"))
    ]
    loads = [
        pltpu.make_async_copy(src, dst, local.at[i])
        for i, (src, dst) in enumerate(
            (
                (vol_in, vol), (cot_in, cot), (w1_in, w1),
                (w2_in, w2), (w3_in, w3), (w4_in, w4),
            )
        )
    ]
    for load in loads:
        load.start()
    stores = []

    def store(src, dst):
        copy = pltpu.make_async_copy(src, dst, local.at[len(loads) + len(stores)])
        copy.start()
        stores.append(copy)

    ix, iy, iz = place.at["x"], place.at["y"], place.at["z"]
    nx, ny = place.size["x"], place.size["y"]
    me = ix * ny + iy
    for x in range(nx + 4):
        pads = (0, ny + 1) if 2 <= x < nx + 2 else range(ny + 2)
        for y in pads:
            wide[x * (ny + 2) + y] = jnp.zeros((16, 512), BF)
    m1[27:32] = jnp.zeros((5, 8, 128), F32)
    m2[27:32] = jnp.zeros((5, 16, 128), BF)
    r, c = rows_cols((256, 256))
    perm = hot(((r & 31) == (c >> 3)) & ((r >> 5) == (c & 7)))
    back = hot(((c & 31) == (r >> 3)) & ((c >> 5) == (r & 7)))

    def fine_rows(dst, zz, rows):
        rows = dot(back, rows).astype(BF)
        dst[:, zz] = rows[:, :128].reshape(32, 8, 128)
        dst[:, zz + 4] = rows[:, 128:].reshape(32, 8, 128)


    def two(ref, zz):
        return jnp.concatenate(
            [ref[:, zz].reshape(256, 128), ref[:, zz + 4].reshape(256, 128)], axis=1
        )

    hv = Halo(place, v_pad, v_face, v_got, send.at[0], recv.at[0], 8, 8, 32, 128)
    hq = Halo(place, q_pad, q_face, q_got, send.at[1], recv.at[1], 4, 4, 32, 64)
    hh = Halo(place, h_pad, h_face, h_got, send.at[2], recv.at[2], 4, 4, 64, 64)
    hg = Halo(place, g_pad, g_face, g_got, send.at[3], recv.at[3], 8, 8, 32, 128)
    sum1 = Total(place, m1, l1, y1, f1, gsend.at[pl.ds(5, 3)], grecv.at[pl.ds(5, 3)])
    sum2 = Total(place, m2, l2, y2, f2, gsend.at[pl.ds(8, 3)], grecv.at[pl.ds(8, 3)])
    loads[0].wait()
    for zz in range(4):
        rows = dot(perm, two(vol, zz)).astype(BF)
        hv.put(zz, rows[:, :128])
        hv.put(zz + 4, rows[:, 128:])
    pl.semaphore_wait(barrier, total)
    hv.start()
    for load in loads[1:]:
        load.wait()

    for zz in range(4):
        cot1[zz] = dot(perm, two(cot, zz)).astype(BF)
    r, c = rows_cols((32, 32))
    eye = hot(r == c)
    toeplitz(t1, lambda kz, kx, ky: w1[kz * 9 + kx * 3 + ky], 8, 32, 32)
    flat1 = dot(eye, w1[...].reshape(864, 32), NT).astype(BF)
    r, c = rows_cols((64, 64))
    flat2 = dot(hot(r == c), w2[...].reshape(864, 64), NT).astype(BF)

    def back_tap(kz, kx, ky):
        return (2 - kz) * 9 + (2 - kx) * 3 + (2 - ky)

    def turned(kz, kx, ky):
        k = back_tap(kz, kx, ky)
        return flat1[:, k * 32 : (k + 1) * 32]

    def straight(kz, kx, ky):
        k = kz * 9 + kx * 3 + ky
        return flat2[:, k * 32 : (k + 1) * 32]

    toeplitz(t2, straight, 4, 64, 32)
    toeplitz(tt1, turned, 8, 32, 32)
    toeplitz(tt2, lambda *k: w2[back_tap(*k)], 4, 32, 64)
    cg = jnp.sum(cot[...].astype(F32), axis=(1, 2))
    cg = cg + roll(cg, -1)
    cg = cg + roll(cg, -2)
    cg = (cg + roll(cg, -4)).astype(BF)

    hv.arrive()
    fill_fine(hv, u1)
    for zz in range(4):
        pre = dot(t1[...], u1[zz : zz + 3].reshape(2880, 256))
        act, slope = silu_slope(pre)
        act1[zz] = act.astype(BF)
        sl1[zz] = slope
    r, c = rows_cols((512, 256))
    z2 = 2 * ((r >> 7) & 1) + (r >> 8)
    pick = hot(((c >> 6) == z2) & ((r & 127) == 2 * (c & 63)))
    pooled = []
    for a, b in ((0, 1), (2, 3)):
        s = act1[a].astype(F32) + act1[b].astype(F32)
        s = jnp.sum(s.reshape(4, 2, 32, 256), axis=1).reshape(128, 256)
        s = s + roll(s, -1)
        pooled.append((s * INV8).astype(BF))
    q1 = dot(jnp.concatenate(pooled, axis=1), pick).astype(BF)
    put_half(hq, q1)
    hq.start()

    hq.arrive()
    fill_half(hq, u2)
    pre2 = dot(t2[...], u2[...].reshape(1728, 256))
    act2, slope2 = silu_slope(pre2)
    s = jnp.sum(act2.astype(BF).astype(F32).reshape(4, 64, 256), axis=0)
    s = s[:, :128] + s[:, 128:]
    s = s + roll(s, 64)
    s = s + roll(s, -1)
    s = s + roll(s, -2)
    cin = (s * 0.125).astype(BF)
    zero = jnp.zeros((64, 128), BF)
    r, c = rows_cols((16, 128))
    own = dot(hot(c == 4 * r), jnp.concatenate([cin, zero], axis=0), NT)
    own += dot(hot(c == 8 * r), jnp.concatenate([zero, cg, zero[:32]], axis=0), NT)
    own = own.astype(BF)
    zbox[2] = own
    above = []
    for step in (-2, -1, 1, 2):
        copy = pltpu.make_async_remote_copy(
            src_ref=zbox.at[2],
            dst_ref=zbox.at[2 - step],
            send_sem=zsend.at[step + 2],
            recv_sem=zrecv.at[step + 2],
            device_id=place.device(step, 0, 0),
            device_id_type=MESH,
        )
        copy.start()
        above.append(copy)
    for copy in above:
        copy.wait_recv()
    zs = []
    for step in range(-2, 3):
        block = zbox[step + 2]
        if step:
            at = iz + step
            block = jnp.where((at >= 0) & (at < place.size["z"]), block, jnp.zeros_like(block))
        zs.append(block)
    zero = jnp.zeros((16, 64), BF)
    cin, cg = [z[:, :64] for z in zs], [z[:, 64:96] for z in zs]
    note[:, 0:256] = jnp.concatenate([*cin[1:4], cg[2], zero[:, :32]], axis=1)
    note[:, 256:512] = jnp.concatenate([cin[0], cin[4], cg[1], cg[3], zero], axis=1)
    mine = (ix + 2) * (ny + 2) + iy + 1

    def send_wide(lanes, kind, dx, dy):
        pltpu.make_async_remote_copy(
            src_ref=note.at[:, pl.ds(0, lanes)],
            dst_ref=wide.at[mine, :, pl.ds(0, lanes)],
            send_sem=zsend.at[kind],
            recv_sem=zrecv.at[kind],
            device_id=place.device(0, dx, dy),
            device_id_type=MESH,
        ).start()

    def all_wide(lanes, kind, count):
        ref = wide.at[pl.ds(0, count), :, pl.ds(0, lanes)]
        return pltpu.make_async_remote_copy(
            src_ref=ref,
            dst_ref=ref,
            send_sem=zsend.at[kind],
            recv_sem=zrecv.at[kind],
            device_id=place.device(0, 0, 1),
            device_id_type=MESH,
        )

    for dy, dx in itertools.product((-1, 1, 0), range(nx)):
        if (dy, dx) != (0, 0):
            send_wide(512, 5, dx, dy)
    far = (ny - 3) * nx
    wide[mine] = note[...]
    taps = list(itertools.product(range(3), range(3), range(3)))

    def w3_rows(kx, ky):
        return jnp.concatenate([w3[kz * 9 + kx * 3 + ky] for kz in range(3)], axis=0)

    near_all, far_all = all_wide(512, 5, 3 * nx - 1), all_wide(256, 7, far)
    near_all.wait_recv()

    def send_far(q, carry):
        send_wide(256, 7, lax.rem(q, nx), 2 + q // nx)
        return carry

    lax.fori_loop(0, far, send_far, 0)

    near, grads = [], []
    for j in range(5):
        slots = pl.ds((ix + j) * (ny + 2) + iy, 3)
        both = wide[slots].reshape(48, 512)
        one, two_ = both[:, :256], both[:, 256:]
        near += [two_[:, :64], one[:, :192], two_[:, 64:128]]
        grads.append([two_[8:40, 128:160], one[8:40, 192:224], two_[8:40, 160:192]])
    r, c = rows_cols((96, 48))
    near = dot(hot(c == (r & 31) + (r >> 5) + 7), jnp.concatenate(near, axis=1)).astype(BF)
    pre3 = 0.0
    for kx, ky in itertools.product(range(3), range(3)):
        rows = [
            near[32 * ky : 32 * ky + 32, 320 * (j + kx) + 64 * z :][:, :192]
            for z, j in itertools.product(range(3), range(3))
        ]
        pre3 = pre3 + dot(jnp.concatenate(rows, axis=0), w3_rows(kx, ky))
    act3, slope3 = silu_slope(pre3)
    act3 = act3[136:152].astype(BF)
    cgs = jnp.concatenate(
        [grads[j + 1][z] for z, j in itertools.product(range(3), range(3))], axis=0
    )
    cgt = own[:, 64:96]
    gp3 = (dot(cgs, w4[...]) * slope3).astype(BF)
    r, c = rows_cols((48, 32))
    near = jnp.concatenate([gp3[32 * i : 32 * i + 32] for i in range(9)], axis=1)
    near = dot(hot(c == (r & 15) + (r >> 4) + 7), near).astype(BF)

    def tap(kz, kx, ky):
        base = (kz * 3 + kx) * 256
        return near[16 * ky : 16 * (ky + 1), base : base + 256]

    gc = sum(
        dot(w3[kz * 9 + kx * 3 + ky], tap(2 - kz, 2 - kx, 2 - ky), NT)
        for kz, kx, ky in taps
    )
    r, c = rows_cols((16, 256))
    pick = hot(r == ((c & 63) >> 2))
    up = sum(dot(part, pick) for part in split(gc)) * 0.125
    gp2 = (jnp.concatenate([up] * 4, axis=0) * slope2).astype(BF)
    put_half(hh, gp2)
    hh.start()
    co = dot(w4[...], act3, NT).astype(BF)
    part4 = dot(cgt, act3, TN)
    for i in range(4):
        half, col = i % 2, 128 * (i // 2)
        m2[27 + i] = part4[16 * half : 16 * half + 16, col : col + 128].astype(BF)
    lane = rows_cols((16, 128))[1]
    for kz in range(3):
        g = dot(u2[3 * kz : 3 * kz + 3].reshape(576, 256), gp2, NT)
        for ky, kx in itertools.product(range(3), range(3)):
            cut = [
                g[ky * 192 + 32 * (x + kx) :][:32, 128 * (x // 2) : 128 * (x // 2) + 128]
                for x in range(4)
            ]
            even, odd = cut[0] + cut[2], cut[1] + cut[3]
            low = (even + roll(odd, 64))[:16]
            high = (roll(even, 64) + odd)[16:]
            m2[kz * 9 + kx * 3 + ky] = jnp.where(lane < 64, low, high).astype(BF)
    sum2.scatter()
    far_all.wait_recv()
    for x in range(nx + 2):
        start = (x + 1) * (ny + 2)
        rows = wide[start : start + ny + 2, :, 0:256].reshape(16 * (ny + 2), 256)
        for ky in range(3):
            near_y[ky, x] = rows[15 + ky : 15 + ky + 16 * ny]
    size = nx * 16 * ny
    pre = 0.0
    for kx, ky in itertools.product(range(3), range(3)):
        rows = near_y[ky, kx : kx + nx].reshape(size, 256)[:, :192]
        pre = pre + dot(rows, w3_rows(kx, ky))
    slope = silu_slope(pre)[1]
    cgs = near_y[1, 1 : nx + 1].reshape(size, 256)[:, 192:224]
    gp = (dot(cgs, w4[...]) * slope).astype(BF)
    k = lax.rem(me, 27)
    kz, kx, ky = k // 9, lax.rem(k // 3, 3), lax.rem(k, 3)
    rows = near_y[ky, pl.ds(kx, nx)].reshape(size, 256)
    tap_part[...] = dot(rows, gp, TN).reshape(4, 8, 8, 256)
    tap_sum[...] = tap_part[kz]
    across.start(lambda index: tap_sum.at[index], tap_line.at[iz])
    tap_line[iz] = tap_sum[iz]
    hh.arrive()
    across.arrive(some(tap_line, across.count - 1))
    s = jnp.sum(tap_line[...], axis=0) * scales[2]
    tap_all[ix, iy, iz] = jnp.concatenate([s[:, :128], s[:, 128:]], axis=0).astype(BF)
    own_tap = tap_all.at[ix, iy, iz]
    deep.start(lambda index: own_tap, own_tap)
    fill_half(hh, uh)
    gpool = dot(tt2[...], uh[...].reshape(3456, 256))
    r, c = rows_cols((256, 256))
    parts = split(gpool)
    for h in range(2):
        pick = hot(((r >> 6) == 2 * (c >> 7) + h) & ((r & 63) == ((c & 127) >> 1)))
        up = sum(dot(part, pick) for part in parts) * INV8
        up = jnp.concatenate(
            [up[32 * (x // 2) : 32 * (x // 2) + 32] for x in range(8)], axis=0
        )
        for zz in (2 * h, 2 * h + 1):
            gp1 = ((cot1[zz].astype(F32) + up) * sl1[zz]).astype(BF)
            hg.put(zz, gp1[:, :128])
            hg.put(zz + 4, gp1[:, 128:])
            g1[:, 256 * zz : 256 * zz + 256] = gp1
    for kz in range(3):
        uc = jnp.concatenate([u1[kz + zz] for zz in range(4)], axis=1)
        g = dot(g1[...], uc, NT)
        for ky in range(3):
            band = sum(
                g[32 * x : 32 * x + 32, ky * 320 + 32 * x : ky * 320 + 32 * x + 96]
                for x in range(8)
            )
            for kx in range(3):
                m1[kz * 9 + kx * 3 + ky] = jnp.concatenate(
                    [band[8 * i : 8 * i + 8, 32 * kx : 32 * kx + 32] for i in range(4)],
                    axis=1,
                )
    sum1.scatter()
    hg.start()
    r, c = rows_cols((16, 128))
    co = dot(co, hot(r == (c >> 3)))
    co = jnp.concatenate([jnp.concatenate([co] * 8, axis=0)] * 2, axis=1)
    for zz in range(4):
        fine_rows(out_v, zz, (act1[zz].astype(F32) + co).astype(BF))
    store(out_v, out)
    deep_all = some(tap_all.at[ix, iy], deep.count - 1)
    deep.arrive(deep_all)
    own_depth = tap_all.at[ix, iy]
    row.start(lambda index: own_depth, own_depth)
    sum2.cross()
    sum1.cross()
    row_all = tap_all.at[pl.ds(0, nx - 1), iy]
    row.arrive(row_all)
    other = iy + 1 - 2 * lax.rem(iy, 2)

    def range_copy(y, target, lane):
        block = tap_all.at[pl.ds(0, nx), y]
        return pltpu.make_async_remote_copy(
            src_ref=block,
            dst_ref=block,
            send_sem=csend.at[lane],
            recv_sem=crecv.at[lane],
            device_id=(ix, target, iz),
            device_id_type=MESH,
        )

    hops = range(1, ny // 2)
    ranges = [range_copy(iy, lax.rem(iy + 2 * s, ny), s) for s in hops]
    for copy in ranges:
        copy.start()
    passed = [range_copy(iy, other, ny // 2)]
    passed[0].start()
    hg.arrive()
    fill_fine(hg, ug)
    sum2.gather(scales[1])
    sum1.gather(scales[0])
    for zz in range(4):
        rows = dot(tt1[...], ug[zz : zz + 3].reshape(2880, 256))
        fine_rows(gvol_v, zz, rows.astype(BF))
    store(gvol_v, gvol)
    for s, copy in zip(hops, ranges):
        copy.wait_recv()
        passed.append(range_copy(lax.rem(iy + ny - 2 * s, ny), other, ny // 2 + s))
        passed[-1].start()
    sum2.arrive()
    store(f2, d2)
    sum1.arrive()
    store(f1, d1)
    for copy in passed:
        copy.wait_recv()
    store(tap_all, d3)
    for copy in ranges + passed:
        copy.wait_send()
    for halo in (hv, hq, hh, hg):
        halo.finish()
    for copy in above:
        copy.wait_send()
    near_all.wait_send()
    far_all.wait_send()
    across.finish(some(tap_line, across.count - 1))
    deep.finish(deep_all)
    row.finish(row_all)
    sum1.finish()
    sum2.finish()
    for copy in stores:
        copy.wait()


def last_kernel(
    scale, out_in, gvol_in, f1_in, f2_in, tap_in,
    out, gvol, d1, d2, d3, d4,
    f1, f2, tap_all, out_v, gvol_v, v1, v2, v3, sems,
):
    copies = []

    def copy(src, dst):
        one = pltpu.make_async_copy(src, dst, sems.at[len(copies)])
        one.start()
        copies.append(one)
        return one

    loads = [
        copy(tap_in, tap_all), copy(f2_in, f2), copy(f1_in, f1),
        copy(out_in, out_v), copy(gvol_in, gvol_v),
    ]
    loads[0].wait()
    for k in range(27):
        for j in range(8):
            block = tap_all[k // 8, k % 8, j].astype(F32)
            v3[k, 8 * j : 8 * j + 8, :] = jnp.concatenate([block[:8], block[8:]], axis=1)
        if k % 9 == 8:
            copy(v3.at[pl.ds(k - 8, 9)], d3.at[pl.ds(k - 8, 9)])
        if k == 8:
            for load in loads[3:]:
                load.wait()
            copy(out_v, out)
            copy(gvol_v, gvol)
    loads[1].wait()
    for k in range(27):
        wide = f2[k].astype(F32)
        v2[k] = jnp.concatenate([wide[:, :64], wide[:, 64:]], axis=0)
    copy(v2, d2)
    loads[2].wait()
    for k in range(27):
        wide = f1[k]
        v1[k] = jnp.concatenate([wide[:, 32 * i : 32 * i + 32] for i in range(4)], axis=0)
    copy(v1, d1)
    for i in range(4):
        half, col = i % 2, 128 * (i // 2)
        d4[16 * half : 16 * half + 16, col : col + 128] = f2[27 + i].astype(F32) * scale
    for one in copies[5:]:
        one.wait()


def halo_scratch(nz, nx, ch):
    return [
        pltpu.VMEM((nz + 2, (nx + 2) * ch, 128), BF),
        pltpu.VMEM((2, 16, nx * ch), BF),
        pltpu.VMEM((3, 2, 3, 16, nx * ch), BF),
    ]


def body(sizes, cells, vol, cot, w1, w2, w3, w4):
    shape = jax.ShapeDtypeStruct
    field = shape((32, 8, 8, 128), BF)
    vmem = pl.BlockSpec(memory_space=pltpu.VMEM)
    nx, ny, nz = sizes
    coarse = 1.0 / math.sqrt(cells / 512.0)
    scales = (1.0 / math.sqrt(cells * 1.0), 1.0 / math.sqrt(cells / 8.0), coarse)
    total = lambda r: [
        pltpu.VMEM((32, r, 128), F32 if r == 8 else BF),
        pltpu.VMEM((32, r, 128), F32 if r == 8 else BF),
        pltpu.VMEM((nz, r, 128), F32),
        pltpu.VMEM((32, r, 128), F32 if r == 8 else BF),
    ]
    anywhere = pl.BlockSpec(memory_space=pl.ANY)
    mid = pl.pallas_call(
        functools.partial(kernel, sizes, scales),
        out_shape=[
            field,
            field,
            shape((32, 8, 128), F32),
            shape((32, 16, 128), BF),
            shape((nx, ny, 8, 16, 128), BF),
        ],
        in_specs=[anywhere] * 6,
        out_specs=[anywhere] * 5,
        scratch_shapes=[
            *halo_scratch(8, 8, 32),
            *halo_scratch(4, 4, 32),
            *halo_scratch(4, 4, 64),
            *halo_scratch(8, 8, 32),
            pltpu.VMEM((6, 960, 256), BF),
            pltpu.VMEM((6, 960, 256), BF),
            pltpu.VMEM((9, 192, 256), BF),
            pltpu.VMEM((9, 384, 256), BF),
            pltpu.VMEM((256, 2880), BF),
            pltpu.VMEM((256, 2880), BF),
            pltpu.VMEM((256, 1728), BF),
            pltpu.VMEM((128, 3456), BF),
            pltpu.VMEM((4, 256, 256), F32),
            pltpu.VMEM((4, 256, 256), BF),
            pltpu.VMEM((4, 256, 256), BF),
            pltpu.VMEM((256, 1024), BF),
            pltpu.SemaphoreType.DMA((4, 26)),
            pltpu.SemaphoreType.DMA((4, 26)),
            pltpu.VMEM((5, 16, 128), BF),
            pltpu.VMEM((16, 512), BF),
            pltpu.VMEM(((nx + 4) * (ny + 2), 16, 512), BF),
            pltpu.VMEM((3, nx + 2, 16 * ny, 256), BF),
            pltpu.VMEM((4, 8, 8, 256), F32),
            pltpu.VMEM((8, 8, 256), F32),
            pltpu.VMEM((nz, 8, 256), F32),
            pltpu.VMEM((nx, ny, 8, 16, 128), BF),
            *total(8),
            *total(16),
            pltpu.SemaphoreType.DMA((11,)),
            pltpu.SemaphoreType.DMA((11,)),
            pltpu.VMEM((32, 8, 8, 128), BF),
            pltpu.VMEM((32, 8, 8, 128), BF),
            pltpu.VMEM((27, 32, 32), BF),
            pltpu.VMEM((27, 32, 64), BF),
            pltpu.VMEM((27, 64, 256), BF),
            pltpu.VMEM((32, 256), BF),
            pltpu.VMEM((32, 8, 8, 128), BF),
            pltpu.VMEM((32, 8, 8, 128), BF),
            pltpu.SemaphoreType.DMA((11,)),
            pltpu.SemaphoreType.DMA((8,)),
            pltpu.SemaphoreType.DMA((8,)),
            pltpu.SemaphoreType.DMA((ny,)),
            pltpu.SemaphoreType.DMA((ny,)),
        ],
        compiler_params=pltpu.CompilerParams(
            collective_id=0, has_side_effects=True, vmem_limit_bytes=60 * 1024 * 1024
        ),
        name="unet",
    )(vol, cot, w1, jnp.swapaxes(w2, 1, 2), jnp.swapaxes(w3, 1, 2), w4)
    finals = [
        field,
        field,
        shape((27, 32, 32), F32),
        shape((27, 32, 64), F32),
        shape((27, 64, 256), F32),
        shape((32, 256), F32),
    ]
    out, gvol, d1, d2, d3, d4 = pl.pallas_call(
        functools.partial(last_kernel, scales[2] / scales[1]),
        out_shape=finals,
        in_specs=[anywhere] * 5,
        out_specs=[anywhere] * 5 + [vmem],
        scratch_shapes=[pltpu.VMEM(f.shape, f.dtype) for f in list(mid[2:]) + finals[:5]]
        + [pltpu.SemaphoreType.DMA((12,))],
        compiler_params=pltpu.CompilerParams(vmem_limit_bytes=60 * 1024 * 1024),
        name="finish",
    )(*mid)
    return out, gvol, d1, jnp.swapaxes(d2, 1, 2), jnp.swapaxes(d3, 1, 2), d4


def solution(mesh):
    sizes = (mesh.shape["gx"], mesh.shape["gy"], mesh.shape["gz"])
    cells = 8 * 8 * 128 * sizes[0] * sizes[1] * sizes[2]
    field = P(None, "gz", "gx", "gy")
    return jax.shard_map(
        functools.partial(body, sizes, cells),
        mesh=mesh,
        in_specs=(field, field, P(), P(), P(), P()),
        out_specs=(field, field, P(), P(), P(), P()),
        check_vma=False,
    )
```

```python
import functools
import itertools
import math

import jax
import jax.numpy as jnp
from jax import lax
from jax.experimental import pallas as pl
from jax.experimental.pallas import tpu as pltpu
from jax.sharding import PartitionSpec as P

MESH = pl.DeviceIdType.MESH
BF = jnp.bfloat16
F32 = jnp.float32
INV8 = 1.0 / math.sqrt(8.0)
STEPS = sorted(
    (d for d in itertools.product((-1, 0, 1), repeat=3) if d != (0, 0, 0)),
    key=lambda d: -sum(map(abs, d)),
)

NN = ((1,), (0,))
NT = ((1,), (1,))
TN = ((0,), (0,))


def dot(a, b, dims=NN):
    return lax.dot_general(a, b, (dims, ((), ())), preferred_element_type=F32)


def rows_cols(shape):
    return (
        lax.broadcasted_iota(jnp.int32, shape, 0),
        lax.broadcasted_iota(jnp.int32, shape, 1),
    )


def hot(cond):
    return jnp.where(cond, 1.0, 0.0).astype(BF)


def roll(a, shift):
    return pltpu.roll(a, shift % a.shape[1], 1)


def silu_slope(pre):
    sig = 0.5 * (1.0 + jnp.tanh(0.5 * pre))
    act = pre * sig
    return act, sig + act * (1.0 - sig)


def split(a):
    high = a.astype(BF)
    return high, (a - high.astype(F32)).astype(BF)


class Place:
    def __init__(self, sizes):
        self.size = dict(zip(("x", "y", "z"), sizes))
        self.at = {
            "x": lax.axis_index("gx"),
            "y": lax.axis_index("gy"),
            "z": lax.axis_index("gz"),
        }

    def near(self, axis, step):
        size = self.size[axis]
        return lax.rem(self.at[axis] + (step + size), size)

    def device(self, dz, dx, dy):
        return (self.near("x", dx), self.near("y", dy), self.near("z", dz))

    def inside(self, axis, step):
        if step == 0:
            return None
        if step < 0:
            return self.at[axis] > 0
        return self.at[axis] < self.size[axis] - 1


class Halo:
    def __init__(self, place, pad, face, got, send, recv, nz, nx, ch, ylen):
        self.place, self.pad, self.face, self.got = place, pad, face, got
        self.send, self.recv = send, recv
        self.nz, self.nx, self.ch, self.ylen = nz, nx, ch, ylen

    def put(self, z, value):
        self.pad[z + 1, self.ch : self.ch * (self.nx + 1), :] = value

    def start(self):
        nz, nx, ch = self.nz, self.nx, self.ch
        r, c = rows_cols((32, nz * 128))
        edge = jnp.where(r >= 16, self.ylen - 1, 0)
        pick = hot(((r & 15) == (c >> 7)) & ((c & 127) == edge))
        own = jnp.concatenate(
            [self.pad[z + 1, ch : ch * (nx + 1), :] for z in range(nz)], axis=1
        )
        both = dot(pick, own, NT).astype(BF)
        self.face[0] = both[:16]
        self.face[1] = both[16:]
        self.copies = []
        for i, (dz, dx, dy) in enumerate(STEPS):
            if dy == 0:
                zs = {-1: (1, 1), 0: (1, nz), 1: (nz, 1)}[dz]
                xs = {-1: (ch, ch), 0: (ch, nx * ch), 1: (nx * ch, ch)}[dx]
                zd = {-1: nz + 1, 0: 1, 1: 0}[dz]
                xd = {-1: (nx + 1) * ch, 0: ch, 1: 0}[dx]
                src = self.pad.at[pl.ds(zs[0], zs[1]), pl.ds(xs[0], xs[1])]
                dst = self.pad.at[pl.ds(zd, zs[1]), pl.ds(xd, xs[1])]
            else:
                side = 0 if dy == 1 else 1
                src = self.face.at[1 - side]
                dst = self.got.at[1 - dx, side, 1 - dz]
            copy = pltpu.make_async_remote_copy(
                src_ref=src,
                dst_ref=dst,
                send_sem=self.send.at[i],
                recv_sem=self.recv.at[i],
                device_id=self.place.device(dz, dx, dy),
                device_id_type=MESH,
            )
            copy.start()
            self.copies.append(copy)

    def arrive(self):
        for copy in self.copies:
            copy.wait_recv()
        nz, nx, ch = self.nz, self.nx, self.ch
        at, size = self.place.at, self.place.size
        plane = jnp.zeros(self.pad.shape[1:], BF)
        column = jnp.zeros((nz + 2, ch, 128), BF)

        @pl.when(at["z"] == 0)
        def _():
            self.pad[0] = plane

        @pl.when(at["z"] == size["z"] - 1)
        def _():
            self.pad[nz + 1] = plane

        @pl.when(at["x"] == 0)
        def _():
            self.pad[:, 0:ch, :] = column

        @pl.when(at["x"] == size["x"] - 1)
        def _():
            self.pad[:, (nx + 1) * ch :, :] = column

    def columns(self):
        nz, nx, ch = self.nz, self.nx, self.ch
        at, size = self.place.at, self.place.size
        r, c = rows_cols((96, 128))
        group, z = r >> 4, r & 15
        side = jnp.where(group >= 3, 1, 0)
        dz = group - 3 * side
        zp = c & 15
        first, last = (
            jnp.where(at["z"] > 0, 0, -1),
            jnp.where(at["z"] < size["z"] - 1, nz + 1, -1),
        )
        low, high = (
            jnp.where(at["y"] > 0, 0, -1),
            jnp.where(at["y"] < size["y"] - 1, 1, -1),
        )
        mid = (dz == 1) & (z < nz) & (zp == z + 1)
        below = (dz == 0) & (z == nz - 1) & (zp == first)
        above = (dz == 2) & (z == 0) & (zp == last)
        lane = (side == (c >> 4)) & ((side == low) | (side == high))
        pick = hot((mid | below | above) & lane)
        parts = []
        for dx in range(3):
            wide = slice(0, nx * ch)
            if dx == 0:
                wide = slice((nx - 1) * ch, nx * ch)
            if dx == 2:
                wide = slice(0, ch)
            src = self.got[dx].reshape(96, nx * ch)[:, wide]
            part = dot(src, pick, TN)
            if dx != 1:
                part = jnp.where(self.place.inside("x", dx - 1), part, 0.0)
            parts.append(part.astype(BF))
        return jnp.concatenate(parts, axis=0)

    def shifted(self):
        cols = self.columns()
        lane = rows_cols(cols.shape)[1]
        for zp in range(self.nz + 2):
            base = self.pad[zp]
            low = jnp.where(lane == 0, roll(cols, -zp), roll(base, 1))
            end = self.ylen - 1
            high = jnp.where(lane == end, roll(cols, end - 16 - zp), roll(base, -1))
            yield zp, (low, base, high)

    def finish(self):
        for copy in self.copies:
            copy.wait_send()


def fill_fine(halo, u):
    rows = (halo.nx + 2) * halo.ch
    for zp, parts in halo.shifted():
        for ky, part in enumerate(parts):
            if zp <= 5:
                u[zp, ky * rows : (ky + 1) * rows, 0:128] = part
            if zp >= 4:
                u[zp - 4, ky * rows : (ky + 1) * rows, 128:256] = part


def fill_half(halo, u):
    before = None
    for zp, parts in halo.shifted():
        if before is not None:
            j = zp - 1
            for ky in range(3):
                lane = rows_cols(parts[ky].shape)[1]
                both = jnp.where(lane < 64, before[ky], roll(parts[ky], 64))
                if j <= 2:
                    u[j * 3 + ky, :, 0:128] = both
                if j >= 2:
                    u[(j - 2) * 3 + ky, :, 128:256] = both
        before = parts


def put_half(halo, value):
    lane = rows_cols((value.shape[0], 128))[1]
    for z in range(4):
        half = value[:, 128 * (z // 2) : 128 * (z // 2) + 128]
        if z % 2:
            half = roll(half, 64)
        halo.put(z, jnp.where(lane < 64, half, jnp.zeros_like(half)))


def toeplitz(dst, blocks, nx, rows, width):
    dst[...] = jnp.zeros(dst.shape, BF)
    for kz, ky in itertools.product(range(3), range(3)):
        band = jnp.concatenate([blocks(kz, kx, ky) for kx in range(3)], axis=1)
        base = (kz * 3 + ky) * (nx + 2) * width
        for x in range(nx):
            dst[rows * x : rows * (x + 1), base + width * x : base + width * (x + 3)] = band


class Group:
    def __init__(self, place, kind, send, recv):
        self.place, self.kind, self.send, self.recv = place, kind, send, recv
        size = place.size
        self.count = {
            "sheet": size["x"] * size["y"],
            "row": size["x"],
            "depth": size["z"],
        }[kind]

    def member(self, q):
        at, size = self.place.at, self.place.size
        if self.kind == "sheet":
            x = lax.rem(at["x"] + q // size["y"], size["x"])
            y = lax.rem(at["y"] + lax.rem(q, size["y"]), size["y"])
            return (x, y, at["z"]), x * size["y"] + y
        if self.kind == "depth":
            z = lax.rem(at["z"] + q, size["z"])
            return (at["x"], at["y"], z), z
        x = lax.rem(at["x"] + q, size["x"])
        return (x, at["y"], at["z"]), x

    def start(self, src, dst):
        def one(q, carry):
            device, index = self.member(q)
            pltpu.make_async_remote_copy(
                src_ref=src(index),
                dst_ref=dst,
                send_sem=self.send,
                recv_sem=self.recv,
                device_id=device,
                device_id_type=MESH,
            ).start()
            return carry

        lax.fori_loop(1, self.count, one, 0)

    def _all(self, ref):
        return pltpu.make_async_remote_copy(
            src_ref=ref,
            dst_ref=ref,
            send_sem=self.send,
            recv_sem=self.recv,
            device_id=self.member(1)[0],
            device_id_type=MESH,
        )

    def arrive(self, ref):
        self._all(ref).wait_recv()

    def finish(self, ref):
        self._all(ref).wait_send()


def some(ref, count):
    return ref.at[pl.ds(0, count)]


class Total:
    def __init__(self, place, mine, landed, line, done, send, recv):
        self.mine, self.landed, self.line, self.done = mine, landed, line, done
        self.at = place.at
        self.me = place.at["x"] * place.size["y"] + place.at["y"]
        self.one = Group(place, "sheet", send.at[0], recv.at[0])
        self.two = Group(place, "depth", send.at[1], recv.at[1])
        self.three = Group(place, "sheet", send.at[2], recv.at[2])

    def scatter(self):
        self.one.start(lambda index: self.mine.at[index], self.landed.at[self.me])
        self.landed[self.me] = self.mine[self.me]

    def cross(self):
        self.one.arrive(some(self.landed, self.one.count - 1))
        self.line[self.at["z"]] = jnp.sum(self.landed[...], axis=0)
        own = self.line.at[self.at["z"]]
        self.two.start(lambda index: own, own)

    def gather(self, scale):
        self.two.arrive(some(self.line, self.two.count - 1))
        total = jnp.sum(self.line[...], axis=0) * scale
        self.done[self.me] = total.astype(self.done.dtype)
        own = self.done.at[self.me]
        self.three.start(lambda index: own, own)

    def arrive(self):
        self.three.arrive(some(self.done, self.one.count - 1))

    def finish(self):
        self.one.finish(some(self.landed, self.one.count - 1))
        self.two.finish(some(self.line, self.two.count - 1))
        self.three.finish(some(self.done, self.one.count - 1))


def kernel(
    sizes, scales, vol_in, cot_in, w1_in, w2_in, w3_in, w4_in,
    out, gvol, d1, d2, d3,
    v_pad, v_face, v_got, q_pad, q_face, q_got,
    h_pad, h_face, h_got, g_pad, g_face, g_got,
    u1, ug, u2, uh, t1, tt1, t2, tt2,
    sl1, act1, cot1, g1, send, recv,
    zbox, note, wide1, wide2, near_y, tap_part, tap_sum, tap_line, tap_all,
    m1, l1, y1, f1, m2, l2, y2, f2, gsend, grecv,
    vol, cot, w1, w2, w3, w4, out_v, gvol_v, local, zsend, zrecv, csend, crecv,
):
    place = Place(sizes)
    barrier = pltpu.get_barrier_semaphore()
    partners = [place.device(*s) for s in STEPS if s[0] != 0 and s[1:] != (0, 0)]
    for device in partners:
        pl.semaphore_signal(barrier, inc=1, device_id=device, device_id_type=MESH)
    total = len(partners)
    for kind in ("sheet", "depth"):
        group = Group(place, kind, None, None)

        def greet(q, carry, group=group):
            device = group.member(q)[0]
            pl.semaphore_signal(barrier, inc=1, device_id=device, device_id_type=MESH)
            return carry

        lax.fori_loop(1, group.count, greet, 0)
        total += group.count - 1
    across, deep, row = [
        Group(place, kind, gsend.at[i], grecv.at[i])
        for i, kind in enumerate(("depth", "depth", "row"))
    ]
    loads = [
        pltpu.make_async_copy(src, dst, local.at[i])
        for i, (src, dst) in enumerate(
            (
                (vol_in, vol), (cot_in, cot), (w1_in, w1),
                (w2_in, w2), (w3_in, w3), (w4_in, w4),
            )
        )
    ]
    for load in loads:
        load.start()
    stores = []

    def store(src, dst):
        copy = pltpu.make_async_copy(src, dst, local.at[len(loads) + len(stores)])
        copy.start()
        stores.append(copy)

    ix, iy, iz = place.at["x"], place.at["y"], place.at["z"]
    nx, ny = place.size["x"], place.size["y"]
    me = ix * ny + iy
    for wide in (wide1, wide2):
        for x in range(nx + 4):
            pads = (0, ny + 1) if 2 <= x < nx + 2 else range(ny + 2)
            for y in pads:
                wide[x * (ny + 2) + y] = jnp.zeros((16, 256), BF)
    m1[27:32] = jnp.zeros((5, 8, 128), F32)
    m2[27:32] = jnp.zeros((5, 16, 128), F32)
    r, c = rows_cols((256, 256))
    perm = hot(((r & 31) == (c >> 3)) & ((r >> 5) == (c & 7)))
    back = hot(((c & 31) == (r >> 3)) & ((c >> 5) == (r & 7)))

    def fine_rows(dst, zz, rows):
        rows = dot(back, rows).astype(BF)
        dst[:, zz] = rows[:, :128].reshape(32, 8, 128)
        dst[:, zz + 4] = rows[:, 128:].reshape(32, 8, 128)


    def two(ref, zz):
        return jnp.concatenate(
            [ref[:, zz].reshape(256, 128), ref[:, zz + 4].reshape(256, 128)], axis=1
        )

    hv = Halo(place, v_pad, v_face, v_got, send.at[0], recv.at[0], 8, 8, 32, 128)
    hq = Halo(place, q_pad, q_face, q_got, send.at[1], recv.at[1], 4, 4, 32, 64)
    hh = Halo(place, h_pad, h_face, h_got, send.at[2], recv.at[2], 4, 4, 64, 64)
    hg = Halo(place, g_pad, g_face, g_got, send.at[3], recv.at[3], 8, 8, 32, 128)
    sum1 = Total(place, m1, l1, y1, f1, gsend.at[pl.ds(5, 3)], grecv.at[pl.ds(5, 3)])
    sum2 = Total(place, m2, l2, y2, f2, gsend.at[pl.ds(8, 3)], grecv.at[pl.ds(8, 3)])
    loads[0].wait()
    for zz in range(4):
        rows = dot(perm, two(vol, zz)).astype(BF)
        hv.put(zz, rows[:, :128])
        hv.put(zz + 4, rows[:, 128:])
    pl.semaphore_wait(barrier, total)
    hv.start()
    for load in loads[1:]:
        load.wait()

    for zz in range(4):
        cot1[zz] = dot(perm, two(cot, zz)).astype(BF)
    r, c = rows_cols((32, 32))
    eye = hot(r == c)
    toeplitz(t1, lambda kz, kx, ky: w1[kz * 9 + kx * 3 + ky], 8, 32, 32)
    flat1 = dot(eye, w1[...].reshape(864, 32), NT).astype(BF)
    r, c = rows_cols((64, 64))
    flat2 = dot(hot(r == c), w2[...].reshape(864, 64), NT).astype(BF)

    def back_tap(kz, kx, ky):
        return (2 - kz) * 9 + (2 - kx) * 3 + (2 - ky)

    def turned(kz, kx, ky):
        k = back_tap(kz, kx, ky)
        return flat1[:, k * 32 : (k + 1) * 32]

    def straight(kz, kx, ky):
        k = kz * 9 + kx * 3 + ky
        return flat2[:, k * 32 : (k + 1) * 32]

    toeplitz(t2, straight, 4, 64, 32)
    toeplitz(tt1, turned, 8, 32, 32)
    toeplitz(tt2, lambda *k: w2[back_tap(*k)], 4, 32, 64)
    cg = jnp.sum(cot[...].astype(F32), axis=(1, 2))
    cg = cg + roll(cg, -1)
    cg = cg + roll(cg, -2)
    cg = (cg + roll(cg, -4)).astype(BF)

    hv.arrive()
    fill_fine(hv, u1)
    for zz in range(4):
        pre = dot(t1[...], u1[zz : zz + 3].reshape(2880, 256))
        act, slope = silu_slope(pre)
        act1[zz] = act.astype(BF)
        sl1[zz] = slope
    r, c = rows_cols((512, 256))
    z2 = 2 * ((r >> 7) & 1) + (r >> 8)
    pick = hot(((c >> 6) == z2) & ((r & 127) == 2 * (c & 63)))
    pooled = []
    for a, b in ((0, 1), (2, 3)):
        s = act1[a].astype(F32) + act1[b].astype(F32)
        s = jnp.sum(s.reshape(4, 2, 32, 256), axis=1).reshape(128, 256)
        s = s + roll(s, -1)
        pooled.append((s * INV8).astype(BF))
    q1 = dot(jnp.concatenate(pooled, axis=1), pick).astype(BF)
    put_half(hq, q1)
    hq.start()

    hq.arrive()
    fill_half(hq, u2)
    pre2 = dot(t2[...], u2[...].reshape(1728, 256))
    act2, slope2 = silu_slope(pre2)
    s = jnp.sum(act2.astype(BF).astype(F32).reshape(4, 64, 256), axis=0)
    s = s[:, :128] + s[:, 128:]
    s = s + roll(s, 64)
    s = s + roll(s, -1)
    s = s + roll(s, -2)
    cin = (s * 0.125).astype(BF)
    zero = jnp.zeros((64, 128), BF)
    r, c = rows_cols((16, 128))
    own = dot(hot(c == 4 * r), jnp.concatenate([cin, zero], axis=0), NT)
    own += dot(hot(c == 8 * r), jnp.concatenate([zero, cg, zero[:32]], axis=0), NT)
    own = own.astype(BF)
    zbox[2] = own
    above = []
    for step in (-2, -1, 1, 2):
        copy = pltpu.make_async_remote_copy(
            src_ref=zbox.at[2],
            dst_ref=zbox.at[2 - step],
            send_sem=zsend.at[step + 2],
            recv_sem=zrecv.at[step + 2],
            device_id=place.device(step, 0, 0),
            device_id_type=MESH,
        )
        copy.start()
        above.append(copy)
    for copy in above:
        copy.wait_recv()
    zs = []
    for step in range(-2, 3):
        block = zbox[step + 2]
        if step:
            at = iz + step
            block = jnp.where((at >= 0) & (at < place.size["z"]), block, jnp.zeros_like(block))
        zs.append(block)
    zero = jnp.zeros((16, 64), BF)
    cin, cg = [z[:, :64] for z in zs], [z[:, 64:96] for z in zs]
    note[0] = jnp.concatenate([cin[1], cin[2], cin[3], cg[2], zero[:, :32]], axis=1)
    note[1] = jnp.concatenate([cin[0], cin[4], cg[1], cg[3], zero], axis=1)
    mine = (ix + 2) * (ny + 2) + iy + 1

    def send_wide(which, dst, kind, dx, dy):
        pltpu.make_async_remote_copy(
            src_ref=note.at[which],
            dst_ref=dst.at[mine],
            send_sem=zsend.at[kind],
            recv_sem=zrecv.at[kind],
            device_id=place.device(0, dx, dy),
            device_id_type=MESH,
        ).start()

    def all_wide(dst, kind, count):
        ref = some(dst, count)
        return pltpu.make_async_remote_copy(
            src_ref=ref,
            dst_ref=ref,
            send_sem=zsend.at[kind],
            recv_sem=zrecv.at[kind],
            device_id=place.device(0, 0, 1),
            device_id_type=MESH,
        )

    for dy, dx in itertools.product((-1, 1, 0), range(nx)):
        if (dy, dx) != (0, 0):
            send_wide(0, wide1, 5, dx, dy)
            send_wide(1, wide2, 6, dx, dy)

    far = (ny - 3) * nx
    wide1[mine] = note[0]
    wide2[mine] = note[1]
    taps = list(itertools.product(range(3), range(3), range(3)))

    def w3_rows(kx, ky):
        return jnp.concatenate([w3[kz * 9 + kx * 3 + ky] for kz in range(3)], axis=0)

    all_wide(wide1, 5, 3 * nx - 1).wait_recv()
    all_wide(wide2, 6, 3 * nx - 1).wait_recv()

    def send_far(q, carry):
        send_wide(0, wide1, 7, lax.rem(q, nx), 2 + q // nx)
        return carry

    lax.fori_loop(0, far, send_far, 0)

    near, grads = [], []
    for j in range(5):
        slots = pl.ds((ix + j) * (ny + 2) + iy, 3)
        one, two_ = wide1[slots].reshape(48, 256), wide2[slots].reshape(48, 256)
        near += [two_[:, :64], one[:, :192], two_[:, 64:128]]
        grads.append([two_[8:40, 128:160], one[8:40, 192:224], two_[8:40, 160:192]])
    r, c = rows_cols((96, 48))
    near = dot(hot(c == (r & 31) + (r >> 5) + 7), jnp.concatenate(near, axis=1)).astype(BF)
    pre3 = 0.0
    for kx, ky in itertools.product(range(3), range(3)):
        rows = [
            near[32 * ky : 32 * ky + 32, 320 * (j + kx) + 64 * z :][:, :192]
            for z, j in itertools.product(range(3), range(3))
        ]
        pre3 = pre3 + dot(jnp.concatenate(rows, axis=0), w3_rows(kx, ky))
    act3, slope3 = silu_slope(pre3)
    act3 = act3[136:152].astype(BF)
    cgs = jnp.concatenate(
        [grads[j + 1][z] for z, j in itertools.product(range(3), range(3))], axis=0
    )
    cgt = own[:, 64:96]
    gp3 = (dot(cgs, w4[...]) * slope3).astype(BF)
    r, c = rows_cols((48, 32))
    near = jnp.concatenate([gp3[32 * i : 32 * i + 32] for i in range(9)], axis=1)
    near = dot(hot(c == (r & 15) + (r >> 4) + 7), near).astype(BF)

    def tap(kz, kx, ky):
        base = (kz * 3 + kx) * 256
        return near[16 * ky : 16 * (ky + 1), base : base + 256]

    gc = sum(
        dot(w3[kz * 9 + kx * 3 + ky], tap(2 - kz, 2 - kx, 2 - ky), NT)
        for kz, kx, ky in taps
    )
    r, c = rows_cols((16, 256))
    pick = hot(r == ((c & 63) >> 2))
    up = sum(dot(part, pick) for part in split(gc)) * 0.125
    gp2 = (jnp.concatenate([up] * 4, axis=0) * slope2).astype(BF)
    put_half(hh, gp2)
    hh.start()
    co = dot(w4[...], act3, NT).astype(BF)
    part4 = dot(cgt, act3, TN)
    for i in range(4):
        half, col = i % 2, 128 * (i // 2)
        m2[27 + i] = part4[16 * half : 16 * half + 16, col : col + 128]
    lane = rows_cols((16, 128))[1]
    for kz in range(3):
        g = dot(u2[3 * kz : 3 * kz + 3].reshape(576, 256), gp2, NT)
        for ky, kx in itertools.product(range(3), range(3)):
            cut = [
                g[ky * 192 + 32 * (x + kx) :][:32, 128 * (x // 2) : 128 * (x // 2) + 128]
                for x in range(4)
            ]
            even, odd = cut[0] + cut[2], cut[1] + cut[3]
            low = (even + roll(odd, 64))[:16]
            high = (roll(even, 64) + odd)[16:]
            m2[kz * 9 + kx * 3 + ky] = jnp.where(lane < 64, low, high)
    r, c = rows_cols((16, 128))
    co = dot(co, hot(r == (c >> 3)))
    co = jnp.concatenate([jnp.concatenate([co] * 8, axis=0)] * 2, axis=1)
    for zz in range(4):
        fine_rows(out_v, zz, (act1[zz].astype(F32) + co).astype(BF))
    store(out_v, out)
    all_wide(wide1, 7, far).wait_recv()
    for x in range(nx + 2):
        start = (x + 1) * (ny + 2)
        rows = wide1[start : start + ny + 2].reshape(16 * (ny + 2), 256)
        for ky in range(3):
            near_y[ky, x] = rows[15 + ky : 15 + ky + 16 * ny]
    size = nx * 16 * ny
    pre = 0.0
    for kx, ky in itertools.product(range(3), range(3)):
        rows = near_y[ky, kx : kx + nx].reshape(size, 256)[:, :192]
        pre = pre + dot(rows, w3_rows(kx, ky))
    slope = silu_slope(pre)[1]
    cgs = near_y[1, 1 : nx + 1].reshape(size, 256)[:, 192:224]
    gp = (dot(cgs, w4[...]) * slope).astype(BF)
    k = lax.rem(me, 27)
    kz, kx, ky = k // 9, lax.rem(k // 3, 3), lax.rem(k, 3)
    rows = near_y[ky, pl.ds(kx, nx)].reshape(size, 256)
    tap_part[...] = dot(rows, gp, TN).reshape(4, 8, 8, 256)
    tap_sum[...] = tap_part[kz]
    across.start(lambda index: tap_sum.at[index], tap_line.at[iz])
    tap_line[iz] = tap_sum[iz]
    hh.arrive()
    sum2.scatter()
    across.arrive(some(tap_line, across.count - 1))
    s = jnp.sum(tap_line[...], axis=0) * scales[2]
    tap_all[ix, iy, iz] = jnp.concatenate([s[:, :128], s[:, 128:]], axis=0).astype(BF)
    own_tap = tap_all.at[ix, iy, iz]
    deep.start(lambda index: own_tap, own_tap)
    fill_half(hh, uh)
    gpool = dot(tt2[...], uh[...].reshape(3456, 256))
    r, c = rows_cols((256, 256))
    parts = split(gpool)
    for h in range(2):
        pick = hot(((r >> 6) == 2 * (c >> 7) + h) & ((r & 63) == ((c & 127) >> 1)))
        up = sum(dot(part, pick) for part in parts) * INV8
        up = jnp.concatenate(
            [up[32 * (x // 2) : 32 * (x // 2) + 32] for x in range(8)], axis=0
        )
        for zz in (2 * h, 2 * h + 1):
            gp1 = ((cot1[zz].astype(F32) + up) * sl1[zz]).astype(BF)
            hg.put(zz, gp1[:, :128])
            hg.put(zz + 4, gp1[:, 128:])
            g1[:, 256 * zz : 256 * zz + 256] = gp1
    for kz in range(3):
        uc = jnp.concatenate([u1[kz + zz] for zz in range(4)], axis=1)
        g = dot(g1[...], uc, NT)
        for ky in range(3):
            band = sum(
                g[32 * x : 32 * x + 32, ky * 320 + 32 * x : ky * 320 + 32 * x + 96]
                for x in range(8)
            )
            for kx in range(3):
                m1[kz * 9 + kx * 3 + ky] = jnp.concatenate(
                    [band[8 * i : 8 * i + 8, 32 * kx : 32 * kx + 32] for i in range(4)],
                    axis=1,
                )
    sum1.scatter()
    hg.start()
    deep_all = some(tap_all.at[ix, iy], deep.count - 1)
    deep.arrive(deep_all)
    own_depth = tap_all.at[ix, iy]
    row.start(lambda index: own_depth, own_depth)
    row_all = tap_all.at[pl.ds(0, nx - 1), iy]
    row.arrive(row_all)
    other = iy + 1 - 2 * lax.rem(iy, 2)

    def range_copy(y, target, lane):
        block = tap_all.at[pl.ds(0, nx), y]
        return pltpu.make_async_remote_copy(
            src_ref=block,
            dst_ref=block,
            send_sem=csend.at[lane],
            recv_sem=crecv.at[lane],
            device_id=(ix, target, iz),
            device_id_type=MESH,
        )

    hops = range(1, ny // 2)
    ranges = [range_copy(iy, lax.rem(iy + 2 * s, ny), s) for s in hops]
    for copy in ranges:
        copy.start()
    passed = [range_copy(iy, other, ny // 2)]
    passed[0].start()
    sum1.cross()
    sum2.cross()
    hg.arrive()
    fill_fine(hg, ug)
    sum2.gather(scales[1])
    sum1.gather(scales[0])
    for zz in range(4):
        rows = dot(tt1[...], ug[zz : zz + 3].reshape(2880, 256))
        fine_rows(gvol_v, zz, rows.astype(BF))
    store(gvol_v, gvol)
    for s, copy in zip(hops, ranges):
        copy.wait_recv()
        passed.append(range_copy(lax.rem(iy + ny - 2 * s, ny), other, ny // 2 + s))
        passed[-1].start()
    sum2.arrive()
    store(f2, d2)
    sum1.arrive()
    store(f1, d1)
    for copy in passed:
        copy.wait_recv()
    store(tap_all, d3)
    for copy in ranges + passed:
        copy.wait_send()
    for halo in (hv, hq, hh, hg):
        halo.finish()
    for copy in above:
        copy.wait_send()
    all_wide(wide1, 5, 3 * nx - 1).wait_send()
    all_wide(wide2, 6, 3 * nx - 1).wait_send()
    all_wide(wide1, 7, far).wait_send()
    across.finish(some(tap_line, across.count - 1))
    deep.finish(deep_all)
    row.finish(row_all)
    sum1.finish()
    sum2.finish()
    for copy in stores:
        copy.wait()


def last_kernel(
    scale, out_in, gvol_in, f1_in, f2_in, tap_in,
    out, gvol, d1, d2, d3, d4,
    f1, f2, tap_all, out_v, gvol_v, v1, v2, v3, sems,
):
    copies = []

    def copy(src, dst):
        one = pltpu.make_async_copy(src, dst, sems.at[len(copies)])
        one.start()
        copies.append(one)
        return one

    loads = [
        copy(tap_in, tap_all), copy(f2_in, f2), copy(f1_in, f1),
        copy(out_in, out_v), copy(gvol_in, gvol_v),
    ]
    loads[0].wait()
    for k in range(27):
        for j in range(8):
            block = tap_all[k // 8, k % 8, j].astype(F32)
            v3[k, 8 * j : 8 * j + 8, :] = jnp.concatenate([block[:8], block[8:]], axis=1)
        if k % 9 == 8:
            copy(v3.at[pl.ds(k - 8, 9)], d3.at[pl.ds(k - 8, 9)])
        if k == 8:
            for load in loads[3:]:
                load.wait()
            copy(out_v, out)
            copy(gvol_v, gvol)
    loads[1].wait()
    for k in range(27):
        wide = f2[k].astype(F32)
        v2[k] = jnp.concatenate([wide[:, :64], wide[:, 64:]], axis=0)
    copy(v2, d2)
    loads[2].wait()
    for k in range(27):
        wide = f1[k]
        v1[k] = jnp.concatenate([wide[:, 32 * i : 32 * i + 32] for i in range(4)], axis=0)
    copy(v1, d1)
    for i in range(4):
        half, col = i % 2, 128 * (i // 2)
        d4[16 * half : 16 * half + 16, col : col + 128] = f2[27 + i].astype(F32) * scale
    for one in copies[5:]:
        one.wait()


def halo_scratch(nz, nx, ch):
    return [
        pltpu.VMEM((nz + 2, (nx + 2) * ch, 128), BF),
        pltpu.VMEM((2, 16, nx * ch), BF),
        pltpu.VMEM((3, 2, 3, 16, nx * ch), BF),
    ]


def body(sizes, cells, vol, cot, w1, w2, w3, w4):
    shape = jax.ShapeDtypeStruct
    field = shape((32, 8, 8, 128), BF)
    vmem = pl.BlockSpec(memory_space=pltpu.VMEM)
    nx, ny, nz = sizes
    coarse = 1.0 / math.sqrt(cells / 512.0)
    scales = (1.0 / math.sqrt(cells * 1.0), 1.0 / math.sqrt(cells / 8.0), coarse)
    total = lambda r: [
        pltpu.VMEM((32, r, 128), F32),
        pltpu.VMEM((32, r, 128), F32),
        pltpu.VMEM((nz, r, 128), F32),
        pltpu.VMEM((32, r, 128), F32 if r == 8 else BF),
    ]
    anywhere = pl.BlockSpec(memory_space=pl.ANY)
    mid = pl.pallas_call(
        functools.partial(kernel, sizes, scales),
        out_shape=[
            field,
            field,
            shape((32, 8, 128), F32),
            shape((32, 16, 128), BF),
            shape((nx, ny, 8, 16, 128), BF),
        ],
        in_specs=[anywhere] * 6,
        out_specs=[anywhere] * 5,
        scratch_shapes=[
            *halo_scratch(8, 8, 32),
            *halo_scratch(4, 4, 32),
            *halo_scratch(4, 4, 64),
            *halo_scratch(8, 8, 32),
            pltpu.VMEM((6, 960, 256), BF),
            pltpu.VMEM((6, 960, 256), BF),
            pltpu.VMEM((9, 192, 256), BF),
            pltpu.VMEM((9, 384, 256), BF),
            pltpu.VMEM((256, 2880), BF),
            pltpu.VMEM((256, 2880), BF),
            pltpu.VMEM((256, 1728), BF),
            pltpu.VMEM((128, 3456), BF),
            pltpu.VMEM((4, 256, 256), F32),
            pltpu.VMEM((4, 256, 256), BF),
            pltpu.VMEM((4, 256, 256), BF),
            pltpu.VMEM((256, 1024), BF),
            pltpu.SemaphoreType.DMA((4, 26)),
            pltpu.SemaphoreType.DMA((4, 26)),
            pltpu.VMEM((5, 16, 128), BF),
            pltpu.VMEM((2, 16, 256), BF),
            pltpu.VMEM(((nx + 4) * (ny + 2), 16, 256), BF),
            pltpu.VMEM(((nx + 4) * (ny + 2), 16, 256), BF),
            pltpu.VMEM((3, nx + 2, 16 * ny, 256), BF),
            pltpu.VMEM((4, 8, 8, 256), F32),
            pltpu.VMEM((8, 8, 256), F32),
            pltpu.VMEM((nz, 8, 256), F32),
            pltpu.VMEM((nx, ny, 8, 16, 128), BF),
            *total(8),
            *total(16),
            pltpu.SemaphoreType.DMA((11,)),
            pltpu.SemaphoreType.DMA((11,)),
            pltpu.VMEM((32, 8, 8, 128), BF),
            pltpu.VMEM((32, 8, 8, 128), BF),
            pltpu.VMEM((27, 32, 32), BF),
            pltpu.VMEM((27, 32, 64), BF),
            pltpu.VMEM((27, 64, 256), BF),
            pltpu.VMEM((32, 256), BF),
            pltpu.VMEM((32, 8, 8, 128), BF),
            pltpu.VMEM((32, 8, 8, 128), BF),
            pltpu.SemaphoreType.DMA((11,)),
            pltpu.SemaphoreType.DMA((8,)),
            pltpu.SemaphoreType.DMA((8,)),
            pltpu.SemaphoreType.DMA((ny,)),
            pltpu.SemaphoreType.DMA((ny,)),
        ],
        compiler_params=pltpu.CompilerParams(
            collective_id=0, has_side_effects=True, vmem_limit_bytes=60 * 1024 * 1024
        ),
        name="unet",
    )(vol, cot, w1, jnp.swapaxes(w2, 1, 2), jnp.swapaxes(w3, 1, 2), w4)
    finals = [
        field,
        field,
        shape((27, 32, 32), F32),
        shape((27, 32, 64), F32),
        shape((27, 64, 256), F32),
        shape((32, 256), F32),
    ]
    out, gvol, d1, d2, d3, d4 = pl.pallas_call(
        functools.partial(last_kernel, scales[2] / scales[1]),
        out_shape=finals,
        in_specs=[anywhere] * 5,
        out_specs=[anywhere] * 5 + [vmem],
        scratch_shapes=[pltpu.VMEM(f.shape, f.dtype) for f in list(mid[2:]) + finals[:5]]
        + [pltpu.SemaphoreType.DMA((12,))],
        compiler_params=pltpu.CompilerParams(vmem_limit_bytes=60 * 1024 * 1024),
        name="finish",
    )(*mid)
    return out, gvol, d1, jnp.swapaxes(d2, 1, 2), jnp.swapaxes(d3, 1, 2), d4


def solution(mesh):
    sizes = (mesh.shape["gx"], mesh.shape["gy"], mesh.shape["gz"])
    cells = 8 * 8 * 128 * sizes[0] * sizes[1] * sizes[2]
    field = P(None, "gz", "gx", "gy")
    return jax.shard_map(
        functools.partial(body, sizes, cells),
        mesh=mesh,
        in_specs=(field, field, P(), P(), P(), P()),
        out_specs=(field, field, P(), P(), P(), P()),
        check_vma=False,
    )
```
